32 devices in a mesh: bins: 8 (over z, y), chan: 4 (over x, core).
Axes of the slice: x: 2, y: 2, z: 4, core: 2. Of those that a mesh axis runs over, the one named last changes fastest.
Arguments:
- tokens_in: bfloat16 [4096, 2048], P('bins', 'chan'), may hold values from -6 to 6
- filters: bfloat16 [4096, 2048], P('bins', 'chan'), may hold values from -0.09375 to 0.09375
- gate: bfloat16 [4096, 2048], P('bins', 'chan'), may hold values from -6 to 6
- skip: float32 [2048], P('chan'), may hold values from 0.5 to 1.5
- out_grad: bfloat16 [4096, 4096], P('bins', 'chan'), may hold values from -6 to 6
- out_weight: bfloat16 [2048, 4096], P('chan'), may hold values from -0.09375 to 0.09375
- owner: int32 [8, 512], P(None, 'bins'), may hold values from 0 to 7, as said below
- slot: int32 [8, 512], P(None, 'bins'), may hold values from 0 to 1023, as said below
Outputs:
- gate_grad: bfloat16 [8, 512, 2048], P(None, 'bins', 'chan')
- filter_grad: float32 [8, 512, 2048], P(None, 'bins', 'chan')
- grad_rows: bfloat16 [8192, 2048], P('bins', 'chan')
The draws below stay inside these ranges and needn't reach their ends.
Inputs may be any that keep to these rules, and one draw needn't show every extreme that they name: Let the column group j be the entries [i, r] with j * 64 <= r < (j + 1) * 64, all i. Within one column group at most 128 entries name the same owner, and in every draw some owner is named exactly 128 times by every column group. An entry of column group j (as for owner) lies in j * 128 to (j + 1) * 128 - 1; no two tokens share an owner and a slot; in every draw some owner has all 1024 slots used.
All inputs are finite; a program needn't handle non-finite values.
Results may differ from the reference program's by a relative error of at most 0.012.
Values may be sent and summed in bfloat16 or wider, within the bound.
No kernel may reach another device: no remote copies, remote signals or barrier semaphores. Data moves between devices by JAX's collectives and lax.ppermute only.
A program may use at most 128 MiB of HBM per device.

```python
import math
import jax
import jax.numpy as jnp

D = 4096
CH = 2048
TOK_DEV = 512
BLOCKS = 8
SEQ = 4096
NFFT = 8192
COLS = 64
SEND = 128
CAP = 1024


def shuffle_one(sub_key):
    return jax.random.permutation(sub_key, TOK_DEV)


def to_grid(held):
    return held.reshape(BLOCKS, BLOCKS, COLS).transpose(1, 0, 2).reshape(BLOCKS, TOK_DEV)


def placement_lists(key):
    base_key = jax.random.fold_in(key, 11)
    key_hot, key_shift, key_order, key_slots = jax.random.split(base_key, 4)
    hot_owner = jax.random.randint(key_hot, (), 0, BLOCKS)
    shifts = jax.random.randint(key_shift, (BLOCKS,), 0, BLOCKS - 1)
    places = jnp.arange(TOK_DEV, dtype=jnp.int32)
    others = (places[None, :] - SEND + shifts[:, None]) % (BLOCKS - 1)
    others = others + (others >= hot_owner).astype(jnp.int32)
    chosen = jnp.where(places[None, :] < SEND, hot_owner, others).astype(jnp.int32)
    shuffles = jax.vmap(shuffle_one)(jax.random.split(key_order, BLOCKS))
    owners_held = jnp.take_along_axis(chosen, shuffles, axis=1)
    one_hot = (owners_held[:, :, None] == jnp.arange(BLOCKS, dtype=jnp.int32)[None, None, :]).astype(jnp.int32)
    earlier = jnp.cumsum(one_hot, axis=1) - one_hot
    ranks = jnp.sum(earlier * one_hot, axis=2)
    scores = jax.random.randint(key_slots, (BLOCKS, BLOCKS, SEND), 0, 2 ** 18) * SEND + jnp.arange(SEND, dtype=jnp.int32)
    orders = jnp.argsort(scores, axis=2).astype(jnp.int32)
    holders = jnp.arange(BLOCKS, dtype=jnp.int32)[:, None]
    positions = orders[holders, owners_held, ranks]
    slots_held = holders * SEND + positions
    return (to_grid(owners_held).astype(jnp.int32), to_grid(slots_held).astype(jnp.int32))


def draw_owner(key, part):
    return placement_lists(key)[0]


def draw_slot(key, part):
    return placement_lists(key)[1]


def block_scale(key, extent, shards, low, largest):
    factor_of, own = 1.0, jax.random.fold_in(key, 6)
    for axis_at, blocks in shards:
        steps = jnp.exp(jax.random.uniform(jax.random.fold_in(own, axis_at), (blocks,), jnp.float32, low / len(shards), largest / len(shards)))
        factor_of = factor_of * jnp.repeat(steps, extent[axis_at] // blocks).reshape([-1 if axis == axis_at else 1 for axis in range(len(extent))])
    return factor_of


def noise(key, extent, scale, reach, cuts=(), held_as=jnp.bfloat16):
    gain = block_scale(key, extent, cuts, -0.22, 0.18) if cuts else 1.0
    entries = jax.random.normal(key, extent, jnp.float32) * scale * gain
    return jnp.minimum(jnp.maximum(entries, -reach), reach).astype(held_as)


def setup_inputs(seed: int = 0) -> dict:
    key_list = jax.random.split(jax.random.key(seed), 9)
    return {
        "tokens_in": noise(key_list[0], (SEQ, CH), 1.0, 6.0, ((0, 8), (1, 4))),
        "filters": noise(key_list[1], (SEQ, CH), SEQ ** -0.5, 0.09375, ((0, 8), (1, 4))),
        "gate": noise(key_list[2], (SEQ, CH), 1.0, 6.0, ((0, 8), (1, 4))),
        "skip": jnp.clip(0.5 + 1.0 * jax.random.uniform(key_list[3], (CH,), jnp.float32) ** block_scale(key_list[3], (CH,), ((0, 4),), -0.2, 0.2), 0.5, 1.5),
        "out_grad": noise(key_list[4], (SEQ, D), 1.0, 6.0, ((0, 8), (1, 4))),
        "out_weight": noise(key_list[5], (CH, D), D ** -0.5, 0.09375, ((0, 4),)),
        "owner": draw_owner(jax.random.fold_in(key_list[8], 71), 0),
        "slot": draw_slot(jax.random.fold_in(key_list[8], 71), 0),
    }


def reference(tokens_in, filters, gate, skip, out_grad, out_weight, owner, slot):
    g_rounded = jnp.dot(out_grad, out_weight.T, preferred_element_type=jnp.float32).astype(jnp.bfloat16)
    grad_in = (g_rounded.astype(jnp.float32) * gate.astype(jnp.float32)).astype(jnp.bfloat16)
    tok_real = tokens_in.astype(jnp.float32)
    spec_x = jnp.fft.rfft(tok_real, n=NFFT, axis=0)
    spec_h = jnp.fft.rfft(filters.astype(jnp.float32), n=NFFT, axis=0)
    spec_y = jnp.fft.rfft(grad_in.astype(jnp.float32), n=NFFT, axis=0)

    def inverse(spectrum):
        return jnp.fft.irfft(spectrum, n=NFFT, axis=0)[:SEQ]
    conv = inverse(spec_x * spec_h)
    gate_grad = (g_rounded.astype(jnp.float32) * (conv + skip * tok_real)).astype(jnp.bfloat16)
    token_grad = (inverse(jnp.conj(spec_h) * spec_y) + skip * grad_in.astype(jnp.float32)).astype(jnp.bfloat16)
    filter_grad = inverse(spec_y * jnp.conj(spec_x)) / math.sqrt(SEQ)
    targets = owner.reshape(-1) * CAP + slot.reshape(-1)
    grad_rows = jnp.zeros((BLOCKS * CAP, CH), jnp.bfloat16).at[targets].set(token_grad)
    return (gate_grad.reshape(BLOCKS, TOK_DEV, CH), filter_grad.reshape(BLOCKS, TOK_DEV, CH), grad_rows)
```

```python
import functools
import math

import jax
import jax.numpy as jnp
import numpy as np
from jax import lax
from jax.experimental import pallas as pl
from jax.experimental.pallas import tpu as pltpu
from jax.sharding import PartitionSpec as P

LANES = 128
F32 = jnp.float32
BF16 = jnp.bfloat16
MIB = 1 << 20


class Plan:
    def __init__(self, blocks, tok, chans):
        self.B = blocks
        self.T = tok
        self.C = chans
        self.cb = chans // blocks
        self.G = LANES // self.cb
        self.R = tok // self.G
        self.tiles = chans // LANES
        self.cols = tok // blocks
        self.send = 2 * self.cols
        self.Q = blocks // self.G
        self.N = 2 * blocks * tok
        self.K = blocks + 1


def wave(num, den):
    ang = 2.0 * np.pi * (np.asarray(num) % den) / den
    return np.cos(ang), -np.sin(ang)


def tables(s):
    rows = np.arange(s.R)
    lane_e = np.arange(LANES) // s.cb
    dft_c, dft_s = wave(rows[:, None] * rows[None, :], s.R)
    stacked = np.concatenate([dft_c, -dft_s], axis=0)
    k1 = np.arange(s.K)
    tw = wave(rows[None, :, None] * (k1[:, None, None] + 2 * s.B * lane_e[None, None, :]), s.N)
    tw = np.stack(tw, axis=1)
    pre = np.stack(wave(k1[:, None] * lane_e[None, :], 2 * s.B * s.G), axis=1)
    return (
        jnp.asarray(stacked, BF16),
        jnp.asarray(tw, F32),
        jnp.asarray(pre, F32),
    )


def lane_group(s, rows):
    return lax.broadcasted_iota(jnp.int32, (rows, LANES), 1) // s.cb


def turn(v, shift):
    shift = shift % LANES
    return v if shift == 0 else pltpu.roll(v, shift, 1)


def lane_transpose(s, parts, group):
    out = []
    for a in range(s.G):
        acc = None
        for g in range(s.G):
            moved = turn(parts[g], (g - a) * s.cb)
            acc = moved if acc is None else jnp.where(group == g, moved, acc)
        out.append(acc)
    return out


def lane_dft(s, re, im, group, sign):
    if s.G == 1:
        return re, im
    if s.G == 2:
        flip = jnp.where(group == 0, 1.0, -1.0).astype(F32)
        return turn(re, s.cb) + flip * re, turn(im, s.cb) + flip * im
    out_re = out_im = None
    for d in range(s.G):
        mre, mim = turn(re, d * s.cb), turn(im, d * s.cb)
        source = (group - d + s.G) % s.G
        angle_index = (group * source) % s.G
        cos_t = jnp.zeros_like(re)
        sin_t = jnp.zeros_like(re)
        for a in range(s.G):
            c, w = wave(a, s.G)
            cos_t = jnp.where(angle_index == a, float(c), cos_t)
            sin_t = jnp.where(angle_index == a, float(w) * sign, sin_t)
        add_re = mre * cos_t - mim * sin_t
        add_im = mre * sin_t + mim * cos_t
        out_re = add_re if out_re is None else out_re + add_re
        out_im = add_im if out_im is None else out_im + add_im
    return out_re, out_im


def weighted(values, weights):
    acc = None
    for v, w in zip(values, weights):
        w = float(w)
        if abs(w) < 1e-12:
            continue
        term = v if abs(w - 1) < 1e-12 else (-v if abs(w + 1) < 1e-12 else v * w)
        acc = term if acc is None else acc + term
    return acc


def add(a, b):
    return b if a is None else (a if b is None else a + b)


def sub(a, b):
    return a if b is None else (-b if a is None else a - b)


def block_dft(s, xs):
    even, odd = range(0, s.B, 2), range(1, s.B, 2)
    out = [None] * s.K
    for k in range(s.B // 2 + 1):
        ce, se = wave(np.array(even) * k, 2 * s.B)
        co, so = wave(np.array(odd) * k, 2 * s.B)
        xe, xo = [xs[i] for i in even], [xs[i] for i in odd]
        ere, eim = weighted(xe, ce), weighted(xe, se)
        ore, oim = weighted(xo, co), weighted(xo, so)
        out[k] = (add(ere, ore), add(eim, oim))
        if k != s.B - k:
            out[s.B - k] = (sub(ere, ore), sub(oim, eim))
    return out


def block_back(s, ts):
    half = s.B // 2
    sums = {}
    for k in range(half + 1):
        tre, tim = ts[k]
        if k == half:
            sums[k] = (tre, tre, tim, tim)
        else:
            ure, uim = ts[s.B - k]
            sums[k] = (tre + ure, tre - ure, tim - uim, tim + uim)
    out = []
    for i in range(s.B):
        acc = None
        for k in range(half + 1):
            c, w = wave(i * k, 2 * s.B)
            gain = 1.0 if k == 0 else 2.0
            re = sums[k][i % 2]
            im = sums[k][2 + i % 2]
            acc = add(acc, weighted([re, im], [gain * float(c), gain * float(w)]))
        out.append(acc)
    return out


CHUNK = 16


def forward_rows(s, load, held, tw, pre):
    def body(c, _):
        rows = pl.ds(pl.multiple_of(c * CHUNK, CHUNK), CHUNK)
        group = lane_group(s, CHUNK)
        spec = block_dft(s, [load(i, rows) for i in range(s.B)])
        for k in range(s.K):
            re, im = spec[k]
            pr, pi = pre[k, 0:1, :], pre[k, 1:2, :]
            if k == 0:
                im = jnp.zeros_like(re)
            elif im is None:
                re, im = re * pr, re * pi
            else:
                re, im = re * pr - im * pi, re * pi + im * pr
            re, im = lane_dft(s, re, im, group, 1.0)
            tr, ti = tw[k, 0, rows, :], tw[k, 1, rows, :]
            held[k, rows, 0:LANES] = (re * tr - im * ti).astype(BF16)
            held[k, rows, LANES : 2 * LANES] = (re * ti + im * tr).astype(BF16)
        return 0

    lax.fori_loop(0, s.R // CHUNK, body, 0)


def forward_bins(s, held_k, dft):
    o = jnp.dot(dft[...], held_k, preferred_element_type=F32)
    re = o[: s.R, :LANES] + o[s.R :, LANES:]
    im = o[: s.R, LANES:] - o[s.R :, :LANES]
    return re, im


def inverse_bins(s, re, im, k, dft, tw, pre, back):
    z = jnp.concatenate([re.astype(BF16), im.astype(BF16)], axis=1)
    o = jnp.dot(dft[...], z, preferred_element_type=F32)
    re = o[: s.R, :LANES] - o[s.R :, LANES:]
    im = o[: s.R, LANES:] + o[s.R :, :LANES]
    tr, ti = tw[k, 0], tw[k, 1]
    re, im = re * tr + im * ti, im * tr - re * ti
    re, im = lane_dft(s, re, im, lane_group(s, s.R), -1.0)
    pr, pi = pre[k, 0:1, :], pre[k, 1:2, :]
    back[k, 0] = re * pr + im * pi
    back[k, 1] = im * pr - re * pi


def inverse_rows(s, back, rows):
    return block_back(s, [(back[k, 0, rows, :], back[k, 1, rows, :]) for k in range(s.K)])


def each_chunk(s, body):
    def step(c, _):
        body(pl.ds(pl.multiple_of(c * CHUNK, CHUNK), CHUNK))
        return 0

    lax.fori_loop(0, s.R // CHUNK, step, 0)


def params(limit=40):
    return pltpu.CompilerParams(vmem_limit_bytes=limit * MIB)


def vmem():
    return pl.BlockSpec(memory_space=pltpu.VMEM)


def cost(flops, nbytes):
    return pl.CostEstimate(flops=int(flops), bytes_accessed=int(nbytes), transcendentals=0)


def pack_kernel(s, n, *refs):
    group = lane_group(s, s.R)
    for a in range(n):
        src, dst = refs[a], refs[n + a]
        for m in range(s.tiles):
            parts = [
                src[p * s.R : (p + 1) * s.R, m * LANES : (m + 1) * LANES].astype(F32)
                for p in range(s.G)
            ]
            for q, v in enumerate(lane_transpose(s, parts, group)):
                dst[s.G * m + q] = v.astype(BF16)


def pack(s, *arrays):
    n = len(arrays)
    return pl.pallas_call(
        functools.partial(pack_kernel, s, n),
        out_shape=[jax.ShapeDtypeStruct((s.B, s.R, LANES), BF16)] * n,
        in_specs=[vmem()] * n,
        out_specs=[vmem()] * n,
        compiler_params=params(32),
        cost_estimate=cost(n * s.T * s.C * 4, n * s.T * s.C * 4),
        name="pack_channels",
    )(*arrays)


def project_kernel(s, n, index, *refs):
    pieces, weight, out, acc = refs[:n], refs[n], refs[n + 1], refs[n + 2]
    k = pl.program_id(0)

    @pl.when(k == 0)
    def _():
        acc[...] = jnp.zeros_like(acc)

    for a in range(n):

        @pl.when(k == a)
        def _():
            acc[...] += lax.dot_general(
                pieces[a][...],
                weight[...],
                (((1,), (1,)), ((), ())),
                preferred_element_type=F32,
            )

    @pl.when(k == n - 1)
    def _():
        group = lane_group(s, s.R)
        for m in range(s.tiles):
            parts = [
                acc[p * s.R : (p + 1) * s.R, m * LANES : (m + 1) * LANES] for p in range(s.G)
            ]
            for q, v in enumerate(lane_transpose(s, parts, group)):
                out[s.G * m + q] = v.astype(BF16)


def project(s, pieces, order, weight):
    n = len(pieces)
    feats = pieces[0].shape[1]
    return pl.pallas_call(
        functools.partial(project_kernel, s, n),
        out_shape=jax.ShapeDtypeStruct((s.B, s.R, LANES), BF16),
        grid_spec=pltpu.PrefetchScalarGridSpec(
            num_scalar_prefetch=1,
            grid=(n,),
            in_specs=[pl.BlockSpec((s.T, feats), lambda k, o: (0, 0))] * n
            + [pl.BlockSpec((s.C, feats), lambda k, o: (0, o[k]))],
            out_specs=pl.BlockSpec((s.B, s.R, LANES), lambda k, o: (0, 0, 0)),
            scratch_shapes=[pltpu.VMEM((s.T, s.C), F32)],
        ),
        compiler_params=params(32),
        cost_estimate=cost(2 * s.T * s.C * feats * n, 2 * n * feats * (s.T + s.C)),
        name="project_cotangent",
    )(order, *pieces, weight)


def conv_kernel(s, x, h, skip, dft, tw, pre, x_spec, h_spec, u, held, back):
    forward_rows(s, lambda i, rows: x[i, rows, :].astype(F32), held, tw, pre)

    def x_bins(k, _):
        re, im = forward_bins(s, held[k], dft)
        x_spec[k, 0] = re
        x_spec[k, 1] = im
        return 0

    lax.fori_loop(0, s.K, x_bins, 0)
    forward_rows(s, lambda i, rows: h[i, rows, :].astype(F32), held, tw, pre)

    def h_bins(k, _):
        hre, him = forward_bins(s, held[k], dft)
        h_spec[k, 0] = hre
        h_spec[k, 1] = him
        xre, xim = x_spec[k, 0], x_spec[k, 1]
        inverse_bins(s, xre * hre - xim * him, xre * him + xim * hre, k, dft, tw, pre, back)
        return 0

    lax.fori_loop(0, s.K, h_bins, 0)

    def last(rows):
        conv = inverse_rows(s, back, rows)
        for i in range(s.B):
            u[i, rows, :] = conv[i] * (1.0 / s.N) + skip[...] * x[i, rows, :].astype(F32)

    each_chunk(s, last)


def gate_kernel(s, g, u, out):
    group = lane_group(s, s.cols)
    for q in range(s.Q):
        rows = slice(q * s.cols, (q + 1) * s.cols)
        for i2 in range(s.Q):
            parts = [
                g[s.G * i2 + a, rows, :].astype(F32) * u[s.G * i2 + a, rows, :]
                for a in range(s.G)
            ]
            for p, v in enumerate(lane_transpose(s, parts, group)):
                out[p * s.Q + q, i2] = v.astype(BF16)


def token_kernel(s, g, gate, h_spec, skip, hot, dft, tw, pre, y_spec, out, dy, held, back, tok):
    step = pl.program_id(0)

    @pl.when(step == 0)
    def _():
        def gated(i, rows):
            v = (g[i, rows, :].astype(F32) * gate[i, rows, :].astype(F32)).astype(BF16)
            dy[i, rows, :] = v
            return v.astype(F32)

        forward_rows(s, gated, held, tw, pre)

        def bins(k, _):
            yre, yim = forward_bins(s, held[k], dft)
            y_spec[k, 0] = yre
            y_spec[k, 1] = yim
            hre, him = h_spec[k, 0], h_spec[k, 1]
            inverse_bins(s, hre * yre + him * yim, hre * yim - him * yre, k, dft, tw, pre, back)
            return 0

        lax.fori_loop(0, s.K, bins, 0)

        def last(rows):
            back_rows = inverse_rows(s, back, rows)
            for i in range(s.B):
                v = back_rows[i] * (1.0 / s.N) + skip[...] * dy[i, rows, :].astype(F32)
                tok[i, rows, :] = v.astype(BF16)

        each_chunk(s, last)

    rows = pl.ds(pl.multiple_of(step * s.cols, s.cols), s.cols)
    v = jnp.concatenate([tok[i, rows, :] for i in range(s.B)], axis=0)
    group = lane_group(s, s.B * s.cols)
    zero = jnp.zeros_like(v)
    v = jnp.concatenate([jnp.where(group == p, v, zero) for p in range(s.G)], axis=0)
    o = jnp.dot(hot[0], v, preferred_element_type=F32)
    for b in range(s.B):
        out[b] = o[b * s.send : (b + 1) * s.send].astype(BF16)


def filter_kernel(s, x_spec, y_spec, dft, tw, pre, out, back):
    def bins(k, _):
        xre, xim = x_spec[k, 0], x_spec[k, 1]
        yre, yim = y_spec[k, 0], y_spec[k, 1]
        inverse_bins(s, yre * xre + yim * xim, yim * xre - yre * xim, k, dft, tw, pre, back)
        return 0

    lax.fori_loop(0, s.K, bins, 0)
    scale = 1.0 / (s.N * math.sqrt(s.B * s.T))
    group = lane_group(s, CHUNK)
    per = s.cols // CHUNK

    def body(c, _):
        rows = pl.ds(pl.multiple_of(c * CHUNK, CHUNK), CHUNK)
        lag = inverse_rows(s, back, rows)
        q = c // per
        inner = pl.ds(pl.multiple_of((c % per) * CHUNK, CHUNK), CHUNK)
        for i2 in range(s.Q):
            parts = [lag[s.G * i2 + a] * scale for a in range(s.G)]
            for p, v in enumerate(lane_transpose(s, parts, group)):
                out[p * s.Q + q, i2, inner, :] = v.astype(BF16)
        return 0

    lax.fori_loop(0, s.R // CHUNK, body, 0)


def hot_kernel(s, code, out):
    rows = s.B * s.send
    wide = s.B * s.cols
    target = lax.broadcasted_iota(jnp.int32, (rows, wide), 0)
    for p in range(s.G):
        match = target == code[0, :, p * wide : (p + 1) * wide]
        out[0, :, p * wide : (p + 1) * wide] = jnp.where(match, 1.0, 0.0).astype(BF16)


def columns_kernel(s, src, out):
    group = lane_group(s, s.cols)
    for i2 in range(s.Q):
        for m in range(s.tiles):
            parts = [src[s.G * m + g, i2].astype(F32) for g in range(s.G)]
            for a, v in enumerate(lane_transpose(s, parts, group)):
                out[s.G * i2 + a, :, m * LANES : (m + 1) * LANES] = v.astype(out.dtype)


def columns(s, src, dtype):
    return pl.pallas_call(
        functools.partial(columns_kernel, s),
        out_shape=jax.ShapeDtypeStruct((s.B, s.cols, s.C), dtype),
        in_specs=[vmem()],
        out_specs=vmem(),
        compiler_params=params(16),
        cost_estimate=cost(s.T * s.C * 4, s.T * s.C * 6),
        name="unpack_columns",
    )(src)


def rows_kernel(s, src, out):
    group = lane_group(s, s.send)
    for m in range(s.tiles):
        for q in range(s.Q):
            rows = slice(q * s.send, (q + 1) * s.send)
            parts = [src[s.G * m + g, rows, :].astype(F32) for g in range(s.G)]
            for p, v in enumerate(lane_transpose(s, parts, group)):
                at = (p * s.Q + q) * s.send
                out[at : at + s.send, m * LANES : (m + 1) * LANES] = v.astype(BF16)


def owner_rows(s, src):
    return pl.pallas_call(
        functools.partial(rows_kernel, s),
        out_shape=jax.ShapeDtypeStruct((s.B * s.send, s.C), BF16),
        in_specs=[vmem()],
        out_specs=vmem(),
        compiler_params=params(16),
        cost_estimate=cost(s.T * s.C * 4, s.T * s.C * 8),
        name="unpack_rows",
    )(src)


def exchange(v):
    return lax.all_to_all(v, "bins", split_axis=0, concat_axis=0, tiled=True)


def shards(tokens_in, filters, gate, skip, out_grad, out_weight, owner, slot):
    s = Plan(lax.axis_size("bins"), *tokens_in.shape)
    me = lax.axis_index("bins")
    chan = lax.axis_index("chan")
    nchan = lax.axis_size("chan")
    dft, tw, pre = tables(s)
    spec_shape = jax.ShapeDtypeStruct((s.K, 2, s.R, LANES), F32)
    spec_bytes = s.K * 2 * s.R * LANES * 4
    transform = 2 * 2 * s.R * s.R * 2 * LANES * s.K
    held = pltpu.VMEM((s.K, s.R, 2 * LANES), BF16)
    back = pltpu.VMEM((s.K, 2, s.R, LANES), F32)

    packed_x, packed_h = pack(s, tokens_in, filters)
    came = exchange(jnp.stack([packed_x, packed_h], axis=1))
    x, h = came[:, 0], came[:, 1]
    (packed_gate,) = pack(s, gate)
    came_gate = exchange(packed_gate)

    half = nchan // 2
    core_pairs = [(c, c ^ 1) for c in range(nchan)]
    far_pairs = [(c, (c + half) % nchan) for c in range(nchan)]
    far = lax.ppermute(out_grad, "chan", far_pairs)
    near = lax.ppermute(out_grad, "chan", core_pairs)
    far_near = lax.ppermute(far, "chan", core_pairs)
    order = jnp.stack([chan, chan ^ 1, (chan + half) % nchan, ((chan ^ 1) + half) % nchan])
    packed_g = project(s, [out_grad, near, far, far_near], order.astype(jnp.int32), out_weight)
    g = exchange(packed_g)

    code = owner * s.send + slot - me * s.send
    codes = lax.all_gather(code.reshape(1, s.B * s.cols), "bins", axis=0, tiled=True)
    codes = codes.reshape(s.G, s.Q, s.B * s.cols).transpose(1, 0, 2)
    codes = codes.reshape(s.Q, 1, s.G * s.B * s.cols)
    hot_shape = (s.Q, s.B * s.send, s.G * s.B * s.cols)
    hot = pl.pallas_call(
        functools.partial(hot_kernel, s),
        out_shape=jax.ShapeDtypeStruct(hot_shape, BF16),
        grid=(s.Q,),
        in_specs=[pl.BlockSpec((1, 1, hot_shape[2]), lambda q: (q, 0, 0))],
        out_specs=pl.BlockSpec((1,) + hot_shape[1:], lambda q: (q, 0, 0)),
        compiler_params=params(32),
        cost_estimate=cost(math.prod(hot_shape), 2 * math.prod(hot_shape)),
        name="row_choice",
    )(codes)

    my_skip = lax.dynamic_slice_in_dim(skip, me * s.cb, s.cb)
    my_skip = jnp.tile(my_skip, s.G).reshape(1, LANES)

    x_spec, h_spec, u = pl.pallas_call(
        functools.partial(conv_kernel, s),
        out_shape=[spec_shape, spec_shape, jax.ShapeDtypeStruct((s.B, s.R, LANES), F32)],
        in_specs=[vmem()] * 6,
        out_specs=[vmem()] * 3,
        scratch_shapes=[held, back],
        compiler_params=params(40),
        cost_estimate=cost(3 * transform, 4 * spec_bytes),
        name="conv_products",
    )(x, h, my_skip, dft, tw, pre)

    gate_out = pl.pallas_call(
        functools.partial(gate_kernel, s),
        out_shape=jax.ShapeDtypeStruct((s.B, s.Q, s.cols, LANES), BF16),
        in_specs=[vmem()] * 2,
        out_specs=vmem(),
        compiler_params=params(16),
        cost_estimate=cost(s.T * s.C * 4, s.T * s.C * 8),
        name="gate_products",
    )(g, u)
    gate_cols = exchange(gate_out)

    const2 = lambda q: (0, 0)
    const3 = lambda q: (0, 0, 0)
    const4 = lambda q: (0, 0, 0, 0)
    whole = pl.BlockSpec((s.B, s.R, LANES), const3)
    spec_block = pl.BlockSpec((s.K, 2, s.R, LANES), const4)
    y_spec, outbox = pl.pallas_call(
        functools.partial(token_kernel, s),
        out_shape=[spec_shape, jax.ShapeDtypeStruct((s.B, s.Q * s.send, LANES), BF16)],
        grid=(s.Q,),
        in_specs=[
            whole,
            whole,
            spec_block,
            pl.BlockSpec((1, LANES), const2),
            pl.BlockSpec((1,) + hot_shape[1:], lambda q: (q, 0, 0)),
            pl.BlockSpec((2 * s.R, s.R), const2),
            spec_block,
            pl.BlockSpec((s.K, 2, LANES), const3),
        ],
        out_specs=[spec_block, pl.BlockSpec((s.B, s.send, LANES), lambda q: (0, q, 0))],
        scratch_shapes=[
            pltpu.VMEM((s.B, s.R, LANES), BF16),
            held,
            back,
            pltpu.VMEM((s.B, s.R, LANES), BF16),
        ],
        compiler_params=params(48),
        cost_estimate=cost(2 * transform, 3 * spec_bytes + 2 * math.prod(hot_shape)),
        name="token_products",
    )(g, came_gate, h_spec, my_skip, hot, dft, tw, pre)
    inbox = exchange(outbox)

    lag_out = pl.pallas_call(
        functools.partial(filter_kernel, s),
        out_shape=jax.ShapeDtypeStruct((s.B, s.Q, s.cols, LANES), BF16),
        in_specs=[vmem()] * 5,
        out_specs=vmem(),
        scratch_shapes=[back],
        compiler_params=params(32),
        cost_estimate=cost(transform, 3 * spec_bytes),
        name="filter_products",
    )(x_spec, y_spec, dft, tw, pre)
    lag_cols = exchange(lag_out)

    gate_grad = columns(s, gate_cols, BF16)
    grad_rows = owner_rows(s, inbox)
    filter_grad = columns(s, lag_cols, F32)
    return (gate_grad, filter_grad, grad_rows)


def solution(mesh):
    return jax.shard_map(
        shards,
        mesh=mesh,
        in_specs=(
            P("bins", "chan"),
            P("bins", "chan"),
            P("bins", "chan"),
            P("chan"),
            P("bins", "chan"),
            P("chan", None),
            P(None, "bins"),
            P(None, "bins"),
        ),
        out_specs=(P(None, "bins", "chan"), P(None, "bins", "chan"), P("bins", "chan")),
        check_vma=False,
    )
```

```python
import functools
import math

import jax
import jax.numpy as jnp
import numpy as np
from jax import lax
from jax.experimental import pallas as pl
from jax.experimental.pallas import tpu as pltpu
from jax.sharding import PartitionSpec as P

LANES = 128
F32 = jnp.float32
BF16 = jnp.bfloat16
MIB = 1 << 20


class Plan:
    def __init__(self, blocks, tok, chans):
        self.B = blocks
        self.T = tok
        self.C = chans
        self.cb = chans // blocks
        self.G = LANES // self.cb
        self.R = tok // self.G
        self.tiles = chans // LANES
        self.cols = tok // blocks
        self.send = 2 * self.cols
        self.Q = blocks // self.G
        self.N = 2 * blocks * tok
        self.K = blocks + 1


def wave(num, den):
    ang = 2.0 * np.pi * (np.asarray(num) % den) / den
    return np.cos(ang), -np.sin(ang)


def tables(s):
    rows = np.arange(s.R)
    lane_e = np.arange(LANES) // s.cb
    dft_c, dft_s = wave(rows[:, None] * rows[None, :], s.R)
    stacked = np.concatenate([dft_c, -dft_s], axis=0)
    k1 = np.arange(s.K)
    tw = wave(rows[None, :, None] * (k1[:, None, None] + 2 * s.B * lane_e[None, None, :]), s.N)
    tw = np.stack(tw, axis=1)
    pre = np.stack(wave(k1[:, None] * lane_e[None, :], 2 * s.B * s.G), axis=1)
    return (
        jnp.asarray(stacked, BF16),
        jnp.asarray(tw, F32),
        jnp.asarray(pre, F32),
    )


def lane_group(s, rows):
    return lax.broadcasted_iota(jnp.int32, (rows, LANES), 1) // s.cb


def turn(v, shift):
    shift = shift % LANES
    return v if shift == 0 else pltpu.roll(v, shift, 1)


def lane_transpose(s, parts, group):
    out = []
    for a in range(s.G):
        acc = None
        for g in range(s.G):
            moved = turn(parts[g], (g - a) * s.cb)
            acc = moved if acc is None else jnp.where(group == g, moved, acc)
        out.append(acc)
    return out


def lane_dft(s, re, im, group, sign):
    if s.G == 1:
        return re, im
    if s.G == 2:
        flip = jnp.where(group == 0, 1.0, -1.0).astype(F32)
        return turn(re, s.cb) + flip * re, turn(im, s.cb) + flip * im
    out_re = out_im = None
    for d in range(s.G):
        mre, mim = turn(re, d * s.cb), turn(im, d * s.cb)
        source = (group - d + s.G) % s.G
        angle_index = (group * source) % s.G
        cos_t = jnp.zeros_like(re)
        sin_t = jnp.zeros_like(re)
        for a in range(s.G):
            c, w = wave(a, s.G)
            cos_t = jnp.where(angle_index == a, float(c), cos_t)
            sin_t = jnp.where(angle_index == a, float(w) * sign, sin_t)
        add_re = mre * cos_t - mim * sin_t
        add_im = mre * sin_t + mim * cos_t
        out_re = add_re if out_re is None else out_re + add_re
        out_im = add_im if out_im is None else out_im + add_im
    return out_re, out_im


def weighted(values, weights):
    acc = None
    for v, w in zip(values, weights):
        w = float(w)
        if abs(w) < 1e-12:
            continue
        term = v if abs(w - 1) < 1e-12 else (-v if abs(w + 1) < 1e-12 else v * w)
        acc = term if acc is None else acc + term
    return acc


def add(a, b):
    return b if a is None else (a if b is None else a + b)


def sub(a, b):
    return a if b is None else (-b if a is None else a - b)


def block_dft(s, xs):
    even, odd = range(0, s.B, 2), range(1, s.B, 2)
    out = [None] * s.K
    for k in range(s.B // 2 + 1):
        ce, se = wave(np.array(even) * k, 2 * s.B)
        co, so = wave(np.array(odd) * k, 2 * s.B)
        xe, xo = [xs[i] for i in even], [xs[i] for i in odd]
        ere, eim = weighted(xe, ce), weighted(xe, se)
        ore, oim = weighted(xo, co), weighted(xo, so)
        out[k] = (add(ere, ore), add(eim, oim))
        if k != s.B - k:
            out[s.B - k] = (sub(ere, ore), sub(oim, eim))
    return out


def block_back(s, ts):
    half = s.B // 2
    sums = {}
    for k in range(half + 1):
        tre, tim = ts[k]
        if k == half:
            sums[k] = (tre, tre, tim, tim)
        else:
            ure, uim = ts[s.B - k]
            sums[k] = (tre + ure, tre - ure, tim - uim, tim + uim)
    out = []
    for i in range(s.B):
        acc = None
        for k in range(half + 1):
            c, w = wave(i * k, 2 * s.B)
            gain = 1.0 if k == 0 else 2.0
            re = sums[k][i % 2]
            im = sums[k][2 + i % 2]
            acc = add(acc, weighted([re, im], [gain * float(c), gain * float(w)]))
        out.append(acc)
    return out


CHUNK = 32
TAIL = 16
TW_PIECES = 2


def forward_rows(s, load, held, tw, pre, ready=()):
    def body(c, _):
        rows = pl.ds(pl.multiple_of(c * CHUNK, CHUNK), CHUNK)
        group = lane_group(s, CHUNK)
        spec = block_dft(s, [load(i, rows) for i in range(s.B)])
        for k in range(s.K):
            re, im = spec[k]
            pr, pi = pre[k, 0:1, :], pre[k, 1:2, :]
            if k == 0:
                im = jnp.zeros_like(re)
            elif im is None:
                re, im = re * pr, re * pi
            else:
                re, im = re * pr - im * pi, re * pi + im * pr
            re, im = lane_dft(s, re, im, group, 1.0)
            tr, ti = tw[k, 0, rows, :], tw[k, 1, rows, :]
            held[k, rows, 0:LANES] = (re * tr - im * ti).astype(BF16)
            held[k, rows, LANES : 2 * LANES] = (re * ti + im * tr).astype(BF16)
        return 0

    pieces = max(len(ready), 1)
    per = s.R // CHUNK // pieces
    for n in range(pieces):
        if ready:
            ready[n].wait()
        lax.fori_loop(n * per, (n + 1) * per, body, 0, unroll=min(2, per))


def forward_bins(s, held_k, dft):
    o = jnp.dot(dft[...], held_k, preferred_element_type=F32)
    re = o[: s.R, :LANES] + o[s.R :, LANES:]
    im = o[: s.R, LANES:] - o[s.R :, :LANES]
    return re, im


def inverse_bins(s, re, im, k, dft, tw, pre, back):
    z = jnp.concatenate([re.astype(BF16), im.astype(BF16)], axis=1)
    o = jnp.dot(dft[...], z, preferred_element_type=F32)
    re = o[: s.R, :LANES] - o[s.R :, LANES:]
    im = o[: s.R, LANES:] + o[s.R :, :LANES]
    tr, ti = tw[k, 0], tw[k, 1]
    re, im = re * tr + im * ti, im * tr - re * ti
    re, im = lane_dft(s, re, im, lane_group(s, s.R), -1.0)
    pr, pi = pre[k, 0:1, :], pre[k, 1:2, :]
    back[k, 0] = re * pr + im * pi
    back[k, 1] = im * pr - re * pi


def inverse_rows(s, back, rows):
    return block_back(s, [(back[k, 0, rows, :], back[k, 1, rows, :]) for k in range(s.K)])


def each_bin(s, body):
    for k in range(s.K):
        body(k)


def each_chunk(s, body):
    def step(c, _):
        body(pl.ds(pl.multiple_of(c * CHUNK, CHUNK), CHUNK), c)
        return 0

    lax.fori_loop(0, s.R // CHUNK, step, 0, unroll=2)


def params():
    return pltpu.CompilerParams(vmem_limit_bytes=60 * MIB)


def hbm():
    return pl.BlockSpec(memory_space=pl.ANY)


def vmem():
    return pl.BlockSpec(memory_space=pltpu.VMEM)


def cost(flops, nbytes):
    return pl.CostEstimate(flops=int(flops), bytes_accessed=int(nbytes), transcendentals=0)


def pack_kernel(s, n, *refs):
    arrays, owner, slot, out = refs[:n], refs[n], refs[n + 1], refs[n + 2]
    held, held_owner, held_slot, tail, sems = refs[n + 3 :]
    me = lax.axis_index("bins")
    group = lane_group(s, s.R)
    copies = [pltpu.make_async_copy(arrays[a], held.at[a], sems.at[a]) for a in range(n)]
    copies.append(pltpu.make_async_copy(owner, held_owner, sems.at[n]))
    copies.append(pltpu.make_async_copy(slot, held_slot, sems.at[n + 1]))
    for c in copies:
        c.start()
    for a in range(n):
        copies[a].wait()
        for m in range(s.tiles):
            parts = [
                held[a, p * s.R : (p + 1) * s.R, m * LANES : (m + 1) * LANES].astype(F32)
                for p in range(s.G)
            ]
            for q, v in enumerate(lane_transpose(s, parts, group)):
                out[s.G * m + q, a * s.R : (a + 1) * s.R, :] = v.astype(BF16)
    copies[n].wait()
    copies[n + 1].wait()
    tail[...] = jnp.zeros_like(tail)
    tail[: s.B, : s.cols] = held_owner[...].astype(F32)
    tail[: s.B, s.cols : 2 * s.cols] = (held_slot[...] - me * s.send).astype(F32)
    for b in range(s.B):
        out[b, n * s.R :, :] = tail[...].astype(BF16)


def pack(s, owner, slot, *arrays):
    n = len(arrays)
    return pl.pallas_call(
        functools.partial(pack_kernel, s, n),
        out_shape=jax.ShapeDtypeStruct((s.B, n * s.R + TAIL, LANES), BF16),
        in_specs=[hbm()] * (n + 2),
        out_specs=vmem(),
        scratch_shapes=[
            pltpu.VMEM((n, s.T, s.C), BF16),
            pltpu.VMEM((s.B, s.cols), jnp.int32),
            pltpu.VMEM((s.B, s.cols), jnp.int32),
            pltpu.VMEM((TAIL, LANES), F32),
            pltpu.SemaphoreType.DMA((n + 2,)),
        ],
        compiler_params=params(),
        cost_estimate=cost(n * s.T * s.C * 4, n * s.T * s.C * 4),
        name="pack_channels",
    )(*arrays, owner, slot)


def swap_partners(s, parts):
    return [parts[0]] + [
        lax.ppermute(parts[x], "bins", [(b, b ^ x) for b in range(s.B)]) for x in range(1, s.B)
    ]


def project_part_kernel(s, n, index, *refs):
    pieces, weight, start, out = refs[:n], refs[n], refs[n + 1 : -1], refs[-1]
    k = pl.program_id(0)
    for a in range(n):

        @pl.when(k == a)
        def _():
            v = lax.dot_general(
                pieces[a][...],
                weight[...],
                (((1,), (1,)), ((), ())),
                preferred_element_type=F32,
            )
            if a > 0:
                v = out[...] + v
            elif start:
                v = start[0][...] + v
            out[...] = v


def project_part(s, pieces, order, weight, start=()):
    n = len(pieces)
    feats = pieces[0].shape[1]
    return pl.pallas_call(
        functools.partial(project_part_kernel, s, n),
        out_shape=jax.ShapeDtypeStruct((s.T, s.C), F32),
        grid_spec=pltpu.PrefetchScalarGridSpec(
            num_scalar_prefetch=1,
            grid=(n,),
            in_specs=[pl.BlockSpec((s.T, feats), lambda k, o: (0, 0))] * n
            + [pl.BlockSpec((s.C, feats), lambda k, o: (0, o[k]))]
            + [pl.BlockSpec((s.T, s.C), lambda k, o: (0, 0))] * len(start),
            out_specs=pl.BlockSpec((s.T, s.C), lambda k, o: (0, 0)),
        ),
        compiler_params=params(),
        cost_estimate=cost(2 * s.T * s.C * feats * n, 2 * n * feats * (s.T + s.C)),
        name="project_part",
    )(order, *pieces, weight, *start)


def project_finish_kernel(s, n, index, *refs):
    pieces, weight, start, gate = refs[:n], refs[n], refs[n + 1], refs[n + 2]
    dy_out, away, kept, acc = refs[n + 3 :]
    k = pl.program_id(0)
    me = lax.axis_index("bins")
    for a in range(n):

        @pl.when(k == a)
        def _():
            v = lax.dot_general(
                pieces[a][...],
                weight[...],
                (((1,), (1,)), ((), ())),
                preferred_element_type=F32,
            )
            acc[...] = v + (start if a == 0 else acc)[...]

    @pl.when(k == n - 1)
    def _():
        g = acc[...].astype(BF16).astype(F32)
        acc[...] = g
        half = s.T // 2
        mine = me // (s.B // 2)
        kept[...] = acc[pl.ds(pl.multiple_of(mine * half, half), half), :].astype(BF16)
        away[...] = acc[pl.ds(pl.multiple_of((1 - mine) * half, half), half), :].astype(BF16)
        group = lane_group(s, s.R)
        for m in range(s.tiles):
            parts = []
            for p in range(s.G):
                at = (slice(p * s.R, (p + 1) * s.R), slice(m * LANES, (m + 1) * LANES))
                parts.append((acc[at] * gate[at].astype(F32)).astype(BF16).astype(F32))
            for q, v in enumerate(lane_transpose(s, parts, group)):
                dy_out[s.G * m + q] = v.astype(BF16)


def project_finish(s, pieces, order, weight, start, gate):
    n = len(pieces)
    feats = pieces[0].shape[1]
    half = jax.ShapeDtypeStruct((s.T // 2, s.C), BF16)
    return pl.pallas_call(
        functools.partial(project_finish_kernel, s, n),
        out_shape=[jax.ShapeDtypeStruct((s.B, s.R, LANES), BF16), half, half],
        grid_spec=pltpu.PrefetchScalarGridSpec(
            num_scalar_prefetch=1,
            grid=(n,),
            in_specs=[pl.BlockSpec((s.T, feats), lambda k, o: (0, 0))] * n
            + [
                pl.BlockSpec((s.C, feats), lambda k, o: (0, o[k])),
                pl.BlockSpec((s.T, s.C), lambda k, o: (0, 0)),
                pl.BlockSpec((s.T, s.C), lambda k, o: (0, 0)),
            ],
            out_specs=[
                pl.BlockSpec((s.B, s.R, LANES), lambda k, o: (0, 0, 0)),
                pl.BlockSpec(half.shape, lambda k, o: (0, 0)),
                pl.BlockSpec(half.shape, lambda k, o: (0, 0)),
            ],
            scratch_shapes=[pltpu.VMEM((s.T, s.C), F32)],
        ),
        compiler_params=params(),
        cost_estimate=cost(2 * s.T * s.C * feats * n, 2 * n * feats * (s.T + s.C)),
        name="project_far",
    )(order, *pieces, weight, start, gate)


def relay_kernel(s, kept, came, *outs):
    me = lax.axis_index("bins")
    for x in range(s.B // 2):
        at = (me ^ x) % (s.B // 2) * s.cols
        rows = pl.ds(pl.multiple_of(at, s.cols), s.cols)
        outs[x][0] = kept[rows, :]
        outs[x][1] = came[rows, :]


def swap_halves(s, away):
    return lax.ppermute(away, "bins", [(b, b ^ (s.B // 2)) for b in range(s.B)])


def to_columns(s, kept, came):
    half = s.B // 2
    parts = pl.pallas_call(
        functools.partial(relay_kernel, s),
        out_shape=[jax.ShapeDtypeStruct((2, s.cols, s.C), BF16)] * half,
        in_specs=[vmem()] * 2,
        out_specs=[vmem()] * half,
        compiler_params=params(),
        cost_estimate=cost(s.T * s.C, s.T * s.C * 4),
        name="relay_rows",
    )(kept, came)
    return [parts[0]] + [
        lax.ppermute(parts[x], "bins", [(b, b ^ x) for b in range(s.B)]) for x in range(1, half)
    ]


def column_blocks(s, out, rows, c, values):
    group = lane_group(s, CHUNK)
    per = s.cols // CHUNK
    q = c // per
    inner = pl.ds(pl.multiple_of(c % per * CHUNK, CHUNK), CHUNK)
    for i2 in range(s.Q):
        parts = [values[s.G * i2 + a] for a in range(s.G)]
        for p, v in enumerate(lane_transpose(s, parts, group)):
            out[p * s.Q + q, i2, inner, :] = v.astype(BF16)


def conv_kernel(s, xh, skip, dft, tw, pre, x_spec, h_spec, u, held, back):
    x, h = xh.at[:, : s.R, :], xh.at[:, s.R : 2 * s.R, :]
    forward_rows(s, lambda i, rows: x[i, rows, :].astype(F32), held, tw, pre)

    def x_bins(k):
        re, im = forward_bins(s, held[k], dft)
        x_spec[k, 0] = re
        x_spec[k, 1] = im

    each_bin(s, x_bins)
    forward_rows(s, lambda i, rows: h[i, rows, :].astype(F32), held, tw, pre)

    def h_bins(k):
        hre, him = forward_bins(s, held[k], dft)
        h_spec[k, 0] = hre
        h_spec[k, 1] = him
        xre, xim = x_spec[k, 0], x_spec[k, 1]
        inverse_bins(s, xre * hre - xim * him, xre * him + xim * hre, k, dft, tw, pre, back)

    each_bin(s, h_bins)

    def last(rows, c):
        conv = inverse_rows(s, back, rows)
        values = [
            conv[i] * (1.0 / s.N) + skip[...] * x[i, rows, :].astype(F32) for i in range(s.B)
        ]
        column_blocks(s, u, rows, c, values)

    each_chunk(s, last)


def row_choice(s, codes, q):
    per = LANES // s.cols
    target = lax.broadcasted_iota(jnp.int32, (s.B * s.send, LANES), 0).astype(F32)
    lane = lax.broadcasted_iota(jnp.int32, (1, LANES), 1) // s.cols
    hits = []
    for p in range(s.G):
        v = codes[p * s.Q + q].astype(F32)
        v = v * float(s.send) + turn(v, -s.cols)
        for t in range(s.B // per):
            row = v[t * per : t * per + 1, :]
            for a in range(1, per):
                other = turn(v[t * per + a : t * per + a + 1, :], a * s.cols)
                row = jnp.where(lane == a, other, row)
            hits.append(jnp.where(target == row, 1.0, 0.0).astype(BF16))
    return jnp.concatenate(hits, axis=1)


def token_kernel(s, *refs):
    dy_at, came, h_at, skip_at, dft_at, tw_at, pre_at, y_at, out_at = refs[:9]
    dy, codes, h_spec, skip, dft, tw, pre, y_spec, out, held, back, tok, sems, y_sems = refs[9:]
    pieces = TW_PIECES
    part = s.R // pieces
    pairs = [(pre_at, pre), (skip_at, skip), (dy_at, dy)]
    for n in range(pieces):
        rows = slice(n * part, (n + 1) * part)
        pairs.append((tw_at.at[:, :, rows, :], tw.at[:, :, rows, :]))
    pairs += [(dft_at, dft), (h_at, h_spec), (came.at[:, 2 * s.R :, :], codes)]
    copies = [pltpu.make_async_copy(a, b, sems.at[n]) for n, (a, b) in enumerate(pairs)]
    for c in copies:
        c.start()
    for c in copies[:3]:
        c.wait()
    forward_rows(s, lambda i, rows: dy[i, rows, :].astype(F32), held, tw, pre, copies[3:-3])
    copies[-3].wait()
    copies[-2].wait()
    stores = []

    def bins(k):
        yre, yim = forward_bins(s, held[k], dft)
        y_spec[k, 0] = yre
        y_spec[k, 1] = yim
        stores.append(pltpu.make_async_copy(y_spec.at[k], y_at.at[k], y_sems.at[k]))
        stores[-1].start()
        hre, him = h_spec[k, 0], h_spec[k, 1]
        inverse_bins(s, hre * yre + him * yim, hre * yim - him * yre, k, dft, tw, pre, back)

    each_bin(s, bins)

    def last(rows, c):
        back_rows = inverse_rows(s, back, rows)
        for i in range(s.B):
            v = back_rows[i] * (1.0 / s.N) + skip[...] * dy[i, rows, :].astype(F32)
            tok[i, rows, :] = v.astype(BF16)

    each_chunk(s, last)

    copies[-1].wait()
    group = lane_group(s, s.B * s.cols)
    for q in range(s.Q):
        rows = slice(q * s.cols, (q + 1) * s.cols)
        v = jnp.concatenate([tok[i, rows, :] for i in range(s.B)], axis=0)
        zero = jnp.zeros_like(v)
        v = jnp.concatenate([jnp.where(group == p, v, zero) for p in range(s.G)], axis=0)
        o = jnp.dot(row_choice(s, codes, q), v, preferred_element_type=F32)
        at = slice(q * s.send, (q + 1) * s.send)
        for b in range(s.B):
            out[b, at, :] = o[b * s.send : (b + 1) * s.send].astype(BF16)
        sem = y_sems.at[s.K + q]
        stores.append(pltpu.make_async_copy(out.at[:, at, :], out_at.at[:, at, :], sem))
        stores[-1].start()
    for c in stores:
        c.wait()


def filter_kernel(s, x_spec, y_spec, u, dft, tw, pre, *refs):
    outs, (back, lags) = refs[: s.B], refs[s.B :]

    def bins(k):
        xre, xim = x_spec[k, 0], x_spec[k, 1]
        yre, yim = y_spec[k, 0], y_spec[k, 1]
        inverse_bins(s, yre * xre + yim * xim, yim * xre - yre * xim, k, dft, tw, pre, back)

    each_bin(s, bins)
    scale = 1.0 / (s.N * math.sqrt(s.B * s.T))

    def last(rows, c):
        column_blocks(s, lags, rows, c, [v * scale for v in inverse_rows(s, back, rows)])

    each_chunk(s, last)
    me = lax.axis_index("bins")
    for x in range(s.B):
        outs[x][0] = u[me ^ x]
        outs[x][1] = lags[me ^ x]


def columns_kernel(s, *refs):
    parts, refs = refs[: s.B], refs[s.B :]
    rows, (gate_grad, filter_grad, src, g) = refs[: s.B // 2], refs[s.B // 2 :]
    me = lax.axis_index("bins")
    for x in range(s.B):
        src[me ^ x] = parts[x][...]
    for x in range(s.B // 2):
        g[me ^ x] = rows[x][0]
        g[me ^ x ^ (s.B // 2)] = rows[x][1]
    group = lane_group(s, s.cols)
    for i2 in range(s.Q):
        for m in range(s.tiles):
            lanes = slice(m * LANES, (m + 1) * LANES)
            for kind in range(2):
                vs = [src[s.G * m + a, kind, i2].astype(F32) for a in range(s.G)]
                for a, v in enumerate(lane_transpose(s, vs, group)):
                    i = s.G * i2 + a
                    if kind == 0:
                        gate_grad[i, :, lanes] = (v * g[i, :, lanes].astype(F32)).astype(BF16)
                    else:
                        filter_grad[i, :, lanes] = v


def columns(s, parts, rows):
    shape = (s.B, s.cols, s.C)
    return pl.pallas_call(
        functools.partial(columns_kernel, s),
        out_shape=[jax.ShapeDtypeStruct(shape, BF16), jax.ShapeDtypeStruct(shape, F32)],
        in_specs=[vmem()] * (s.B + s.B // 2),
        out_specs=[vmem()] * 2,
        scratch_shapes=[
            pltpu.VMEM((s.B, 2, s.Q, s.cols, LANES), BF16),
            pltpu.VMEM(shape, BF16),
        ],
        compiler_params=params(),
        cost_estimate=cost(s.T * s.C * 8, s.T * s.C * 12),
        name="unpack_columns",
    )(*parts, *rows)


def rows_kernel(s, src, out):
    group = lane_group(s, s.send)
    for m in range(s.tiles):
        for q in range(s.Q):
            rows = slice(q * s.send, (q + 1) * s.send)
            parts = [src[s.G * m + g, rows, :].astype(F32) for g in range(s.G)]
            for p, v in enumerate(lane_transpose(s, parts, group)):
                at = (p * s.Q + q) * s.send
                out[at : at + s.send, m * LANES : (m + 1) * LANES] = v.astype(BF16)


def owner_rows(s, src):
    return pl.pallas_call(
        functools.partial(rows_kernel, s),
        out_shape=jax.ShapeDtypeStruct((s.B * s.send, s.C), BF16),
        in_specs=[vmem()],
        out_specs=vmem(),
        compiler_params=params(),
        cost_estimate=cost(s.T * s.C * 4, s.T * s.C * 8),
        name="unpack_rows",
    )(src)


def exchange(v):
    return lax.all_to_all(v, "bins", split_axis=0, concat_axis=0, tiled=True)


def shards(tokens_in, filters, gate, skip, out_grad, out_weight, owner, slot):
    s = Plan(lax.axis_size("bins"), *tokens_in.shape)
    me = lax.axis_index("bins")
    chan = lax.axis_index("chan")
    nchan = lax.axis_size("chan")
    dft, tw, pre = tables(s)
    spec_shape = jax.ShapeDtypeStruct((s.K, 2, s.R, LANES), F32)
    spec_bytes = s.K * 2 * s.R * LANES * 4
    transform = 2 * 2 * s.R * s.R * 2 * LANES * s.K
    held = pltpu.VMEM((s.K, s.R, 2 * LANES), BF16)
    back = pltpu.VMEM((s.K, 2, s.R, LANES), F32)

    came = exchange(pack(s, owner, slot, tokens_in, filters))

    half = nchan // 2
    core_pairs = [(c, c ^ 1) for c in range(nchan)]
    far_pairs = [(c, (c + half) % nchan) for c in range(nchan)]
    far = lax.ppermute(out_grad, "chan", far_pairs)
    near = lax.ppermute(out_grad, "chan", core_pairs)
    order = jnp.stack([chan, chan ^ 1]).astype(jnp.int32)
    start = project_part(s, [out_grad, near], order, out_weight)
    far, start = lax.optimization_barrier((far, start))
    far_near = lax.ppermute(far, "chan", core_pairs)
    far_order = (order + half) % nchan
    start = project_part(s, [far], far_order[:1], out_weight, (start,))
    packed_dy, away, kept = project_finish(s, [far_near], far_order[1:], out_weight, start, gate)
    dy = exchange(packed_dy)
    g_came = swap_halves(s, away)

    my_skip = lax.dynamic_slice_in_dim(skip, me * s.cb, s.cb)
    my_skip = jnp.tile(my_skip, s.G).reshape(1, LANES)

    cols_shape = (s.Q, s.cols, LANES)
    by_dest = (s.B,) + cols_shape
    x_spec, h_spec, u = pl.pallas_call(
        functools.partial(conv_kernel, s),
        out_shape=[spec_shape, spec_shape, jax.ShapeDtypeStruct(by_dest, BF16)],
        in_specs=[vmem()] * 5,
        out_specs=[vmem()] * 3,
        scratch_shapes=[held, back],
        compiler_params=params(),
        cost_estimate=cost(3 * transform, 4 * spec_bytes),
        name="conv_products",
    )(came, my_skip, dft, tw, pre)

    outbox_shape = (s.B, s.Q * s.send, LANES)
    y_spec, outbox = pl.pallas_call(
        functools.partial(token_kernel, s),
        out_shape=[spec_shape, jax.ShapeDtypeStruct(outbox_shape, BF16)],
        in_specs=[hbm()] * 7,
        out_specs=[hbm()] * 2,
        scratch_shapes=[
            pltpu.VMEM((s.B, s.R, LANES), BF16),
            pltpu.VMEM((s.B, TAIL, LANES), BF16),
            back,
            pltpu.VMEM((1, LANES), F32),
            pltpu.VMEM((2 * s.R, s.R), BF16),
            back,
            pltpu.VMEM((s.K, 2, LANES), F32),
            back,
            pltpu.VMEM(outbox_shape, BF16),
            held,
            back,
            pltpu.VMEM((s.B, s.R, LANES), BF16),
            pltpu.SemaphoreType.DMA((6 + TW_PIECES,)),
            pltpu.SemaphoreType.DMA((s.K + s.Q,)),
        ],
        compiler_params=params(),
        cost_estimate=cost(2 * transform, 3 * spec_bytes),
        name="token_products",
    )(dy, came, h_spec, my_skip, dft, tw, pre)
    outbox, g_came = lax.optimization_barrier((outbox, g_came))
    inbox = exchange(outbox)

    parts = pl.pallas_call(
        functools.partial(filter_kernel, s),
        out_shape=[jax.ShapeDtypeStruct((2,) + cols_shape, BF16)] * s.B,
        in_specs=[vmem()] * 6,
        out_specs=[vmem()] * s.B,
        scratch_shapes=[back, pltpu.VMEM(by_dest, BF16)],
        compiler_params=params(),
        cost_estimate=cost(transform, 3 * spec_bytes),
        name="filter_products",
    )(x_spec, y_spec, u, dft, tw, pre)
    parts = swap_partners(s, parts)
    g_rows = to_columns(s, kept, g_came)

    grad_rows = owner_rows(s, inbox)
    parts, grad_rows = lax.optimization_barrier((parts, grad_rows))
    gate_grad, filter_grad = columns(s, parts, g_rows)
    return (gate_grad, filter_grad, grad_rows)


def solution(mesh):
    return jax.shard_map(
        shards,
        mesh=mesh,
        in_specs=(
            P("bins", "chan"),
            P("bins", "chan"),
            P("bins", "chan"),
            P("chan"),
            P("bins", "chan"),
            P("chan", None),
            P(None, "bins"),
            P(None, "bins"),
        ),
        out_specs=(P(None, "bins", "chan"), P(None, "bins", "chan"), P("bins", "chan")),
        check_vma=False,
    )
```

```python
import functools
import math

import jax
import jax.numpy as jnp
import numpy as np
from jax import lax
from jax.experimental import pallas as pl
from jax.experimental.pallas import tpu as pltpu
from jax.sharding import PartitionSpec as P

LANES = 128
F32 = jnp.float32
BF16 = jnp.bfloat16
MIB = 1 << 20


class Plan:
    def __init__(self, blocks, tok, chans):
        self.B = blocks
        self.T = tok
        self.C = chans
        self.cb = chans // blocks
        self.G = LANES // self.cb
        self.R = tok // self.G
        self.tiles = chans // LANES
        self.cols = tok // blocks
        self.send = 2 * self.cols
        self.Q = blocks // self.G
        self.N = 2 * blocks * tok
        self.K = blocks + 1


def wave(num, den):
    ang = 2.0 * np.pi * (np.asarray(num) % den) / den
    return np.cos(ang), -np.sin(ang)


def tables(s):
    rows = np.arange(s.R)
    lane_e = np.arange(LANES) // s.cb
    dft_c, dft_s = wave(rows[:, None] * rows[None, :], s.R)
    stacked = np.concatenate([dft_c, -dft_s], axis=0)
    k1 = np.arange(s.K)
    tw = wave(rows[None, :, None] * (k1[:, None, None] + 2 * s.B * lane_e[None, None, :]), s.N)
    tw = np.stack(tw, axis=1)
    pre = np.stack(wave(k1[:, None] * lane_e[None, :], 2 * s.B * s.G), axis=1)
    return (
        jnp.asarray(stacked, BF16),
        jnp.asarray(tw, F32),
        jnp.asarray(pre, F32),
    )


def lane_group(s, rows):
    return lax.broadcasted_iota(jnp.int32, (rows, LANES), 1) // s.cb


def turn(v, shift):
    shift = shift % LANES
    return v if shift == 0 else pltpu.roll(v, shift, 1)


def lane_transpose(s, parts, group):
    out = []
    for a in range(s.G):
        acc = None
        for g in range(s.G):
            moved = turn(parts[g], (g - a) * s.cb)
            acc = moved if acc is None else jnp.where(group == g, moved, acc)
        out.append(acc)
    return out


def lane_dft(s, re, im, group, sign):
    if s.G == 1:
        return re, im
    if s.G == 2:
        flip = jnp.where(group == 0, 1.0, -1.0).astype(F32)
        return turn(re, s.cb) + flip * re, turn(im, s.cb) + flip * im
    out_re = out_im = None
    for d in range(s.G):
        mre, mim = turn(re, d * s.cb), turn(im, d * s.cb)
        source = (group - d + s.G) % s.G
        angle_index = (group * source) % s.G
        cos_t = jnp.zeros_like(re)
        sin_t = jnp.zeros_like(re)
        for a in range(s.G):
            c, w = wave(a, s.G)
            cos_t = jnp.where(angle_index == a, float(c), cos_t)
            sin_t = jnp.where(angle_index == a, float(w) * sign, sin_t)
        add_re = mre * cos_t - mim * sin_t
        add_im = mre * sin_t + mim * cos_t
        out_re = add_re if out_re is None else out_re + add_re
        out_im = add_im if out_im is None else out_im + add_im
    return out_re, out_im


def weighted(values, weights):
    acc = None
    for v, w in zip(values, weights):
        w = float(w)
        if abs(w) < 1e-12:
            continue
        term = v if abs(w - 1) < 1e-12 else (-v if abs(w + 1) < 1e-12 else v * w)
        acc = term if acc is None else acc + term
    return acc


def add(a, b):
    return b if a is None else (a if b is None else a + b)


def sub(a, b):
    return a if b is None else (-b if a is None else a - b)


def block_dft(s, xs):
    even, odd = range(0, s.B, 2), range(1, s.B, 2)
    out = [None] * s.K
    for k in range(s.B // 2 + 1):
        ce, se = wave(np.array(even) * k, 2 * s.B)
        co, so = wave(np.array(odd) * k, 2 * s.B)
        xe, xo = [xs[i] for i in even], [xs[i] for i in odd]
        ere, eim = weighted(xe, ce), weighted(xe, se)
        ore, oim = weighted(xo, co), weighted(xo, so)
        out[k] = (add(ere, ore), add(eim, oim))
        if k != s.B - k:
            out[s.B - k] = (sub(ere, ore), sub(oim, eim))
    return out


def block_back(s, ts):
    half = s.B // 2
    sums = {}
    for k in range(half + 1):
        tre, tim = ts[k]
        if k == half:
            sums[k] = (tre, tre, tim, tim)
        else:
            ure, uim = ts[s.B - k]
            sums[k] = (tre + ure, tre - ure, tim - uim, tim + uim)
    out = []
    for i in range(s.B):
        acc = None
        for k in range(half + 1):
            c, w = wave(i * k, 2 * s.B)
            gain = 1.0 if k == 0 else 2.0
            re = sums[k][i % 2]
            im = sums[k][2 + i % 2]
            acc = add(acc, weighted([re, im], [gain * float(c), gain * float(w)]))
        out.append(acc)
    return out


CHUNK = 32
TAIL = 16
TW_PIECES = 2


def forward_rows(s, load, held, tw, pre, ready=()):
    def body(c, _):
        rows = pl.ds(pl.multiple_of(c * CHUNK, CHUNK), CHUNK)
        group = lane_group(s, CHUNK)
        spec = block_dft(s, [load(i, rows) for i in range(s.B)])
        for k in range(s.K):
            re, im = spec[k]
            pr, pi = pre[k, 0:1, :], pre[k, 1:2, :]
            if k == 0:
                im = jnp.zeros_like(re)
            elif im is None:
                re, im = re * pr, re * pi
            else:
                re, im = re * pr - im * pi, re * pi + im * pr
            re, im = lane_dft(s, re, im, group, 1.0)
            tr, ti = tw[k, 0, rows, :], tw[k, 1, rows, :]
            held[k, rows, 0:LANES] = (re * tr - im * ti).astype(BF16)
            held[k, rows, LANES : 2 * LANES] = (re * ti + im * tr).astype(BF16)
        return 0

    pieces = max(len(ready), 1)
    per = s.R // CHUNK // pieces
    for n in range(pieces):
        if ready:
            ready[n].wait()
        lax.fori_loop(n * per, (n + 1) * per, body, 0, unroll=min(2, per))


def forward_bins(s, held_k, dft):
    o = jnp.dot(dft[...], held_k, preferred_element_type=F32)
    re = o[: s.R, :LANES] + o[s.R :, LANES:]
    im = o[: s.R, LANES:] - o[s.R :, :LANES]
    return re, im


def inverse_bins(s, re, im, k, dft, tw, pre, back):
    z = jnp.concatenate([re.astype(BF16), im.astype(BF16)], axis=1)
    o = jnp.dot(dft[...], z, preferred_element_type=F32)
    re = o[: s.R, :LANES] - o[s.R :, LANES:]
    im = o[: s.R, LANES:] + o[s.R :, :LANES]
    tr, ti = tw[k, 0], tw[k, 1]
    re, im = re * tr + im * ti, im * tr - re * ti
    re, im = lane_dft(s, re, im, lane_group(s, s.R), -1.0)
    pr, pi = pre[k, 0:1, :], pre[k, 1:2, :]
    back[k, 0] = re * pr + im * pi
    back[k, 1] = im * pr - re * pi


def inverse_rows(s, back, rows):
    return block_back(s, [(back[k, 0, rows, :], back[k, 1, rows, :]) for k in range(s.K)])


def each_bin(s, body):
    for k in range(s.K):
        body(k)


def each_chunk(s, body):
    def step(c, _):
        body(pl.ds(pl.multiple_of(c * CHUNK, CHUNK), CHUNK), c)
        return 0

    lax.fori_loop(0, s.R // CHUNK, step, 0, unroll=2)


def params(limit=60):
    return pltpu.CompilerParams(vmem_limit_bytes=limit * MIB)


def hbm():
    return pl.BlockSpec(memory_space=pl.ANY)


def vmem():
    return pl.BlockSpec(memory_space=pltpu.VMEM)


def cost(flops, nbytes):
    return pl.CostEstimate(flops=int(flops), bytes_accessed=int(nbytes), transcendentals=0)


def pack_kernel(s, n, *refs):
    arrays, owner, slot, out_at = refs[:n], *refs[n : n + 3]
    out, held, held_owner, held_slot, tail, sems, out_sems = refs[n + 3 :]
    me = lax.axis_index("bins")
    group = lane_group(s, s.R)
    copies = [pltpu.make_async_copy(owner, held_owner, sems.at[n])]
    copies.append(pltpu.make_async_copy(slot, held_slot, sems.at[n + 1]))
    copies += [pltpu.make_async_copy(arrays[a], held.at[a], sems.at[a]) for a in range(n)]
    for c in copies:
        c.start()
    stores = []

    def store(at):
        sem = out_sems.at[len(stores)]
        stores.append(pltpu.make_async_copy(out.at[:, at, :], out_at.at[:, at, :], sem))
        stores[-1].start()

    copies[0].wait()
    copies[1].wait()
    tail[...] = jnp.zeros_like(tail)
    tail[: s.B, : s.cols] = held_owner[...].astype(F32)
    tail[: s.B, s.cols : 2 * s.cols] = (held_slot[...] - me * s.send).astype(F32)
    for b in range(s.B):
        out[b, n * s.R :, :] = tail[...].astype(BF16)
    store(slice(n * s.R, n * s.R + TAIL))
    for a in range(n):
        copies[2 + a].wait()
        for m in range(s.tiles):
            parts = [
                held[a, p * s.R : (p + 1) * s.R, m * LANES : (m + 1) * LANES].astype(F32)
                for p in range(s.G)
            ]
            for q, v in enumerate(lane_transpose(s, parts, group)):
                out[s.G * m + q, a * s.R : (a + 1) * s.R, :] = v.astype(BF16)
        store(slice(a * s.R, (a + 1) * s.R))
    for c in stores:
        c.wait()


def pack(s, owner, slot, *arrays):
    n = len(arrays)
    rows = n * s.R + TAIL
    return pl.pallas_call(
        functools.partial(pack_kernel, s, n),
        out_shape=jax.ShapeDtypeStruct((s.B, rows, LANES), BF16),
        in_specs=[hbm()] * (n + 2),
        out_specs=hbm(),
        scratch_shapes=[
            pltpu.VMEM((s.B, rows, LANES), BF16),
            pltpu.VMEM((n, s.T, s.C), BF16),
            pltpu.VMEM((s.B, s.cols), jnp.int32),
            pltpu.VMEM((s.B, s.cols), jnp.int32),
            pltpu.VMEM((TAIL, LANES), F32),
            pltpu.SemaphoreType.DMA((n + 2,)),
            pltpu.SemaphoreType.DMA((n + 1,)),
        ],
        compiler_params=params(),
        cost_estimate=cost(n * s.T * s.C * 4, n * s.T * s.C * 4),
        name="pack_channels",
    )(*arrays, owner, slot)


def skip_kernel(s, skip, out):
    me = lax.axis_index("bins")
    row = skip[pl.ds(me // s.G, 1), :]
    lane = lane_group(s, 1)
    for q in range(s.G):
        v = lane_transpose(s, [jnp.where(lane == q, row, 0.0)] * s.G, lane)[q]

        @pl.when(me % s.G == q)
        def _():
            out[...] = v


def own_skip(s, skip):
    return pl.pallas_call(
        functools.partial(skip_kernel, s),
        out_shape=jax.ShapeDtypeStruct((1, LANES), F32),
        in_specs=[vmem()],
        out_specs=vmem(),
        compiler_params=params(),
        cost_estimate=cost(LANES, s.C * 4),
        name="own_skip",
    )(skip.reshape(s.tiles, LANES))


def swap_partners(s, parts, after):
    out = [None] * s.B
    out[0] = parts[0]
    for x in [*range(s.B // 2, s.B), *range(s.B // 2 - 1, 0, -1)]:
        part = parts[x]
        if x in after:
            part, out[after[x]] = lax.optimization_barrier((part, out[after[x]]))
        out[x] = lax.ppermute(part, "bins", [(b, b ^ x) for b in range(s.B)])
    return out


def load_parts(s, hops, pieces, weight, piece_held, weight_held, sems):
    chan = lax.axis_index("chan")
    feats = pieces[0].shape[1]
    copies = []
    for a, hop in enumerate(hops):
        at = pl.ds(pl.multiple_of((chan ^ hop) * feats, feats), feats)
        copies.append(
            (
                pltpu.make_async_copy(pieces[a], piece_held.at[a], sems.at[2 * a]),
                pltpu.make_async_copy(weight.at[:, at], weight_held.at[a], sems.at[2 * a + 1]),
            )
        )
    return copies


def multiply(piece, weight):
    return lax.dot_general(
        piece[...], weight[...], (((1,), (1,)), ((), ())), preferred_element_type=F32
    )


def project_part_kernel(s, hops, *refs):
    n = len(hops)
    pieces, weight, refs = refs[:n], refs[n], refs[n + 1 :]
    out_at, out, piece_held, weight_held, sems = refs[-5:]
    start = refs[:-5]
    copies = load_parts(s, hops, pieces, weight, piece_held, weight_held, sems)
    for pair in copies:
        for c in pair:
            c.start()
    if start:
        first = pltpu.make_async_copy(start[0], out, sems.at[2 * n])
        first.start()
    for a, pair in enumerate(copies):
        for c in pair:
            c.wait()
        v = multiply(piece_held.at[a], weight_held.at[a])
        if start and a == 0:
            first.wait()
        out[...] = out[...] + v if start or a else v
    store = pltpu.make_async_copy(out, out_at, sems.at[2 * n + 1])
    store.start()
    store.wait()


def project_scratch(s, n, feats):
    return [
        pltpu.VMEM((s.T, s.C), F32),
        pltpu.VMEM((n, s.T, feats), BF16),
        pltpu.VMEM((n, s.C, feats), BF16),
        pltpu.SemaphoreType.DMA((2 * n + 2,)),
    ]


def project_cost(s, n, feats):
    return cost(s.T * s.C * n, s.T * s.C)


def project_part(s, pieces, hops, weight, start=()):
    n, feats = len(pieces), pieces[0].shape[1]
    return pl.pallas_call(
        functools.partial(project_part_kernel, s, hops),
        out_shape=jax.ShapeDtypeStruct((s.T, s.C), F32),
        in_specs=[hbm()] * (n + 1 + len(start)),
        out_specs=hbm(),
        scratch_shapes=project_scratch(s, n, feats),
        compiler_params=params(40),
        cost_estimate=project_cost(s, n, feats),
        name="project_part",
    )(*pieces, weight, *start)


def project_finish_kernel(s, hops, *refs):
    pieces, weight, start, gate_at, refs = refs[:1], refs[1], refs[2], refs[3], refs[4:]
    dy_at, (away_at, kept_at, acc, piece_held, weight_held, sems) = refs[: s.B], refs[s.B : s.B + 6]
    gate, dy, g, out_sems = refs[s.B + 6 :]
    me = lax.axis_index("bins")
    ((piece_copy, weight_copy),) = load_parts(
        s, hops, pieces, weight, piece_held, weight_held, sems
    )
    first = pltpu.make_async_copy(start, acc, sems.at[2])
    gate_copy = pltpu.make_async_copy(gate_at, gate, sems.at[3])
    loads = (weight_copy, piece_copy, first, gate_copy)
    for c in loads:
        c.start()
    for c in loads:
        c.wait()
    stores = []

    def store(src, dst):
        stores.append(pltpu.make_async_copy(src, dst, out_sems.at[len(stores)]))
        stores[-1].start()

    v = acc[...] + multiply(piece_held.at[0], weight_held.at[0])
    g[...] = v.astype(BF16)
    group = lane_group(s, s.R)
    for m in range(s.tiles):
        lanes = slice(m * LANES, (m + 1) * LANES)
        parts = []
        for p in range(s.G):
            at = (slice(p * s.R, (p + 1) * s.R), lanes)
            parts.append((g[at].astype(F32) * gate[at].astype(F32)).astype(BF16).astype(F32))
        for q, v in enumerate(lane_transpose(s, parts, group)):
            dy[s.G * m + q] = v.astype(BF16)
    for x in range(s.B):
        store(dy.at[me ^ x], dy_at[x])
    half = s.T // 2
    mine = me // (s.B // 2)
    store(g.at[pl.ds(pl.multiple_of(mine * half, half), half), :], kept_at)
    store(g.at[pl.ds(pl.multiple_of((1 - mine) * half, half), half), :], away_at)
    for c in stores:
        c.wait()


def project_finish(s, piece, hop, weight, start, gate):
    feats = piece.shape[1]
    half = jax.ShapeDtypeStruct((s.T // 2, s.C), BF16)
    return pl.pallas_call(
        functools.partial(project_finish_kernel, s, (hop,)),
        out_shape=[jax.ShapeDtypeStruct((s.R, LANES), BF16)] * s.B + [half, half],
        in_specs=[hbm()] * 4,
        out_specs=[hbm()] * (s.B + 2),
        scratch_shapes=project_scratch(s, 1, feats)
        + [
            pltpu.VMEM((s.T, s.C), BF16),
            pltpu.VMEM((s.B, s.R, LANES), BF16),
            pltpu.VMEM((s.T, s.C), BF16),
            pltpu.SemaphoreType.DMA((s.B + 2,)),
        ],
        compiler_params=params(40),
        cost_estimate=project_cost(s, 1, feats),
        name="project_finish",
    )(piece, weight, start, gate)


def swap_halves(s, away):
    return lax.ppermute(away, "bins", [(b, b ^ (s.B // 2)) for b in range(s.B)])


def column_blocks(s, out, rows, c, values):
    group = lane_group(s, CHUNK)
    per = s.cols // CHUNK
    q = c // per
    inner = pl.ds(pl.multiple_of(c % per * CHUNK, CHUNK), CHUNK)
    for i2 in range(s.Q):
        parts = [values[s.G * i2 + a] for a in range(s.G)]
        for p, v in enumerate(lane_transpose(s, parts, group)):
            out[p * s.Q + q, i2, inner, :] = v.astype(BF16)


def tw_copies(s, tw_at, tw, sems, first):
    part = s.R // TW_PIECES
    out = []
    for n in range(TW_PIECES):
        rows = slice(n * part, (n + 1) * part)
        src, dst = tw_at.at[:, :, rows, :], tw.at[:, :, rows, :]
        out.append(pltpu.make_async_copy(src, dst, sems.at[first + n]))
    return out


def spectrum_kernel(s, xh_at, dft_at, tw_at, pre, h_at, h, dft, tw, h_spec, held, sems, out_sems):
    h_copy = pltpu.make_async_copy(xh_at.at[:, s.R : 2 * s.R, :], h, sems.at[0])
    dft_copy = pltpu.make_async_copy(dft_at, dft, sems.at[1])
    tables_in = tw_copies(s, tw_at, tw, sems, 2)
    for c in [h_copy] + tables_in + [dft_copy]:
        c.start()
    h_copy.wait()
    forward_rows(s, lambda i, rows: h[i, rows, :].astype(F32), held, tw, pre, tables_in)
    dft_copy.wait()
    stores = []

    def bins(k):
        re, im = forward_bins(s, held[k], dft)
        h_spec[k, 0] = re
        h_spec[k, 1] = im
        stores.append(pltpu.make_async_copy(h_spec.at[k], h_at.at[k], out_sems.at[k]))
        stores[-1].start()

    each_bin(s, bins)
    for c in stores:
        c.wait()


def row_choice(s, codes, q):
    per = LANES // s.cols
    target = lax.broadcasted_iota(jnp.int32, (s.B * s.send, LANES), 0).astype(F32)
    lane = lax.broadcasted_iota(jnp.int32, (1, LANES), 1) // s.cols
    hits = []
    for p in range(s.G):
        v = codes[p * s.Q + q].astype(F32)
        v = v * float(s.send) + turn(v, -s.cols)
        for t in range(s.B // per):
            row = v[t * per : t * per + 1, :]
            for a in range(1, per):
                other = turn(v[t * per + a : t * per + a + 1, :], a * s.cols)
                row = jnp.where(lane == a, other, row)
            hits.append(jnp.where(target == row, 1.0, 0.0).astype(BF16))
    return jnp.concatenate(hits, axis=1)


def token_kernel(s, *refs):
    parts, refs = refs[: s.B], refs[s.B :]
    came, h_at, skip_at, dft_at, tw_at, pre_at, y_at, out_at = refs[:8]
    dy, codes, h_spec, skip, dft, tw, pre, y_spec, out, held, back, tok, sems, y_sems = refs[8:]
    me = lax.axis_index("bins")
    pairs = [(came.at[:, 2 * s.R :, :], codes), (pre_at, pre), (skip_at, skip)]
    pairs += [(parts[x], dy.at[me ^ x]) for x in range(s.B)]
    pairs += [(dft_at, dft), (h_at, h_spec)]
    copies = [pltpu.make_async_copy(a, b, sems.at[n]) for n, (a, b) in enumerate(pairs)]
    copies[-2:-2] = tw_copies(s, tw_at, tw, sems, len(pairs))
    for c in copies:
        c.start()
    copies[0].wait()
    first = s.B + 3
    for c in copies[1:first]:
        c.wait()
    forward_rows(s, lambda i, rows: dy[i, rows, :].astype(F32), held, tw, pre, copies[first:-2])
    copies[-2].wait()
    copies[-1].wait()
    stores = []

    def bins(k):
        yre, yim = forward_bins(s, held[k], dft)
        y_spec[k, 0] = yre
        y_spec[k, 1] = yim
        stores.append(pltpu.make_async_copy(y_spec.at[k], y_at.at[k], y_sems.at[k]))
        stores[-1].start()
        hre, him = h_spec[k, 0], h_spec[k, 1]
        inverse_bins(s, hre * yre + him * yim, hre * yim - him * yre, k, dft, tw, pre, back)

    each_bin(s, bins)

    def last(rows, c):
        back_rows = inverse_rows(s, back, rows)
        for i in range(s.B):
            v = back_rows[i] * (1.0 / s.N) + skip[...] * dy[i, rows, :].astype(F32)
            tok[i, rows, :] = v.astype(BF16)

    each_chunk(s, last)

    group = lane_group(s, s.B * s.cols)
    for q in range(s.Q):
        rows = slice(q * s.cols, (q + 1) * s.cols)
        v = jnp.concatenate([tok[i, rows, :] for i in range(s.B)], axis=0)
        zero = jnp.zeros_like(v)
        v = jnp.concatenate([jnp.where(group == p, v, zero) for p in range(s.G)], axis=0)
        o = jnp.dot(row_choice(s, codes, q), v, preferred_element_type=F32)
        at = slice(q * s.send, (q + 1) * s.send)
        for b in range(s.B):
            out[b, at, :] = o[b * s.send : (b + 1) * s.send].astype(BF16)
        sem = y_sems.at[s.K + q]
        stores.append(pltpu.make_async_copy(out.at[:, at, :], out_at.at[:, at, :], sem))
        stores[-1].start()
    for c in stores:
        c.wait()


def products_kernel(s, xh_at, h_at, y_at, kept, g_came, skip, dft_at, tw_at, pre, *refs):
    outs, refs = refs[: s.B], refs[s.B :]
    x, h_spec, y_spec, dft, tw, x_spec, held, back, u, lags, sems = refs
    x_copy = pltpu.make_async_copy(xh_at.at[:, : s.R, :], x, sems.at[0])
    dft_copy = pltpu.make_async_copy(dft_at, dft, sems.at[1])
    h_copy = pltpu.make_async_copy(h_at, h_spec, sems.at[2])
    y_copy = pltpu.make_async_copy(y_at, y_spec, sems.at[3])
    tables_in = tw_copies(s, tw_at, tw, sems, 4)
    for c in [x_copy] + tables_in + [dft_copy, h_copy, y_copy]:
        c.start()
    x_copy.wait()
    forward_rows(s, lambda i, rows: x[i, rows, :].astype(F32), held, tw, pre, tables_in)
    dft_copy.wait()
    h_copy.wait()

    def x_bins(k):
        xre, xim = forward_bins(s, held[k], dft)
        x_spec[k, 0] = xre
        x_spec[k, 1] = xim
        hre, him = h_spec[k, 0], h_spec[k, 1]
        inverse_bins(s, xre * hre - xim * him, xre * him + xim * hre, k, dft, tw, pre, back)

    each_bin(s, x_bins)

    def conv_rows(rows, c):
        conv = inverse_rows(s, back, rows)
        values = [
            conv[i] * (1.0 / s.N) + skip[...] * x[i, rows, :].astype(F32) for i in range(s.B)
        ]
        column_blocks(s, u, rows, c, values)

    each_chunk(s, conv_rows)
    y_copy.wait()

    def lag_bins(k):
        xre, xim = x_spec[k, 0], x_spec[k, 1]
        yre, yim = y_spec[k, 0], y_spec[k, 1]
        inverse_bins(s, yre * xre + yim * xim, yim * xre - yre * xim, k, dft, tw, pre, back)

    each_bin(s, lag_bins)
    scale = 1.0 / (s.N * math.sqrt(s.B * s.T))

    def lag_rows(rows, c):
        column_blocks(s, lags, rows, c, [v * scale for v in inverse_rows(s, back, rows)])

    each_chunk(s, lag_rows)
    me = lax.axis_index("bins")
    for d in range(s.B):
        outs[d][0] = u[me ^ d]
        outs[d][1] = lags[me ^ d]
        if d < s.B // 2:
            at = (me ^ d) % (s.B // 2) * s.cols
            rows = pl.ds(pl.multiple_of(at, s.cols), s.cols)
            for m in range(s.tiles):
                lanes = slice(m * LANES, (m + 1) * LANES)
                outs[d][2, m] = kept[rows, lanes]
                outs[d][3, m] = g_came[rows, lanes]


def rows_kernel(s, inbox_at, rows_at, inbox, rows, in_sems, sems):
    copies = []
    for m in range(s.tiles):
        at = slice(m * s.G, (m + 1) * s.G)
        copies.append(pltpu.make_async_copy(inbox_at.at[at], inbox.at[at], in_sems.at[m]))
        copies[-1].start()
    stores = []
    group = lane_group(s, s.send)
    for m in range(s.tiles):
        copies[m].wait()
        lanes = slice(m * LANES, (m + 1) * LANES)
        for q in range(s.Q):
            vs = [
                inbox[s.G * m + a, q * s.send : (q + 1) * s.send, :].astype(F32)
                for a in range(s.G)
            ]
            for p, v in enumerate(lane_transpose(s, vs, group)):
                at = (p * s.Q + q) * s.send
                rows[at : at + s.send, lanes] = v.astype(BF16)
        src, dst = rows.at[:, lanes], rows_at.at[:, lanes]
        stores.append(pltpu.make_async_copy(src, dst, sems.at[m]))
        stores[-1].start()
    for c in stores:
        c.wait()


def owner_rows(s, inbox):
    rows_shape = (s.B * s.send, s.C)
    return pl.pallas_call(
        functools.partial(rows_kernel, s),
        out_shape=jax.ShapeDtypeStruct(rows_shape, BF16),
        in_specs=[hbm()],
        out_specs=hbm(),
        scratch_shapes=[
            pltpu.VMEM(inbox.shape, BF16),
            pltpu.VMEM(rows_shape, BF16),
            pltpu.SemaphoreType.DMA((s.tiles,)),
            pltpu.SemaphoreType.DMA((s.tiles,)),
        ],
        compiler_params=params(40),
        cost_estimate=cost(s.T * s.C * 4, s.T * s.C * 8),
        name="owner_rows",
    )(inbox)


def columns_kernel(s, *refs):
    parts, refs = refs[: s.B], refs[s.B :]
    half = s.B // 2
    gate_at, filter_at, src, g, gate_grad, filter_grad, part_sems, g_sems, sems = refs
    me = lax.axis_index("bins")
    copies = []
    for x in range(s.B):
        block = src.at[me ^ x]
        copies.append(pltpu.make_async_copy(parts[x].at[:2], block, part_sems.at[x]))
    for x in range(half):
        for far in range(2):
            block = g.at[me ^ x ^ (far * half)]
            sem = g_sems.at[2 * x + far]
            copies.append(pltpu.make_async_copy(parts[x].at[2 + far], block, sem))
    for c in copies:
        c.start()
    for c in copies[s.B :]:
        c.wait()
    stores = []
    group = lane_group(s, s.cols)
    for n in range(s.tiles):
        for c in copies[s.G * n : s.G * (n + 1)]:
            c.wait()
        m = me // s.G ^ n
        lanes = pl.ds(pl.multiple_of(m * LANES, LANES), LANES)
        for kind, (out, out_at) in enumerate(((gate_grad, gate_at), (filter_grad, filter_at))):
            for i2 in range(s.Q):
                vs = [src[s.G * m + a, kind, i2].astype(F32) for a in range(s.G)]
                for a, v in enumerate(lane_transpose(s, vs, group)):
                    i = s.G * i2 + a
                    if kind == 0:
                        v = (v * g[i, m].astype(F32)).astype(BF16)
                    out[i, :, lanes] = v
            sem = sems.at[len(stores)]
            at = (slice(None), slice(None), lanes)
            stores.append(pltpu.make_async_copy(out.at[at], out_at.at[at], sem))
            stores[-1].start()
    for c in stores:
        c.wait()


def columns(s, parts):
    cols_shape = (s.B, s.cols, s.C)
    return pl.pallas_call(
        functools.partial(columns_kernel, s),
        out_shape=[
            jax.ShapeDtypeStruct(cols_shape, BF16),
            jax.ShapeDtypeStruct(cols_shape, F32),
        ],
        in_specs=[hbm()] * s.B,
        out_specs=[hbm()] * 2,
        scratch_shapes=[
            pltpu.VMEM((s.B,) + parts[-1].shape, BF16),
            pltpu.VMEM((s.B, s.tiles, s.cols, LANES), BF16),
            pltpu.VMEM(cols_shape, BF16),
            pltpu.VMEM(cols_shape, F32),
            pltpu.SemaphoreType.DMA((s.B,)),
            pltpu.SemaphoreType.DMA((s.B,)),
            pltpu.SemaphoreType.DMA((2 * s.tiles,)),
        ],
        compiler_params=params(40),
        cost_estimate=cost(s.T * s.C * 8, s.T * s.C * 12),
        name="columns",
    )(*parts)


def exchange(v):
    return lax.all_to_all(v, "bins", split_axis=0, concat_axis=0, tiled=True)


def shards(tokens_in, filters, gate, skip, out_grad, out_weight, owner, slot):
    s = Plan(lax.axis_size("bins"), *tokens_in.shape)
    me = lax.axis_index("bins")
    nchan = lax.axis_size("chan")
    dft, tw, pre = tables(s)
    spec_shape = jax.ShapeDtypeStruct((s.K, 2, s.R, LANES), F32)
    spec_bytes = s.K * 2 * s.R * LANES * 4
    transform = 2 * 2 * s.R * s.R * 2 * LANES * s.K
    held = pltpu.VMEM((s.K, s.R, 2 * LANES), BF16)
    back = pltpu.VMEM((s.K, 2, s.R, LANES), F32)

    packed = pack(s, owner, slot, tokens_in, filters)
    came = exchange(packed)

    across = nchan // 2
    core_pairs = [(c, c ^ 1) for c in range(nchan)]
    far = lax.ppermute(out_grad, "chan", [(c, c ^ across) for c in range(nchan)])
    near = lax.ppermute(out_grad, "chan", core_pairs)
    start = project_part(s, [out_grad, near], (0, 1), out_weight)
    my_skip = own_skip(s, skip)
    far, start, my_skip = lax.optimization_barrier((far, start, my_skip))
    far_near = lax.ppermute(far, "chan", core_pairs)
    start = project_part(s, [far], (across,), out_weight, (start,))
    *dy, away, kept = project_finish(s, far_near, across ^ 1, out_weight, start, gate)
    dy = swap_partners(s, dy, {1: 2})

    block = pltpu.VMEM((s.B, s.R, LANES), BF16)
    dft_held = pltpu.VMEM((2 * s.R, s.R), BF16)
    h_spec = pl.pallas_call(
        functools.partial(spectrum_kernel, s),
        out_shape=spec_shape,
        in_specs=[hbm(), hbm(), hbm(), vmem()],
        out_specs=hbm(),
        scratch_shapes=[
            block,
            dft_held,
            back,
            back,
            held,
            pltpu.SemaphoreType.DMA((2 + TW_PIECES,)),
            pltpu.SemaphoreType.DMA((s.K,)),
        ],
        compiler_params=params(),
        cost_estimate=cost(10 * transform, 2 * spec_bytes),
        name="filter_spectrum",
    )(came, dft, tw, pre)

    away, dy[4] = lax.optimization_barrier((away, dy[4]))
    g_came = swap_halves(s, away)

    outbox_shape = (s.B, s.Q * s.send, LANES)
    y_spec, outbox = pl.pallas_call(
        functools.partial(token_kernel, s),
        out_shape=[spec_shape, jax.ShapeDtypeStruct(outbox_shape, BF16)],
        in_specs=[hbm()] * (s.B + 6),
        out_specs=[hbm()] * 2,
        scratch_shapes=[
            block,
            pltpu.VMEM((s.B, TAIL, LANES), BF16),
            back,
            pltpu.VMEM((1, LANES), F32),
            dft_held,
            back,
            pltpu.VMEM((s.K, 2, LANES), F32),
            back,
            pltpu.VMEM(outbox_shape, BF16),
            held,
            back,
            block,
            pltpu.SemaphoreType.DMA((s.B + 5 + TW_PIECES,)),
            pltpu.SemaphoreType.DMA((s.K + s.Q,)),
        ],
        compiler_params=params(),
        cost_estimate=cost(20 * transform, 3 * spec_bytes),
        name="token_products",
    )(*dy, came, h_spec, my_skip, dft, tw, pre)
    outbox, g_came = lax.optimization_barrier((outbox, g_came))
    inbox = exchange(outbox)

    cols_shape = (s.Q, s.cols, LANES)
    by_dest = pltpu.VMEM((s.B,) + cols_shape, BF16)
    parts = pl.pallas_call(
        functools.partial(products_kernel, s),
        out_shape=[
            jax.ShapeDtypeStruct((4 if x < s.B // 2 else 2,) + cols_shape, BF16)
            for x in range(s.B)
        ],
        in_specs=[hbm()] * 3 + [vmem()] * 3 + [hbm()] * 2 + [vmem()],
        out_specs=[vmem()] * s.B,
        scratch_shapes=[
            block,
            back,
            back,
            dft_held,
            back,
            back,
            held,
            back,
            by_dest,
            by_dest,
            pltpu.SemaphoreType.DMA((4 + TW_PIECES,)),
        ],
        compiler_params=params(),
        cost_estimate=cost(3 * transform, 4 * spec_bytes),
        name="conv_and_filter",
    )(came, h_spec, y_spec, kept, g_came, my_skip, dft, tw, pre)
    grad_rows = owner_rows(s, inbox)
    *parts, last = parts
    last, grad_rows = lax.optimization_barrier((last, grad_rows))
    parts = swap_partners(s, [*parts, last], {1: 2})
    gate_grad, filter_grad = columns(s, parts)
    return (gate_grad, filter_grad, grad_rows)


def solution(mesh):
    return jax.shard_map(
        shards,
        mesh=mesh,
        in_specs=(
            P("bins", "chan"),
            P("bins", "chan"),
            P("bins", "chan"),
            P("chan"),
            P("bins", "chan"),
            P("chan", None),
            P(None, "bins"),
            P(None, "bins"),
        ),
        out_specs=(P(None, "bins", "chan"), P(None, "bins", "chan"), P("bins", "chan")),
        check_vma=False,
    )
```

```python
import functools
import math

import jax
import jax.numpy as jnp
import numpy as np
from jax import lax
from jax.experimental import pallas as pl
from jax.experimental.pallas import tpu as pltpu
from jax.sharding import PartitionSpec as P

LANES = 128
F32 = jnp.float32
BF16 = jnp.bfloat16
MIB = 1 << 20


class Plan:
    def __init__(self, blocks, tok, chans):
        self.B = blocks
        self.T = tok
        self.C = chans
        self.cb = chans // blocks
        self.G = LANES // self.cb
        self.R = tok // self.G
        self.tiles = chans // LANES
        self.cols = tok // blocks
        self.send = 2 * self.cols
        self.Q = blocks // self.G
        self.N = 2 * blocks * tok
        self.K = blocks + 1


def wave(num, den):
    ang = 2.0 * np.pi * (np.asarray(num) % den) / den
    return np.cos(ang), -np.sin(ang)


def tables(s):
    rows = np.arange(s.R)
    lane_e = np.arange(LANES) // s.cb
    dft_c, dft_s = wave(rows[:, None] * rows[None, :], s.R)
    stacked = np.concatenate([dft_c, -dft_s], axis=0)
    k1 = np.arange(s.K)
    tw = wave(rows[None, :, None] * (k1[:, None, None] + 2 * s.B * lane_e[None, None, :]), s.N)
    tw = np.stack(tw, axis=1)
    pre = np.stack(wave(k1[:, None] * lane_e[None, :], 2 * s.B * s.G), axis=1)
    return (
        jnp.asarray(stacked, BF16),
        jnp.asarray(tw, F32),
        jnp.asarray(pre, F32),
    )


def lane_group(s, rows):
    return lax.broadcasted_iota(jnp.int32, (rows, LANES), 1) // s.cb


def turn(v, shift):
    shift = shift % LANES
    return v if shift == 0 else pltpu.roll(v, shift, 1)


def lane_transpose(s, parts, group):
    out = []
    for a in range(s.G):
        acc = None
        for g in range(s.G):
            moved = turn(parts[g], (g - a) * s.cb)
            acc = moved if acc is None else jnp.where(group == g, moved, acc)
        out.append(acc)
    return out


def lane_dft(s, re, im, group, sign):
    if s.G == 1:
        return re, im
    if s.G == 2:
        flip = jnp.where(group == 0, 1.0, -1.0).astype(F32)
        return turn(re, s.cb) + flip * re, turn(im, s.cb) + flip * im
    out_re = out_im = None
    for d in range(s.G):
        mre, mim = turn(re, d * s.cb), turn(im, d * s.cb)
        source = (group - d + s.G) % s.G
        angle_index = (group * source) % s.G
        cos_t = jnp.zeros_like(re)
        sin_t = jnp.zeros_like(re)
        for a in range(s.G):
            c, w = wave(a, s.G)
            cos_t = jnp.where(angle_index == a, float(c), cos_t)
            sin_t = jnp.where(angle_index == a, float(w) * sign, sin_t)
        add_re = mre * cos_t - mim * sin_t
        add_im = mre * sin_t + mim * cos_t
        out_re = add_re if out_re is None else out_re + add_re
        out_im = add_im if out_im is None else out_im + add_im
    return out_re, out_im


def weighted(values, weights):
    acc = None
    for v, w in zip(values, weights):
        w = float(w)
        if abs(w) < 1e-12:
            continue
        term = v if abs(w - 1) < 1e-12 else (-v if abs(w + 1) < 1e-12 else v * w)
        acc = term if acc is None else acc + term
    return acc


def add(a, b):
    return b if a is None else (a if b is None else a + b)


def sub(a, b):
    return a if b is None else (-b if a is None else a - b)


def block_dft(s, xs):
    even, odd = range(0, s.B, 2), range(1, s.B, 2)
    out = [None] * s.K
    for k in range(s.B // 2 + 1):
        ce, se = wave(np.array(even) * k, 2 * s.B)
        co, so = wave(np.array(odd) * k, 2 * s.B)
        xe, xo = [xs[i] for i in even], [xs[i] for i in odd]
        ere, eim = weighted(xe, ce), weighted(xe, se)
        ore, oim = weighted(xo, co), weighted(xo, so)
        out[k] = (add(ere, ore), add(eim, oim))
        if k != s.B - k:
            out[s.B - k] = (sub(ere, ore), sub(oim, eim))
    return out


def block_back(s, ts):
    half = s.B // 2
    sums = {}
    for k in range(half + 1):
        tre, tim = ts[k]
        if k == half:
            sums[k] = (tre, tre, tim, tim)
        else:
            ure, uim = ts[s.B - k]
            sums[k] = (tre + ure, tre - ure, tim - uim, tim + uim)
    out = []
    for i in range(s.B):
        acc = None
        for k in range(half + 1):
            c, w = wave(i * k, 2 * s.B)
            gain = 1.0 if k == 0 else 2.0
            re = sums[k][i % 2]
            im = sums[k][2 + i % 2]
            acc = add(acc, weighted([re, im], [gain * float(c), gain * float(w)]))
        out.append(acc)
    return out


CHUNK = 32
TAIL = 16
TW_PIECES = 2


def forward_rows(s, load, held, tw, pre, ready=()):
    def body(c, _):
        rows = pl.ds(pl.multiple_of(c * CHUNK, CHUNK), CHUNK)
        group = lane_group(s, CHUNK)
        spec = block_dft(s, [load(i, rows) for i in range(s.B)])
        for k in range(s.K):
            re, im = spec[k]
            pr, pi = pre[k, 0:1, :], pre[k, 1:2, :]
            if k == 0:
                im = jnp.zeros_like(re)
            elif im is None:
                re, im = re * pr, re * pi
            else:
                re, im = re * pr - im * pi, re * pi + im * pr
            re, im = lane_dft(s, re, im, group, 1.0)
            tr, ti = tw[k, 0, rows, :], tw[k, 1, rows, :]
            held[k, rows, 0:LANES] = (re * tr - im * ti).astype(BF16)
            held[k, rows, LANES : 2 * LANES] = (re * ti + im * tr).astype(BF16)
        return 0

    pieces = max(len(ready), 1)
    per = s.R // CHUNK // pieces
    for n in range(pieces):
        if ready:
            ready[n].wait()
        lax.fori_loop(n * per, (n + 1) * per, body, 0, unroll=min(2, per))


def forward_bins(s, held_k, dft):
    o = jnp.dot(dft[...], held_k, preferred_element_type=F32)
    re = o[: s.R, :LANES] + o[s.R :, LANES:]
    im = o[: s.R, LANES:] - o[s.R :, :LANES]
    return re, im


def inverse_bins(s, re, im, k, dft, tw, pre, back):
    z = jnp.concatenate([re.astype(BF16), im.astype(BF16)], axis=1)
    o = jnp.dot(dft[...], z, preferred_element_type=F32)
    re = o[: s.R, :LANES] - o[s.R :, LANES:]
    im = o[: s.R, LANES:] + o[s.R :, :LANES]
    tr, ti = tw[k, 0], tw[k, 1]
    re, im = re * tr + im * ti, im * tr - re * ti
    re, im = lane_dft(s, re, im, lane_group(s, s.R), -1.0)
    pr, pi = pre[k, 0:1, :], pre[k, 1:2, :]
    back[k, 0] = re * pr + im * pi
    back[k, 1] = im * pr - re * pi


def inverse_rows(s, back, rows):
    return block_back(s, [(back[k, 0, rows, :], back[k, 1, rows, :]) for k in range(s.K)])


def each_bin(s, body):
    for k in range(s.K):
        body(k)


def each_chunk(s, body):
    def step(c, _):
        body(pl.ds(pl.multiple_of(c * CHUNK, CHUNK), CHUNK), c)
        return 0

    lax.fori_loop(0, s.R // CHUNK, step, 0, unroll=2)


def params(limit=60):
    return pltpu.CompilerParams(vmem_limit_bytes=limit * MIB)


def hbm():
    return pl.BlockSpec(memory_space=pl.ANY)


def vmem():
    return pl.BlockSpec(memory_space=pltpu.VMEM)


def cost(flops, nbytes):
    return pl.CostEstimate(flops=int(flops), bytes_accessed=int(nbytes), transcendentals=0)


def pack_kernel(s, n, *refs):
    arrays, owner, slot, out_at = refs[:n], *refs[n : n + 3]
    out, held, held_owner, held_slot, tail, sems, out_sems = refs[n + 3 :]
    me = lax.axis_index("bins")
    group = lane_group(s, s.R)
    copies = [pltpu.make_async_copy(owner, held_owner, sems.at[n])]
    copies.append(pltpu.make_async_copy(slot, held_slot, sems.at[n + 1]))
    copies += [pltpu.make_async_copy(arrays[a], held.at[a], sems.at[a]) for a in range(n)]
    for c in copies:
        c.start()
    stores = []

    def store(at):
        sem = out_sems.at[len(stores)]
        stores.append(pltpu.make_async_copy(out.at[:, at, :], out_at.at[:, at, :], sem))
        stores[-1].start()

    copies[0].wait()
    copies[1].wait()
    tail[...] = jnp.zeros_like(tail)
    tail[: s.B, : s.cols] = held_owner[...].astype(F32)
    tail[: s.B, s.cols : 2 * s.cols] = (held_slot[...] - me * s.send).astype(F32)
    for b in range(s.B):
        out[b, n * s.R :, :] = tail[...].astype(BF16)
    store(slice(n * s.R, n * s.R + TAIL))
    for a in range(n):
        copies[2 + a].wait()
        for m in range(s.tiles):
            parts = [
                held[a, p * s.R : (p + 1) * s.R, m * LANES : (m + 1) * LANES].astype(F32)
                for p in range(s.G)
            ]
            for q, v in enumerate(lane_transpose(s, parts, group)):
                out[s.G * m + q, a * s.R : (a + 1) * s.R, :] = v.astype(BF16)
        store(slice(a * s.R, (a + 1) * s.R))
    for c in stores:
        c.wait()


def pack(s, owner, slot, *arrays):
    n = len(arrays)
    rows = n * s.R + TAIL
    return pl.pallas_call(
        functools.partial(pack_kernel, s, n),
        out_shape=jax.ShapeDtypeStruct((s.B, rows, LANES), BF16),
        in_specs=[hbm()] * (n + 2),
        out_specs=hbm(),
        scratch_shapes=[
            pltpu.VMEM((s.B, rows, LANES), BF16),
            pltpu.VMEM((n, s.T, s.C), BF16),
            pltpu.VMEM((s.B, s.cols), jnp.int32),
            pltpu.VMEM((s.B, s.cols), jnp.int32),
            pltpu.VMEM((TAIL, LANES), F32),
            pltpu.SemaphoreType.DMA((n + 2,)),
            pltpu.SemaphoreType.DMA((n + 1,)),
        ],
        compiler_params=params(),
        cost_estimate=cost(n * s.T * s.C * 4, n * s.T * s.C * 4),
        name="pack_channels",
    )(*arrays, owner, slot)


def skip_kernel(s, skip, out):
    me = lax.axis_index("bins")
    row = skip[pl.ds(me // s.G, 1), :]
    lane = lane_group(s, 1)
    for q in range(s.G):
        v = lane_transpose(s, [jnp.where(lane == q, row, 0.0)] * s.G, lane)[q]

        @pl.when(me % s.G == q)
        def _():
            out[...] = v


def own_skip(s, skip):
    return pl.pallas_call(
        functools.partial(skip_kernel, s),
        out_shape=jax.ShapeDtypeStruct((1, LANES), F32),
        in_specs=[vmem()],
        out_specs=vmem(),
        compiler_params=params(),
        cost_estimate=cost(LANES, s.C * 4),
        name="own_skip",
    )(skip.reshape(s.tiles, LANES))


def swap_partners(s, parts, after):
    out = [None] * s.B
    out[0] = parts[0]
    for x in [*range(s.B // 2, s.B), *range(s.B // 2 - 1, 0, -1)]:
        part = parts[x]
        if x in after:
            part, out[after[x]] = lax.optimization_barrier((part, out[after[x]]))
        out[x] = lax.ppermute(part, "bins", [(b, b ^ x) for b in range(s.B)])
    return out


def load_parts(s, hops, pieces, weight, piece_held, weight_held, sems):
    chan = lax.axis_index("chan")
    feats = pieces[0].shape[1]
    copies = []
    for a, hop in enumerate(hops):
        at = pl.ds(pl.multiple_of((chan ^ hop) * feats, feats), feats)
        copies.append(
            (
                pltpu.make_async_copy(pieces[a], piece_held.at[a], sems.at[2 * a]),
                pltpu.make_async_copy(weight.at[:, at], weight_held.at[a], sems.at[2 * a + 1]),
            )
        )
    return copies


def multiply(piece, weight):
    return lax.dot_general(
        piece[...], weight[...], (((1,), (1,)), ((), ())), preferred_element_type=F32
    )


def project_part_kernel(s, hops, *refs):
    n = len(hops)
    pieces, weight, refs = refs[:n], refs[n], refs[n + 1 :]
    out_at, out, piece_held, weight_held, sems = refs[-5:]
    start = refs[:-5]
    copies = load_parts(s, hops, pieces, weight, piece_held, weight_held, sems)
    for pair in copies:
        for c in pair:
            c.start()
    if start:
        first = pltpu.make_async_copy(start[0], out, sems.at[2 * n])
        first.start()
    for a, pair in enumerate(copies):
        for c in pair:
            c.wait()
        v = multiply(piece_held.at[a], weight_held.at[a])
        if start and a == 0:
            first.wait()
        out[...] = out[...] + v if start or a else v
    store = pltpu.make_async_copy(out, out_at, sems.at[2 * n + 1])
    store.start()
    store.wait()


def project_scratch(s, n, feats):
    return [
        pltpu.VMEM((s.T, s.C), F32),
        pltpu.VMEM((n, s.T, feats), BF16),
        pltpu.VMEM((n, s.C, feats), BF16),
        pltpu.SemaphoreType.DMA((2 * n + 2,)),
    ]


def project_cost(s, n, feats):
    return cost(s.T * s.C * n, s.T * s.C)


def project_part(s, pieces, hops, weight, start=()):
    n, feats = len(pieces), pieces[0].shape[1]
    return pl.pallas_call(
        functools.partial(project_part_kernel, s, hops),
        out_shape=jax.ShapeDtypeStruct((s.T, s.C), F32),
        in_specs=[hbm()] * (n + 1 + len(start)),
        out_specs=hbm(),
        scratch_shapes=project_scratch(s, n, feats),
        compiler_params=params(40),
        cost_estimate=project_cost(s, n, feats),
        name="project_part",
    )(*pieces, weight, *start)


def project_finish_kernel(s, hops, *refs):
    pieces, weight, start, gate_at, refs = refs[:1], refs[1], refs[2], refs[3], refs[4:]
    dy_at, (away_at, kept_at, acc, piece_held, weight_held, sems) = refs[: s.B], refs[s.B : s.B + 6]
    gate, dy, g, out_sems = refs[s.B + 6 :]
    me = lax.axis_index("bins")
    ((piece_copy, weight_copy),) = load_parts(
        s, hops, pieces, weight, piece_held, weight_held, sems
    )
    first = pltpu.make_async_copy(start, acc, sems.at[2])
    gate_copy = pltpu.make_async_copy(gate_at, gate, sems.at[3])
    loads = (weight_copy, piece_copy, first, gate_copy)
    for c in loads:
        c.start()
    for c in loads:
        c.wait()
    stores = []

    def store(src, dst):
        stores.append(pltpu.make_async_copy(src, dst, out_sems.at[len(stores)]))
        stores[-1].start()

    v = acc[...] + multiply(piece_held.at[0], weight_held.at[0])
    g[...] = v.astype(BF16)
    group = lane_group(s, s.R)
    for m in range(s.tiles):
        lanes = slice(m * LANES, (m + 1) * LANES)
        parts = []
        for p in range(s.G):
            at = (slice(p * s.R, (p + 1) * s.R), lanes)
            parts.append((g[at].astype(F32) * gate[at].astype(F32)).astype(BF16).astype(F32))
        for q, v in enumerate(lane_transpose(s, parts, group)):
            dy[s.G * m + q] = v.astype(BF16)
    for x in range(s.B):
        store(dy.at[me ^ x], dy_at[x])
    half = s.T // 2
    mine = me // (s.B // 2)
    store(g.at[pl.ds(pl.multiple_of(mine * half, half), half), :], kept_at)
    store(g.at[pl.ds(pl.multiple_of((1 - mine) * half, half), half), :], away_at)
    for c in stores:
        c.wait()


def project_finish(s, piece, hop, weight, start, gate):
    feats = piece.shape[1]
    half = jax.ShapeDtypeStruct((s.T // 2, s.C), BF16)
    return pl.pallas_call(
        functools.partial(project_finish_kernel, s, (hop,)),
        out_shape=[pltpu.HBM((s.R, LANES), BF16)] * s.B + [pltpu.HBM(half.shape, BF16)] * 2,
        in_specs=[hbm()] * 4,
        out_specs=[hbm()] * (s.B + 2),
        scratch_shapes=project_scratch(s, 1, feats)
        + [
            pltpu.VMEM((s.T, s.C), BF16),
            pltpu.VMEM((s.B, s.R, LANES), BF16),
            pltpu.VMEM((s.T, s.C), BF16),
            pltpu.SemaphoreType.DMA((s.B + 2,)),
        ],
        compiler_params=params(40),
        cost_estimate=project_cost(s, 1, feats),
        name="project_finish",
    )(piece, weight, start, gate)


def swap_halves(s, away):
    return lax.ppermute(away, "bins", [(b, b ^ (s.B // 2)) for b in range(s.B)])


def column_blocks(s, out, rows, c, values):
    group = lane_group(s, CHUNK)
    per = s.cols // CHUNK
    q = c // per
    inner = pl.ds(pl.multiple_of(c % per * CHUNK, CHUNK), CHUNK)
    for i2 in range(s.Q):
        parts = [values[s.G * i2 + a] for a in range(s.G)]
        for p, v in enumerate(lane_transpose(s, parts, group)):
            out[p * s.Q + q, i2, inner, :] = v.astype(BF16)


def tw_copies(s, tw_at, tw, sems, first):
    part = s.R // TW_PIECES
    out = []
    for n in range(TW_PIECES):
        rows = slice(n * part, (n + 1) * part)
        src, dst = tw_at.at[:, :, rows, :], tw.at[:, :, rows, :]
        out.append(pltpu.make_async_copy(src, dst, sems.at[first + n]))
    return out


def spectrum_kernel(s, xh_at, dft_at, tw_at, pre, *refs):
    h_at, x_at, codes_at, h, x, codes, dft, tw, h_spec, held, sems, out_sems = refs
    h_copy = pltpu.make_async_copy(xh_at.at[:, s.R : 2 * s.R, :], h, sems.at[0])
    dft_copy = pltpu.make_async_copy(dft_at, dft, sems.at[1])
    tables_in = tw_copies(s, tw_at, tw, sems, 2)
    base = 2 + TW_PIECES
    through = [
        pltpu.make_async_copy(xh_at.at[:, : s.R, :], x, sems.at[base]),
        pltpu.make_async_copy(xh_at.at[:, 2 * s.R :, :], codes, sems.at[base + 1]),
    ]
    stores = [
        pltpu.make_async_copy(x, x_at, out_sems.at[s.K]),
        pltpu.make_async_copy(codes, codes_at, out_sems.at[s.K + 1]),
    ]
    for c in [h_copy] + tables_in + [dft_copy] + through:
        c.start()
    h_copy.wait()
    forward_rows(s, lambda i, rows: h[i, rows, :].astype(F32), held, tw, pre, tables_in)
    dft_copy.wait()
    for came, kept in zip(through, stores):
        came.wait()
        kept.start()

    def bins(k):
        re, im = forward_bins(s, held[k], dft)
        h_spec[k, 0] = re
        h_spec[k, 1] = im
        stores.append(pltpu.make_async_copy(h_spec.at[k], h_at.at[k], out_sems.at[k]))
        stores[-1].start()

    each_bin(s, bins)
    for c in stores:
        c.wait()


def row_choice(s, codes, q):
    per = LANES // s.cols
    target = lax.broadcasted_iota(jnp.int32, (s.B * s.send, LANES), 0).astype(F32)
    lane = lax.broadcasted_iota(jnp.int32, (1, LANES), 1) // s.cols
    hits = []
    for p in range(s.G):
        v = codes[p * s.Q + q].astype(F32)
        v = v * float(s.send) + turn(v, -s.cols)
        for t in range(s.B // per):
            row = v[t * per : t * per + 1, :]
            for a in range(1, per):
                other = turn(v[t * per + a : t * per + a + 1, :], a * s.cols)
                row = jnp.where(lane == a, other, row)
            hits.append(jnp.where(target == row, 1.0, 0.0).astype(BF16))
    return jnp.concatenate(hits, axis=1)


def arrival_order(s):
    return [*range(s.B // 2, s.B), 0, *range(2, s.B // 2), 1]


def token_kernel(s, *refs):
    parts, refs = refs[: s.B], refs[s.B :]
    codes_at, h_at, skip_at, dft_at, tw_at, pre_at, y_at, out_at = refs[:8]
    dy, codes, h_spec, skip, dft, tw, pre, y_spec, out, held, back, tok, sems, y_sems = refs[8:]
    me = lax.axis_index("bins")
    pairs = [(codes_at, codes), (pre_at, pre), (skip_at, skip)]
    pairs += [(parts[n], dy.at[me ^ x]) for n, x in enumerate(arrival_order(s))]
    pairs += [(dft_at, dft), (h_at, h_spec)]
    copies = [pltpu.make_async_copy(a, b, sems.at[n]) for n, (a, b) in enumerate(pairs)]
    copies[-2:-2] = tw_copies(s, tw_at, tw, sems, len(pairs))
    for c in copies:
        c.start()
    copies[0].wait()
    first = s.B + 3
    for c in copies[1:first]:
        c.wait()
    forward_rows(s, lambda i, rows: dy[i, rows, :].astype(F32), held, tw, pre, copies[first:-2])
    copies[-2].wait()
    copies[-1].wait()
    stores = []

    def bins(k):
        yre, yim = forward_bins(s, held[k], dft)
        y_spec[k, 0] = yre
        y_spec[k, 1] = yim
        stores.append(pltpu.make_async_copy(y_spec.at[k], y_at.at[k], y_sems.at[k]))
        stores[-1].start()
        hre, him = h_spec[k, 0], h_spec[k, 1]
        inverse_bins(s, hre * yre + him * yim, hre * yim - him * yre, k, dft, tw, pre, back)

    each_bin(s, bins)

    def last(rows, c):
        back_rows = inverse_rows(s, back, rows)
        for i in range(s.B):
            v = back_rows[i] * (1.0 / s.N) + skip[...] * dy[i, rows, :].astype(F32)
            tok[i, rows, :] = v.astype(BF16)

    each_chunk(s, last)

    group = lane_group(s, s.B * s.cols)
    for q in range(s.Q):
        rows = slice(q * s.cols, (q + 1) * s.cols)
        v = jnp.concatenate([tok[i, rows, :] for i in range(s.B)], axis=0)
        zero = jnp.zeros_like(v)
        v = jnp.concatenate([jnp.where(group == p, v, zero) for p in range(s.G)], axis=0)
        o = jnp.dot(row_choice(s, codes, q), v, preferred_element_type=F32)
        at = slice(q * s.send, (q + 1) * s.send)
        for b in range(s.B):
            out[b, at, :] = o[b * s.send : (b + 1) * s.send].astype(BF16)
        sem = y_sems.at[s.K + q]
        stores.append(pltpu.make_async_copy(out.at[:, at, :], out_at.at[:, at, :], sem))
        stores[-1].start()
    for c in stores:
        c.wait()


def products_kernel(s, x_at, h_at, y_at, kept, g_came, skip, dft_at, tw_at, pre, *refs):
    outs, refs = refs[: s.B], refs[s.B :]
    x, h_spec, y_spec, dft, tw, x_spec, held, back, u, lags, sems = refs
    x_copy = pltpu.make_async_copy(x_at, x, sems.at[0])
    dft_copy = pltpu.make_async_copy(dft_at, dft, sems.at[1])
    h_copy = pltpu.make_async_copy(h_at, h_spec, sems.at[2])
    y_copy = pltpu.make_async_copy(y_at, y_spec, sems.at[3])
    tables_in = tw_copies(s, tw_at, tw, sems, 4)
    for c in [x_copy] + tables_in + [dft_copy, h_copy, y_copy]:
        c.start()
    x_copy.wait()
    forward_rows(s, lambda i, rows: x[i, rows, :].astype(F32), held, tw, pre, tables_in)
    dft_copy.wait()
    h_copy.wait()

    def x_bins(k):
        xre, xim = forward_bins(s, held[k], dft)
        x_spec[k, 0] = xre
        x_spec[k, 1] = xim
        hre, him = h_spec[k, 0], h_spec[k, 1]
        inverse_bins(s, xre * hre - xim * him, xre * him + xim * hre, k, dft, tw, pre, back)

    each_bin(s, x_bins)

    def conv_rows(rows, c):
        conv = inverse_rows(s, back, rows)
        values = [
            conv[i] * (1.0 / s.N) + skip[...] * x[i, rows, :].astype(F32) for i in range(s.B)
        ]
        column_blocks(s, u, rows, c, values)

    each_chunk(s, conv_rows)
    y_copy.wait()

    def lag_bins(k):
        xre, xim = x_spec[k, 0], x_spec[k, 1]
        yre, yim = y_spec[k, 0], y_spec[k, 1]
        inverse_bins(s, yre * xre + yim * xim, yim * xre - yre * xim, k, dft, tw, pre, back)

    each_bin(s, lag_bins)
    scale = 1.0 / (s.N * math.sqrt(s.B * s.T))

    def lag_rows(rows, c):
        column_blocks(s, lags, rows, c, [v * scale for v in inverse_rows(s, back, rows)])

    each_chunk(s, lag_rows)
    me = lax.axis_index("bins")
    for d in range(s.B):
        outs[d][0] = u[me ^ d]
        outs[d][1] = lags[me ^ d]
        if d < s.B // 2:
            at = (me ^ d) % (s.B // 2) * s.cols
            rows = pl.ds(pl.multiple_of(at, s.cols), s.cols)
            for m in range(s.tiles):
                lanes = slice(m * LANES, (m + 1) * LANES)
                outs[d][2, m] = kept[rows, lanes]
                outs[d][3, m] = g_came[rows, lanes]


def rows_kernel(s, inbox_at, rows_at, inbox, rows, in_sems, sems):
    copies = []
    for m in range(s.tiles):
        at = slice(m * s.G, (m + 1) * s.G)
        copies.append(pltpu.make_async_copy(inbox_at.at[at], inbox.at[at], in_sems.at[m]))
        copies[-1].start()
    stores = []
    group = lane_group(s, s.send)
    for m in range(s.tiles):
        copies[m].wait()
        lanes = slice(m * LANES, (m + 1) * LANES)
        for q in range(s.Q):
            vs = [
                inbox[s.G * m + a, q * s.send : (q + 1) * s.send, :].astype(F32)
                for a in range(s.G)
            ]
            for p, v in enumerate(lane_transpose(s, vs, group)):
                at = (p * s.Q + q) * s.send
                rows[at : at + s.send, lanes] = v.astype(BF16)
        src, dst = rows.at[:, lanes], rows_at.at[:, lanes]
        stores.append(pltpu.make_async_copy(src, dst, sems.at[m]))
        stores[-1].start()
    for c in stores:
        c.wait()


def owner_rows(s, inbox):
    rows_shape = (s.B * s.send, s.C)
    return pl.pallas_call(
        functools.partial(rows_kernel, s),
        out_shape=jax.ShapeDtypeStruct(rows_shape, BF16),
        in_specs=[hbm()],
        out_specs=hbm(),
        scratch_shapes=[
            pltpu.VMEM(inbox.shape, BF16),
            pltpu.VMEM(rows_shape, BF16),
            pltpu.SemaphoreType.DMA((s.tiles,)),
            pltpu.SemaphoreType.DMA((s.tiles,)),
        ],
        compiler_params=params(40),
        cost_estimate=cost(s.T * s.C * 4, s.T * s.C * 8),
        name="owner_rows",
    )(inbox)


def columns_kernel(s, *refs):
    parts, refs = refs[: s.B], refs[s.B :]
    half = s.B // 2
    gate_at, filter_at, src, g, gate_grad, filter_grad, part_sems, g_sems, sems = refs
    me = lax.axis_index("bins")
    copies = []
    for x in range(s.B):
        block = src.at[me ^ x]
        copies.append(pltpu.make_async_copy(parts[x].at[:2], block, part_sems.at[x]))
    for x in range(half):
        for far in range(2):
            block = g.at[me ^ x ^ (far * half)]
            sem = g_sems.at[2 * x + far]
            copies.append(pltpu.make_async_copy(parts[x].at[2 + far], block, sem))
    for c in copies:
        c.start()
    for c in copies[s.B :]:
        c.wait()
    stores = []
    group = lane_group(s, s.cols)
    for n in range(s.tiles):
        for c in copies[s.G * n : s.G * (n + 1)]:
            c.wait()
        m = me // s.G ^ n
        lanes = pl.ds(pl.multiple_of(m * LANES, LANES), LANES)
        for kind, (out, out_at) in enumerate(((gate_grad, gate_at), (filter_grad, filter_at))):
            for i2 in range(s.Q):
                vs = [src[s.G * m + a, kind, i2].astype(F32) for a in range(s.G)]
                for a, v in enumerate(lane_transpose(s, vs, group)):
                    i = s.G * i2 + a
                    if kind == 0:
                        v = (v * g[i, m].astype(F32)).astype(BF16)
                    out[i, :, lanes] = v
            sem = sems.at[len(stores)]
            at = (slice(None), slice(None), lanes)
            stores.append(pltpu.make_async_copy(out.at[at], out_at.at[at], sem))
            stores[-1].start()
    for c in stores:
        c.wait()


def columns(s, parts):
    cols_shape = (s.B, s.cols, s.C)
    return pl.pallas_call(
        functools.partial(columns_kernel, s),
        out_shape=[
            jax.ShapeDtypeStruct(cols_shape, BF16),
            jax.ShapeDtypeStruct(cols_shape, F32),
        ],
        in_specs=[hbm()] * s.B,
        out_specs=[hbm()] * 2,
        scratch_shapes=[
            pltpu.VMEM((s.B,) + parts[-1].shape, BF16),
            pltpu.VMEM((s.B, s.tiles, s.cols, LANES), BF16),
            pltpu.VMEM(cols_shape, BF16),
            pltpu.VMEM(cols_shape, F32),
            pltpu.SemaphoreType.DMA((s.B,)),
            pltpu.SemaphoreType.DMA((s.B,)),
            pltpu.SemaphoreType.DMA((2 * s.tiles,)),
        ],
        compiler_params=params(56),
        cost_estimate=cost(s.T * s.C * 8, s.T * s.C * 12),
        name="columns",
    )(*parts)


def exchange(v):
    return lax.all_to_all(v, "bins", split_axis=0, concat_axis=0, tiled=True)


def shards(tokens_in, filters, gate, skip, out_grad, out_weight, owner, slot):
    s = Plan(lax.axis_size("bins"), *tokens_in.shape)
    me = lax.axis_index("bins")
    nchan = lax.axis_size("chan")
    dft, tw, pre = tables(s)
    spec_shape = jax.ShapeDtypeStruct((s.K, 2, s.R, LANES), F32)
    spec_bytes = s.K * 2 * s.R * LANES * 4
    transform = 2 * 2 * s.R * s.R * 2 * LANES * s.K
    held = pltpu.VMEM((s.K, s.R, 2 * LANES), BF16)
    back = pltpu.VMEM((s.K, 2, s.R, LANES), F32)

    packed = pack(s, owner, slot, tokens_in, filters)
    came = exchange(packed)

    across = nchan // 2
    core_pairs = [(c, c ^ 1) for c in range(nchan)]
    far = lax.ppermute(out_grad, "chan", [(c, c ^ across) for c in range(nchan)])
    near = lax.ppermute(out_grad, "chan", core_pairs)
    start = project_part(s, [out_grad], (0,), out_weight)
    my_skip = own_skip(s, skip)
    far, start, my_skip = lax.optimization_barrier((far, start, my_skip))
    far_near = lax.ppermute(far, "chan", core_pairs)
    start = project_part(s, [near, far], (1, across), out_weight, (start,))
    *dy, away, kept = project_finish(s, far_near, across ^ 1, out_weight, start, gate)
    dy = swap_partners(s, dy, {1: 2})

    block = pltpu.VMEM((s.B, s.R, LANES), BF16)
    dft_held = pltpu.VMEM((2 * s.R, s.R), BF16)
    h_spec, x, codes = pl.pallas_call(
        functools.partial(spectrum_kernel, s),
        out_shape=[
            pltpu.HBM(spec_shape.shape, F32),
            pltpu.HBM((s.B, s.R, LANES), BF16),
            pltpu.HBM((s.B, TAIL, LANES), BF16),
        ],
        in_specs=[hbm(), hbm(), hbm(), vmem()],
        out_specs=[hbm()] * 3,
        scratch_shapes=[
            block,
            block,
            pltpu.VMEM((s.B, TAIL, LANES), BF16),
            dft_held,
            back,
            back,
            held,
            pltpu.SemaphoreType.DMA((4 + TW_PIECES,)),
            pltpu.SemaphoreType.DMA((s.K + 2,)),
        ],
        compiler_params=params(58),
        cost_estimate=cost(10 * transform, 2 * spec_bytes),
        name="filter_spectrum",
    )(came, dft, tw, pre)

    away, dy[s.B - 1] = lax.optimization_barrier((away, dy[s.B - 1]))
    g_came = swap_halves(s, away)

    outbox_shape = (s.B, s.Q * s.send, LANES)
    y_spec, outbox = pl.pallas_call(
        functools.partial(token_kernel, s),
        out_shape=[pltpu.HBM(spec_shape.shape, F32), pltpu.HBM(outbox_shape, BF16)],
        in_specs=[hbm()] * (s.B + 6),
        out_specs=[hbm()] * 2,
        scratch_shapes=[
            block,
            pltpu.VMEM((s.B, TAIL, LANES), BF16),
            back,
            pltpu.VMEM((1, LANES), F32),
            dft_held,
            back,
            pltpu.VMEM((s.K, 2, LANES), F32),
            back,
            pltpu.VMEM(outbox_shape, BF16),
            held,
            back,
            block,
            pltpu.SemaphoreType.DMA((s.B + 5 + TW_PIECES,)),
            pltpu.SemaphoreType.DMA((s.K + s.Q,)),
        ],
        compiler_params=params(60),
        cost_estimate=cost(20 * transform, 3 * spec_bytes),
        name="token_products",
    )(*[dy[x] for x in arrival_order(s)], codes, h_spec, my_skip, dft, tw, pre)
    outbox, g_came = lax.optimization_barrier((outbox, g_came))
    inbox = exchange(outbox)

    cols_shape = (s.Q, s.cols, LANES)
    by_dest = pltpu.VMEM((s.B,) + cols_shape, BF16)
    parts = pl.pallas_call(
        functools.partial(products_kernel, s),
        out_shape=[
            jax.ShapeDtypeStruct((4 if x < s.B // 2 else 2,) + cols_shape, BF16)
            for x in range(s.B)
        ],
        in_specs=[hbm()] * 3 + [vmem()] * 3 + [hbm()] * 2 + [vmem()],
        out_specs=[vmem()] * s.B,
        scratch_shapes=[
            block,
            back,
            back,
            dft_held,
            back,
            back,
            held,
            back,
            by_dest,
            by_dest,
            pltpu.SemaphoreType.DMA((4 + TW_PIECES,)),
        ],
        compiler_params=params(),
        cost_estimate=cost(3 * transform, 4 * spec_bytes),
        name="conv_and_filter",
    )(x, h_spec, y_spec, kept, g_came, my_skip, dft, tw, pre)
    grad_rows = owner_rows(s, inbox)
    *parts, last = parts
    last, grad_rows = lax.optimization_barrier((last, grad_rows))
    parts = swap_partners(s, [*parts, last], {1: 2})
    gate_grad, filter_grad = columns(s, parts)
    return (gate_grad, filter_grad, grad_rows)


def solution(mesh):
    return jax.shard_map(
        shards,
        mesh=mesh,
        in_specs=(
            P("bins", "chan"),
            P("bins", "chan"),
            P("bins", "chan"),
            P("chan"),
            P("bins", "chan"),
            P("chan", None),
            P(None, "bins"),
            P(None, "bins"),
        ),
        out_specs=(P(None, "bins", "chan"), P(None, "bins", "chan"), P("bins", "chan")),
        check_vma=False,
    )
```

```python
import functools
import math

import jax
import jax.numpy as jnp
import numpy as np
from jax import lax
from jax.experimental import pallas as pl
from jax.experimental.pallas import tpu as pltpu
from jax.sharding import PartitionSpec as P

LANES = 128
F32 = jnp.float32
BF16 = jnp.bfloat16
MIB = 1 << 20


class Plan:
    def __init__(self, blocks, tok, chans):
        self.B = blocks
        self.T = tok
        self.C = chans
        self.cb = chans // blocks
        self.G = LANES // self.cb
        self.R = tok // self.G
        self.tiles = chans // LANES
        self.cols = tok // blocks
        self.send = 2 * self.cols
        self.Q = blocks // self.G
        self.N = 2 * blocks * tok
        self.K = blocks + 1


def wave(num, den):
    ang = 2.0 * np.pi * (np.asarray(num) % den) / den
    return np.cos(ang), -np.sin(ang)


def tables(s):
    rows = np.arange(s.R)
    lane_e = np.arange(LANES) // s.cb
    dft_c, dft_s = wave(rows[:, None] * rows[None, :], s.R)
    stacked = np.concatenate([dft_c, -dft_s], axis=0)
    k1 = np.arange(s.K)
    tw = wave(rows[None, :, None] * (k1[:, None, None] + 2 * s.B * lane_e[None, None, :]), s.N)
    tw = np.stack(tw, axis=1)
    pre = np.stack(wave(k1[:, None] * lane_e[None, :], 2 * s.B * s.G), axis=1)
    return (
        jnp.asarray(stacked, BF16),
        jnp.asarray(tw, F32),
        jnp.asarray(pre, F32),
    )


def lane_group(s, rows):
    return lax.broadcasted_iota(jnp.int32, (rows, LANES), 1) // s.cb


def turn(v, shift):
    shift = shift % LANES
    return v if shift == 0 else pltpu.roll(v, shift, 1)


def lane_transpose(s, parts, group):
    out = []
    for a in range(s.G):
        acc = None
        for g in range(s.G):
            moved = turn(parts[g], (g - a) * s.cb)
            acc = moved if acc is None else jnp.where(group == g, moved, acc)
        out.append(acc)
    return out


def lane_dft(s, re, im, group, sign):
    if s.G == 1:
        return re, im
    if s.G == 2:
        flip = jnp.where(group == 0, 1.0, -1.0).astype(F32)
        return turn(re, s.cb) + flip * re, turn(im, s.cb) + flip * im
    out_re = out_im = None
    for d in range(s.G):
        mre, mim = turn(re, d * s.cb), turn(im, d * s.cb)
        source = (group - d + s.G) % s.G
        angle_index = (group * source) % s.G
        cos_t = jnp.zeros_like(re)
        sin_t = jnp.zeros_like(re)
        for a in range(s.G):
            c, w = wave(a, s.G)
            cos_t = jnp.where(angle_index == a, float(c), cos_t)
            sin_t = jnp.where(angle_index == a, float(w) * sign, sin_t)
        add_re = mre * cos_t - mim * sin_t
        add_im = mre * sin_t + mim * cos_t
        out_re = add_re if out_re is None else out_re + add_re
        out_im = add_im if out_im is None else out_im + add_im
    return out_re, out_im


def weighted(values, weights):
    acc = None
    for v, w in zip(values, weights):
        w = float(w)
        if abs(w) < 1e-12:
            continue
        term = v if abs(w - 1) < 1e-12 else (-v if abs(w + 1) < 1e-12 else v * w)
        acc = term if acc is None else acc + term
    return acc


def add(a, b):
    return b if a is None else (a if b is None else a + b)


def sub(a, b):
    return a if b is None else (-b if a is None else a - b)


def block_dft(s, xs):
    even, odd = range(0, s.B, 2), range(1, s.B, 2)
    out = [None] * s.K
    for k in range(s.B // 2 + 1):
        ce, se = wave(np.array(even) * k, 2 * s.B)
        co, so = wave(np.array(odd) * k, 2 * s.B)
        xe, xo = [xs[i] for i in even], [xs[i] for i in odd]
        ere, eim = weighted(xe, ce), weighted(xe, se)
        ore, oim = weighted(xo, co), weighted(xo, so)
        out[k] = (add(ere, ore), add(eim, oim))
        if k != s.B - k:
            out[s.B - k] = (sub(ere, ore), sub(oim, eim))
    return out


def block_back(s, ts):
    half = s.B // 2
    sums = {}
    for k in range(half + 1):
        tre, tim = ts[k]
        if k == half:
            sums[k] = (tre, tre, tim, tim)
        else:
            ure, uim = ts[s.B - k]
            sums[k] = (tre + ure, tre - ure, tim - uim, tim + uim)
    out = []
    for i in range(s.B):
        acc = None
        for k in range(half + 1):
            c, w = wave(i * k, 2 * s.B)
            gain = 1.0 if k == 0 else 2.0
            re = sums[k][i % 2]
            im = sums[k][2 + i % 2]
            acc = add(acc, weighted([re, im], [gain * float(c), gain * float(w)]))
        out.append(acc)
    return out


CHUNK = 32
TAIL = 16
TW_PIECES = 2


def forward_rows(s, load, held, tw, pre, ready=()):
    def body(c, _):
        rows = pl.ds(pl.multiple_of(c * CHUNK, CHUNK), CHUNK)
        group = lane_group(s, CHUNK)
        spec = block_dft(s, [load(i, rows) for i in range(s.B)])
        for k in range(s.K):
            re, im = spec[k]
            pr, pi = pre[k, 0:1, :], pre[k, 1:2, :]
            if k == 0:
                im = jnp.zeros_like(re)
            elif im is None:
                re, im = re * pr, re * pi
            else:
                re, im = re * pr - im * pi, re * pi + im * pr
            re, im = lane_dft(s, re, im, group, 1.0)
            tr, ti = tw[k, 0, rows, :], tw[k, 1, rows, :]
            held[k, rows, 0:LANES] = (re * tr - im * ti).astype(BF16)
            held[k, rows, LANES : 2 * LANES] = (re * ti + im * tr).astype(BF16)
        return 0

    pieces = max(len(ready), 1)
    per = s.R // CHUNK // pieces
    for n in range(pieces):
        if ready:
            ready[n].wait()
        lax.fori_loop(n * per, (n + 1) * per, body, 0, unroll=min(2, per))


def forward_bins(s, held_k, dft):
    o = jnp.dot(dft[...], held_k, preferred_element_type=F32)
    re = o[: s.R, :LANES] + o[s.R :, LANES:]
    im = o[: s.R, LANES:] - o[s.R :, :LANES]
    return re, im


def inverse_bins(s, re, im, k, dft, tw, pre, back):
    z = jnp.concatenate([re.astype(BF16), im.astype(BF16)], axis=1)
    o = jnp.dot(dft[...], z, preferred_element_type=F32)
    re = o[: s.R, :LANES] - o[s.R :, LANES:]
    im = o[: s.R, LANES:] + o[s.R :, :LANES]
    tr, ti = tw[k, 0], tw[k, 1]
    re, im = re * tr + im * ti, im * tr - re * ti
    re, im = lane_dft(s, re, im, lane_group(s, s.R), -1.0)
    pr, pi = pre[k, 0:1, :], pre[k, 1:2, :]
    back[k, 0] = re * pr + im * pi
    back[k, 1] = im * pr - re * pi


def inverse_rows(s, back, rows):
    return block_back(s, [(back[k, 0, rows, :], back[k, 1, rows, :]) for k in range(s.K)])


def each_bin(s, body):
    for k in range(s.K):
        body(k)


def each_chunk(s, body):
    def step(c, _):
        body(pl.ds(pl.multiple_of(c * CHUNK, CHUNK), CHUNK), c)
        return 0

    lax.fori_loop(0, s.R // CHUNK, step, 0, unroll=2)


def params(limit=60):
    return pltpu.CompilerParams(vmem_limit_bytes=limit * MIB)


def hbm():
    return pl.BlockSpec(memory_space=pl.ANY)


def vmem():
    return pl.BlockSpec(memory_space=pltpu.VMEM)


def cost(flops, nbytes):
    return pl.CostEstimate(flops=int(flops), bytes_accessed=int(nbytes), transcendentals=0)


def pack_kernel(s, n, *refs):
    arrays, owner, slot, out_at = refs[:n], *refs[n : n + 3]
    out, held, held_owner, held_slot, tail, sems, out_sems = refs[n + 3 :]
    me = lax.axis_index("bins")
    group = lane_group(s, s.R)
    copies = [pltpu.make_async_copy(owner, held_owner, sems.at[n])]
    copies.append(pltpu.make_async_copy(slot, held_slot, sems.at[n + 1]))
    copies += [pltpu.make_async_copy(arrays[a], held.at[a], sems.at[a]) for a in range(n)]
    for c in copies:
        c.start()
    stores = []

    def store(at):
        sem = out_sems.at[len(stores)]
        stores.append(pltpu.make_async_copy(out.at[:, at, :], out_at.at[:, at, :], sem))
        stores[-1].start()

    copies[0].wait()
    copies[1].wait()
    tail[...] = jnp.zeros_like(tail)
    tail[: s.B, : s.cols] = held_owner[...].astype(F32)
    tail[: s.B, s.cols : 2 * s.cols] = (held_slot[...] - me * s.send).astype(F32)
    for b in range(s.B):
        out[b, n * s.R :, :] = tail[...].astype(BF16)
    store(slice(n * s.R, n * s.R + TAIL))
    for a in range(n):
        copies[2 + a].wait()
        for m in range(s.tiles):
            parts = [
                held[a, p * s.R : (p + 1) * s.R, m * LANES : (m + 1) * LANES].astype(F32)
                for p in range(s.G)
            ]
            for q, v in enumerate(lane_transpose(s, parts, group)):
                out[s.G * m + q, a * s.R : (a + 1) * s.R, :] = v.astype(BF16)
        store(slice(a * s.R, (a + 1) * s.R))
    for c in stores:
        c.wait()


def pack(s, owner, slot, *arrays):
    n = len(arrays)
    rows = n * s.R + TAIL
    return pl.pallas_call(
        functools.partial(pack_kernel, s, n),
        out_shape=jax.ShapeDtypeStruct((s.B, rows, LANES), BF16),
        in_specs=[hbm()] * (n + 2),
        out_specs=hbm(),
        scratch_shapes=[
            pltpu.VMEM((s.B, rows, LANES), BF16),
            pltpu.VMEM((n, s.T, s.C), BF16),
            pltpu.VMEM((s.B, s.cols), jnp.int32),
            pltpu.VMEM((s.B, s.cols), jnp.int32),
            pltpu.VMEM((TAIL, LANES), F32),
            pltpu.SemaphoreType.DMA((n + 2,)),
            pltpu.SemaphoreType.DMA((n + 1,)),
        ],
        compiler_params=params(),
        cost_estimate=cost(n * s.T * s.C * 4, n * s.T * s.C * 4),
        name="pack_channels",
    )(*arrays, owner, slot)


def skip_kernel(s, skip, out):
    me = lax.axis_index("bins")
    row = skip[pl.ds(me // s.G, 1), :]
    lane = lane_group(s, 1)
    for q in range(s.G):
        v = lane_transpose(s, [jnp.where(lane == q, row, 0.0)] * s.G, lane)[q]

        @pl.when(me % s.G == q)
        def _():
            out[...] = v


def own_skip(s, skip):
    return pl.pallas_call(
        functools.partial(skip_kernel, s),
        out_shape=jax.ShapeDtypeStruct((1, LANES), F32),
        in_specs=[vmem()],
        out_specs=vmem(),
        compiler_params=params(),
        cost_estimate=cost(LANES, s.C * 4),
        name="own_skip",
    )(skip.reshape(s.tiles, LANES))


def swap_partners(s, parts, after):
    out = [None] * s.B
    out[0] = parts[0]
    for x in [*range(s.B // 2, s.B), *range(s.B // 2 - 1, 0, -1)]:
        part = parts[x]
        if x in after:
            part, out[after[x]] = lax.optimization_barrier((part, out[after[x]]))
        out[x] = lax.ppermute(part, "bins", [(b, b ^ x) for b in range(s.B)])
    return out


def load_parts(s, hops, pieces, weight, piece_held, weight_held, sems):
    chan = lax.axis_index("chan")
    feats = pieces[0].shape[1]
    copies = []
    for a, hop in enumerate(hops):
        at = pl.ds(pl.multiple_of((chan ^ hop) * feats, feats), feats)
        copies.append(
            (
                pltpu.make_async_copy(pieces[a], piece_held.at[a], sems.at[2 * a]),
                pltpu.make_async_copy(weight.at[:, at], weight_held.at[a], sems.at[2 * a + 1]),
            )
        )
    return copies


def multiply(piece, weight):
    return lax.dot_general(
        piece[...], weight[...], (((1,), (1,)), ((), ())), preferred_element_type=F32
    )


def project_part_kernel(s, hops, *refs):
    n = len(hops)
    pieces, weight, refs = refs[:n], refs[n], refs[n + 1 :]
    out_at, out, piece_held, weight_held, sems = refs[-5:]
    start = refs[:-5]
    copies = load_parts(s, hops, pieces, weight, piece_held, weight_held, sems)
    for pair in copies:
        for c in pair:
            c.start()
    if start:
        first = pltpu.make_async_copy(start[0], out, sems.at[2 * n])
        first.start()
    for a, pair in enumerate(copies):
        for c in pair:
            c.wait()
        v = multiply(piece_held.at[a], weight_held.at[a])
        if start and a == 0:
            first.wait()
        out[...] = out[...] + v if start or a else v
    store = pltpu.make_async_copy(out, out_at, sems.at[2 * n + 1])
    store.start()
    store.wait()


def project_scratch(s, n, feats):
    return [
        pltpu.VMEM((s.T, s.C), F32),
        pltpu.VMEM((n, s.T, feats), BF16),
        pltpu.VMEM((n, s.C, feats), BF16),
        pltpu.SemaphoreType.DMA((2 * n + 2,)),
    ]


def project_cost(s, n, feats):
    return cost(s.T * s.C * n, s.T * s.C)


def project_part(s, pieces, hops, weight, start=()):
    n, feats = len(pieces), pieces[0].shape[1]
    return pl.pallas_call(
        functools.partial(project_part_kernel, s, hops),
        out_shape=jax.ShapeDtypeStruct((s.T, s.C), F32),
        in_specs=[hbm()] * (n + 1 + len(start)),
        out_specs=hbm(),
        scratch_shapes=project_scratch(s, n, feats),
        compiler_params=params(40),
        cost_estimate=project_cost(s, n, feats),
        name="project_part",
    )(*pieces, weight, *start)


def project_finish_kernel(s, hops, *refs):
    pieces, weight, start, gate_at, refs = refs[:1], refs[1], refs[2], refs[3], refs[4:]
    dy_at, (away_at, kept_at, acc, piece_held, weight_held, sems) = refs[: s.B], refs[s.B : s.B + 6]
    gate, dy, g, out_sems = refs[s.B + 6 :]
    me = lax.axis_index("bins")
    ((piece_copy, weight_copy),) = load_parts(
        s, hops, pieces, weight, piece_held, weight_held, sems
    )
    first = pltpu.make_async_copy(start, acc, sems.at[2])
    gate_copy = pltpu.make_async_copy(gate_at, gate, sems.at[3])
    loads = (weight_copy, piece_copy, first, gate_copy)
    for c in loads:
        c.start()
    for c in loads:
        c.wait()
    stores = []

    def store(src, dst):
        stores.append(pltpu.make_async_copy(src, dst, out_sems.at[len(stores)]))
        stores[-1].start()

    v = acc[...] + multiply(piece_held.at[0], weight_held.at[0])
    g[...] = v.astype(BF16)
    group = lane_group(s, s.R)
    for m in range(s.tiles):
        lanes = slice(m * LANES, (m + 1) * LANES)
        parts = []
        for p in range(s.G):
            at = (slice(p * s.R, (p + 1) * s.R), lanes)
            parts.append((g[at].astype(F32) * gate[at].astype(F32)).astype(BF16).astype(F32))
        for q, v in enumerate(lane_transpose(s, parts, group)):
            dy[s.G * m + q] = v.astype(BF16)
    for x in range(s.B):
        store(dy.at[me ^ x], dy_at[x])
    half = s.T // 2
    mine = me // (s.B // 2)
    store(g.at[pl.ds(pl.multiple_of(mine * half, half), half), :], kept_at)
    store(g.at[pl.ds(pl.multiple_of((1 - mine) * half, half), half), :], away_at)
    for c in stores:
        c.wait()


def project_finish(s, piece, hop, weight, start, gate):
    feats = piece.shape[1]
    half = jax.ShapeDtypeStruct((s.T // 2, s.C), BF16)
    return pl.pallas_call(
        functools.partial(project_finish_kernel, s, (hop,)),
        out_shape=[pltpu.HBM((s.R, LANES), BF16)] * s.B + [pltpu.HBM(half.shape, BF16)] * 2,
        in_specs=[hbm()] * 4,
        out_specs=[hbm()] * (s.B + 2),
        scratch_shapes=project_scratch(s, 1, feats)
        + [
            pltpu.VMEM((s.T, s.C), BF16),
            pltpu.VMEM((s.B, s.R, LANES), BF16),
            pltpu.VMEM((s.T, s.C), BF16),
            pltpu.SemaphoreType.DMA((s.B + 2,)),
        ],
        compiler_params=params(40),
        cost_estimate=project_cost(s, 1, feats),
        name="project_finish",
    )(piece, weight, start, gate)


def swap_halves(s, away):
    return lax.ppermute(away, "bins", [(b, b ^ (s.B // 2)) for b in range(s.B)])


def column_blocks(s, out, rows, c, values):
    group = lane_group(s, CHUNK)
    per = s.cols // CHUNK
    q = c // per
    inner = pl.ds(pl.multiple_of(c % per * CHUNK, CHUNK), CHUNK)
    for i2 in range(s.Q):
        parts = [values[s.G * i2 + a] for a in range(s.G)]
        for p, v in enumerate(lane_transpose(s, parts, group)):
            out[p * s.Q + q, i2, inner, :] = v.astype(BF16)


def tw_copies(s, tw_at, tw, sems, first):
    part = s.R // TW_PIECES
    out = []
    for n in range(TW_PIECES):
        rows = slice(n * part, (n + 1) * part)
        src, dst = tw_at.at[:, :, rows, :], tw.at[:, :, rows, :]
        out.append(pltpu.make_async_copy(src, dst, sems.at[first + n]))
    return out


def spectrum_kernel(s, xh_at, dft_at, tw_at, pre, *refs):
    h_at, x_at, codes_at, h, x, codes, dft, tw, h_spec, held, sems, out_sems = refs
    h_copy = pltpu.make_async_copy(xh_at.at[:, s.R : 2 * s.R, :], h, sems.at[0])
    dft_copy = pltpu.make_async_copy(dft_at, dft, sems.at[1])
    tables_in = tw_copies(s, tw_at, tw, sems, 2)
    base = 2 + TW_PIECES
    through = [
        pltpu.make_async_copy(xh_at.at[:, : s.R, :], x, sems.at[base]),
        pltpu.make_async_copy(xh_at.at[:, 2 * s.R :, :], codes, sems.at[base + 1]),
    ]
    stores = [
        pltpu.make_async_copy(x, x_at, out_sems.at[s.K]),
        pltpu.make_async_copy(codes, codes_at, out_sems.at[s.K + 1]),
    ]
    for c in [h_copy] + tables_in + [dft_copy] + through:
        c.start()
    h_copy.wait()
    forward_rows(s, lambda i, rows: h[i, rows, :].astype(F32), held, tw, pre, tables_in)
    dft_copy.wait()
    for came, kept in zip(through, stores):
        came.wait()
        kept.start()

    def bins(k):
        re, im = forward_bins(s, held[k], dft)
        h_spec[k, 0] = re
        h_spec[k, 1] = im
        stores.append(pltpu.make_async_copy(h_spec.at[k], h_at.at[k], out_sems.at[k]))
        stores[-1].start()

    each_bin(s, bins)
    for c in stores:
        c.wait()


def row_choice(s, codes, q):
    per = LANES // s.cols
    target = lax.broadcasted_iota(jnp.int32, (s.B * s.send, LANES), 0).astype(F32)
    lane = lax.broadcasted_iota(jnp.int32, (1, LANES), 1) // s.cols
    hits = []
    for p in range(s.G):
        v = codes[p * s.Q + q].astype(F32)
        v = v * float(s.send) + turn(v, -s.cols)
        for t in range(s.B // per):
            row = v[t * per : t * per + 1, :]
            for a in range(1, per):
                other = turn(v[t * per + a : t * per + a + 1, :], a * s.cols)
                row = jnp.where(lane == a, other, row)
            hits.append(jnp.where(target == row, 1.0, 0.0).astype(BF16))
    return jnp.concatenate(hits, axis=1)


def arrival_order(s):
    return [*range(s.B // 2, s.B), 0, *range(2, s.B // 2), 1]


def token_kernel(s, *refs):
    parts, refs = refs[: s.B], refs[s.B :]
    codes_at, h_at, skip_at, dft_at, tw_at, pre_at, y_at, out_at = refs[:8]
    dy, codes, h_spec, skip, dft, tw, pre, y_spec, out, held, back, tok, sems, y_sems = refs[8:]
    me = lax.axis_index("bins")
    pairs = [(codes_at, codes), (pre_at, pre), (skip_at, skip)]
    pairs += [(parts[n], dy.at[me ^ x]) for n, x in enumerate(arrival_order(s))]
    pairs += [(dft_at, dft), (h_at, h_spec)]
    copies = [pltpu.make_async_copy(a, b, sems.at[n]) for n, (a, b) in enumerate(pairs)]
    copies[-2:-2] = tw_copies(s, tw_at, tw, sems, len(pairs))
    for c in copies:
        c.start()
    copies[0].wait()
    first = s.B + 3
    for c in copies[1:first]:
        c.wait()
    forward_rows(s, lambda i, rows: dy[i, rows, :].astype(F32), held, tw, pre, copies[first:-2])
    copies[-2].wait()
    copies[-1].wait()
    stores = []

    def bins(k):
        yre, yim = forward_bins(s, held[k], dft)
        y_spec[k, 0] = yre
        y_spec[k, 1] = yim
        stores.append(pltpu.make_async_copy(y_spec.at[k], y_at.at[k], y_sems.at[k]))
        stores[-1].start()
        hre, him = h_spec[k, 0], h_spec[k, 1]
        inverse_bins(s, hre * yre + him * yim, hre * yim - him * yre, k, dft, tw, pre, back)

    each_bin(s, bins)

    def last(rows, c):
        back_rows = inverse_rows(s, back, rows)
        for i in range(s.B):
            v = back_rows[i] * (1.0 / s.N) + skip[...] * dy[i, rows, :].astype(F32)
            tok[i, rows, :] = v.astype(BF16)

    each_chunk(s, last)

    group = lane_group(s, s.B * s.cols)
    for q in range(s.Q):
        rows = slice(q * s.cols, (q + 1) * s.cols)
        v = jnp.concatenate([tok[i, rows, :] for i in range(s.B)], axis=0)
        zero = jnp.zeros_like(v)
        v = jnp.concatenate([jnp.where(group == p, v, zero) for p in range(s.G)], axis=0)
        o = jnp.dot(row_choice(s, codes, q), v, preferred_element_type=F32)
        at = slice(q * s.send, (q + 1) * s.send)
        for b in range(s.B):
            out[b, at, :] = o[b * s.send : (b + 1) * s.send].astype(BF16)
        sem = y_sems.at[s.K + q]
        stores.append(pltpu.make_async_copy(out.at[:, at, :], out_at.at[:, at, :], sem))
        stores[-1].start()
    for c in stores:
        c.wait()


def products_kernel(s, x_at, h_at, y_at, kept, g_came, skip, dft_at, tw_at, pre, *refs):
    outs, refs = refs[: s.B], refs[s.B :]
    x, h_spec, y_spec, dft, tw, x_spec, held, back, u, lags, sems = refs
    x_copy = pltpu.make_async_copy(x_at, x, sems.at[0])
    dft_copy = pltpu.make_async_copy(dft_at, dft, sems.at[1])
    h_copy = pltpu.make_async_copy(h_at, h_spec, sems.at[2])
    y_copy = pltpu.make_async_copy(y_at, y_spec, sems.at[3])
    tables_in = tw_copies(s, tw_at, tw, sems, 4)
    for c in [x_copy] + tables_in + [dft_copy, h_copy, y_copy]:
        c.start()
    x_copy.wait()
    forward_rows(s, lambda i, rows: x[i, rows, :].astype(F32), held, tw, pre, tables_in)
    dft_copy.wait()
    h_copy.wait()

    def x_bins(k):
        xre, xim = forward_bins(s, held[k], dft)
        x_spec[k, 0] = xre
        x_spec[k, 1] = xim
        hre, him = h_spec[k, 0], h_spec[k, 1]
        inverse_bins(s, xre * hre - xim * him, xre * him + xim * hre, k, dft, tw, pre, back)

    each_bin(s, x_bins)

    def conv_rows(rows, c):
        conv = inverse_rows(s, back, rows)
        values = [
            conv[i] * (1.0 / s.N) + skip[...] * x[i, rows, :].astype(F32) for i in range(s.B)
        ]
        column_blocks(s, u, rows, c, values)

    each_chunk(s, conv_rows)
    y_copy.wait()

    def lag_bins(k):
        xre, xim = x_spec[k, 0], x_spec[k, 1]
        yre, yim = y_spec[k, 0], y_spec[k, 1]
        inverse_bins(s, yre * xre + yim * xim, yim * xre - yre * xim, k, dft, tw, pre, back)

    each_bin(s, lag_bins)
    scale = 1.0 / (s.N * math.sqrt(s.B * s.T))

    def lag_rows(rows, c):
        column_blocks(s, lags, rows, c, [v * scale for v in inverse_rows(s, back, rows)])

    each_chunk(s, lag_rows)
    me = lax.axis_index("bins")
    for d in range(s.B):
        outs[d][0] = u[me ^ d]
        outs[d][1] = lags[me ^ d]
        if d < s.B // 2:
            at = (me ^ d) % (s.B // 2) * s.cols
            rows = pl.ds(pl.multiple_of(at, s.cols), s.cols)
            for m in range(s.tiles):
                lanes = slice(m * LANES, (m + 1) * LANES)
                outs[d][2, m] = kept[rows, lanes]
                outs[d][3, m] = g_came[rows, lanes]


def rows_kernel(s, inbox_at, rows_at, inbox, rows, in_sems, sems):
    copies = []
    for m in range(s.tiles):
        at = slice(m * s.G, (m + 1) * s.G)
        copies.append(pltpu.make_async_copy(inbox_at.at[at], inbox.at[at], in_sems.at[m]))
        copies[-1].start()
    stores = []
    group = lane_group(s, s.send)
    for m in range(s.tiles):
        copies[m].wait()
        lanes = slice(m * LANES, (m + 1) * LANES)
        for q in range(s.Q):
            vs = [
                inbox[s.G * m + a, q * s.send : (q + 1) * s.send, :].astype(F32)
                for a in range(s.G)
            ]
            for p, v in enumerate(lane_transpose(s, vs, group)):
                at = (p * s.Q + q) * s.send
                rows[at : at + s.send, lanes] = v.astype(BF16)
        src, dst = rows.at[:, lanes], rows_at.at[:, lanes]
        stores.append(pltpu.make_async_copy(src, dst, sems.at[m]))
        stores[-1].start()
    for c in stores:
        c.wait()


def owner_rows(s, inbox):
    rows_shape = (s.B * s.send, s.C)
    return pl.pallas_call(
        functools.partial(rows_kernel, s),
        out_shape=jax.ShapeDtypeStruct(rows_shape, BF16),
        in_specs=[hbm()],
        out_specs=hbm(),
        scratch_shapes=[
            pltpu.VMEM(inbox.shape, BF16),
            pltpu.VMEM(rows_shape, BF16),
            pltpu.SemaphoreType.DMA((s.tiles,)),
            pltpu.SemaphoreType.DMA((s.tiles,)),
        ],
        compiler_params=params(40),
        cost_estimate=cost(s.T * s.C * 4, s.T * s.C * 8),
        name="owner_rows",
    )(inbox)


def columns_kernel(s, *refs):
    parts, refs = refs[: s.B], refs[s.B :]
    half = s.B // 2
    gate_at, filter_at, src, g, gate_grad, filter_grad, part_sems, g_sems, sems = refs
    me = lax.axis_index("bins")
    copies = []
    for x in range(s.B):
        block = src.at[me ^ x]
        copies.append(pltpu.make_async_copy(parts[x].at[:2], block, part_sems.at[x]))
    for x in range(half):
        for far in range(2):
            block = g.at[me ^ x ^ (far * half)]
            sem = g_sems.at[2 * x + far]
            copies.append(pltpu.make_async_copy(parts[x].at[2 + far], block, sem))
    for c in copies:
        c.start()
    for c in copies[s.B :]:
        c.wait()
    stores = []
    group = lane_group(s, s.cols)
    for n in range(s.tiles):
        for c in copies[s.G * n : s.G * (n + 1)]:
            c.wait()
        m = me // s.G ^ n
        lanes = pl.ds(pl.multiple_of(m * LANES, LANES), LANES)
        for kind, (out, out_at) in enumerate(((gate_grad, gate_at), (filter_grad, filter_at))):
            for i2 in range(s.Q):
                vs = [src[s.G * m + a, kind, i2].astype(F32) for a in range(s.G)]
                for a, v in enumerate(lane_transpose(s, vs, group)):
                    i = s.G * i2 + a
                    if kind == 0:
                        v = (v * g[i, m].astype(F32)).astype(BF16)
                    out[i, :, lanes] = v
            sem = sems.at[len(stores)]
            at = (slice(None), slice(None), lanes)
            stores.append(pltpu.make_async_copy(out.at[at], out_at.at[at], sem))
            stores[-1].start()
    for c in stores:
        c.wait()


def columns(s, parts):
    cols_shape = (s.B, s.cols, s.C)
    return pl.pallas_call(
        functools.partial(columns_kernel, s),
        out_shape=[
            jax.ShapeDtypeStruct(cols_shape, BF16),
            jax.ShapeDtypeStruct(cols_shape, F32),
        ],
        in_specs=[hbm()] * s.B,
        out_specs=[hbm()] * 2,
        scratch_shapes=[
            pltpu.VMEM((s.B,) + parts[-1].shape, BF16),
            pltpu.VMEM((s.B, s.tiles, s.cols, LANES), BF16),
            pltpu.VMEM(cols_shape, BF16),
            pltpu.VMEM(cols_shape, F32),
            pltpu.SemaphoreType.DMA((s.B,)),
            pltpu.SemaphoreType.DMA((s.B,)),
            pltpu.SemaphoreType.DMA((2 * s.tiles,)),
        ],
        compiler_params=params(56),
        cost_estimate=cost(s.T * s.C * 8, s.T * s.C * 12),
        name="columns",
    )(*parts)


def exchange(v):
    return lax.all_to_all(v, "bins", split_axis=0, concat_axis=0, tiled=True)


def shards(tokens_in, filters, gate, skip, out_grad, out_weight, owner, slot):
    s = Plan(lax.axis_size("bins"), *tokens_in.shape)
    me = lax.axis_index("bins")
    nchan = lax.axis_size("chan")
    dft, tw, pre = tables(s)
    spec_shape = jax.ShapeDtypeStruct((s.K, 2, s.R, LANES), F32)
    spec_bytes = s.K * 2 * s.R * LANES * 4
    transform = 2 * 2 * s.R * s.R * 2 * LANES * s.K
    held = pltpu.VMEM((s.K, s.R, 2 * LANES), BF16)
    back = pltpu.VMEM((s.K, 2, s.R, LANES), F32)

    packed = pack(s, owner, slot, tokens_in, filters)
    came = exchange(packed)

    core_pairs = [(c, c ^ 1) for c in range(nchan)]
    hops = list(range(2, nchan, 2))
    far = [lax.ppermute(out_grad, "chan", [(c, c ^ h) for c in range(nchan)]) for h in hops]
    near = lax.ppermute(out_grad, "chan", core_pairs)
    start = project_part(s, [out_grad], (0,), out_weight)
    my_skip = own_skip(s, skip)
    *far, start, my_skip = lax.optimization_barrier((*far, start, my_skip))
    far_near = [lax.ppermute(v, "chan", core_pairs) for v in far]
    start = project_part(s, [near, *far], (1, *hops), out_weight, (start,))
    for v, h in zip(far_near[:-1], hops[:-1]):
        start = project_part(s, [v], (h ^ 1,), out_weight, (start,))
    *dy, away, kept = project_finish(s, far_near[-1], hops[-1] ^ 1, out_weight, start, gate)
    dy = swap_partners(s, dy, {1: 2})

    block = pltpu.VMEM((s.B, s.R, LANES), BF16)
    dft_held = pltpu.VMEM((2 * s.R, s.R), BF16)
    h_spec, x, codes = pl.pallas_call(
        functools.partial(spectrum_kernel, s),
        out_shape=[
            pltpu.HBM(spec_shape.shape, F32),
            pltpu.HBM((s.B, s.R, LANES), BF16),
            pltpu.HBM((s.B, TAIL, LANES), BF16),
        ],
        in_specs=[hbm(), hbm(), hbm(), vmem()],
        out_specs=[hbm()] * 3,
        scratch_shapes=[
            block,
            block,
            pltpu.VMEM((s.B, TAIL, LANES), BF16),
            dft_held,
            back,
            back,
            held,
            pltpu.SemaphoreType.DMA((4 + TW_PIECES,)),
            pltpu.SemaphoreType.DMA((s.K + 2,)),
        ],
        compiler_params=params(58),
        cost_estimate=cost(10 * transform, 2 * spec_bytes),
        name="filter_spectrum",
    )(came, dft, tw, pre)

    away, dy[s.B - 1] = lax.optimization_barrier((away, dy[s.B - 1]))
    g_came = swap_halves(s, away)

    outbox_shape = (s.B, s.Q * s.send, LANES)
    y_spec, outbox = pl.pallas_call(
        functools.partial(token_kernel, s),
        out_shape=[pltpu.HBM(spec_shape.shape, F32), pltpu.HBM(outbox_shape, BF16)],
        in_specs=[hbm()] * (s.B + 6),
        out_specs=[hbm()] * 2,
        scratch_shapes=[
            block,
            pltpu.VMEM((s.B, TAIL, LANES), BF16),
            back,
            pltpu.VMEM((1, LANES), F32),
            dft_held,
            back,
            pltpu.VMEM((s.K, 2, LANES), F32),
            back,
            pltpu.VMEM(outbox_shape, BF16),
            held,
            back,
            block,
            pltpu.SemaphoreType.DMA((s.B + 5 + TW_PIECES,)),
            pltpu.SemaphoreType.DMA((s.K + s.Q,)),
        ],
        compiler_params=params(60),
        cost_estimate=cost(20 * transform, 3 * spec_bytes),
        name="token_products",
    )(*[dy[x] for x in arrival_order(s)], codes, h_spec, my_skip, dft, tw, pre)
    outbox, g_came = lax.optimization_barrier((outbox, g_came))
    inbox = exchange(outbox)

    cols_shape = (s.Q, s.cols, LANES)
    by_dest = pltpu.VMEM((s.B,) + cols_shape, BF16)
    parts = pl.pallas_call(
        functools.partial(products_kernel, s),
        out_shape=[
            jax.ShapeDtypeStruct((4 if x < s.B // 2 else 2,) + cols_shape, BF16)
            for x in range(s.B)
        ],
        in_specs=[hbm()] * 3 + [vmem()] * 3 + [hbm()] * 2 + [vmem()],
        out_specs=[vmem()] * s.B,
        scratch_shapes=[
            block,
            back,
            back,
            dft_held,
            back,
            back,
            held,
            back,
            by_dest,
            by_dest,
            pltpu.SemaphoreType.DMA((4 + TW_PIECES,)),
        ],
        compiler_params=params(),
        cost_estimate=cost(3 * transform, 4 * spec_bytes),
        name="conv_and_filter",
    )(x, h_spec, y_spec, kept, g_came, my_skip, dft, tw, pre)
    grad_rows = owner_rows(s, inbox)
    *parts, last = parts
    last, grad_rows = lax.optimization_barrier((last, grad_rows))
    parts = swap_partners(s, [*parts, last], {1: 2})
    gate_grad, filter_grad = columns(s, parts)
    return (gate_grad, filter_grad, grad_rows)


def solution(mesh):
    return jax.shard_map(
        shards,
        mesh=mesh,
        in_specs=(
            P("bins", "chan"),
            P("bins", "chan"),
            P("bins", "chan"),
            P("chan"),
            P("bins", "chan"),
            P("chan", None),
            P(None, "bins"),
            P(None, "bins"),
        ),
        out_specs=(P(None, "bins", "chan"), P(None, "bins", "chan"), P("bins", "chan")),
        check_vma=False,
    )
```

```python
import functools
import math

import jax
import jax.numpy as jnp
import numpy as np
from jax import lax
from jax.experimental import pallas as pl
from jax.experimental.pallas import tpu as pltpu
from jax.sharding import PartitionSpec as P

LANES = 128
F32 = jnp.float32
BF16 = jnp.bfloat16
MIB = 1 << 20


class Plan:
    def __init__(self, blocks, tok, chans):
        self.B = blocks
        self.T = tok
        self.C = chans
        self.cb = chans // blocks
        self.G = LANES // self.cb
        self.R = tok // self.G
        self.tiles = chans // LANES
        self.cols = tok // blocks
        self.send = 2 * self.cols
        self.Q = blocks // self.G
        self.N = 2 * blocks * tok
        self.K = blocks + 1


def wave(num, den):
    ang = 2.0 * np.pi * (np.asarray(num) % den) / den
    return np.cos(ang), -np.sin(ang)


def tables(s):
    rows = np.arange(s.R)
    lane_e = np.arange(LANES) // s.cb
    dft_c, dft_s = wave(rows[:, None] * rows[None, :], s.R)
    stacked = np.concatenate([dft_c, -dft_s], axis=0)
    k1 = np.arange(s.K)
    tw = wave(rows[None, :, None] * (k1[:, None, None] + 2 * s.B * lane_e[None, None, :]), s.N)
    tw = np.stack(tw, axis=1)
    pre = np.stack(wave(k1[:, None] * lane_e[None, :], 2 * s.B * s.G), axis=1)
    return (
        jnp.asarray(stacked, BF16),
        jnp.asarray(tw, F32),
        jnp.asarray(pre, F32),
    )


def lane_group(s, rows):
    return lax.broadcasted_iota(jnp.int32, (rows, LANES), 1) // s.cb


def turn(v, shift):
    shift = shift % LANES
    return v if shift == 0 else pltpu.roll(v, shift, 1)


def lane_transpose(s, parts, group):
    out = []
    for a in range(s.G):
        acc = None
        for g in range(s.G):
            moved = turn(parts[g], (g - a) * s.cb)
            acc = moved if acc is None else jnp.where(group == g, moved, acc)
        out.append(acc)
    return out


def lane_dft(s, re, im, group, sign):
    if s.G == 1:
        return re, im
    if s.G == 2:
        flip = jnp.where(group == 0, 1.0, -1.0).astype(F32)
        return turn(re, s.cb) + flip * re, turn(im, s.cb) + flip * im
    out_re = out_im = None
    for d in range(s.G):
        mre, mim = turn(re, d * s.cb), turn(im, d * s.cb)
        source = (group - d + s.G) % s.G
        angle_index = (group * source) % s.G
        cos_t = jnp.zeros_like(re)
        sin_t = jnp.zeros_like(re)
        for a in range(s.G):
            c, w = wave(a, s.G)
            cos_t = jnp.where(angle_index == a, float(c), cos_t)
            sin_t = jnp.where(angle_index == a, float(w) * sign, sin_t)
        add_re = mre * cos_t - mim * sin_t
        add_im = mre * sin_t + mim * cos_t
        out_re = add_re if out_re is None else out_re + add_re
        out_im = add_im if out_im is None else out_im + add_im
    return out_re, out_im


def weighted(values, weights):
    acc = None
    for v, w in zip(values, weights):
        w = float(w)
        if abs(w) < 1e-12:
            continue
        term = v if abs(w - 1) < 1e-12 else (-v if abs(w + 1) < 1e-12 else v * w)
        acc = term if acc is None else acc + term
    return acc


def add(a, b):
    return b if a is None else (a if b is None else a + b)


def sub(a, b):
    return a if b is None else (-b if a is None else a - b)


def block_dft(s, xs):
    even, odd = range(0, s.B, 2), range(1, s.B, 2)
    out = [None] * s.K
    for k in range(s.B // 2 + 1):
        ce, se = wave(np.array(even) * k, 2 * s.B)
        co, so = wave(np.array(odd) * k, 2 * s.B)
        xe, xo = [xs[i] for i in even], [xs[i] for i in odd]
        ere, eim = weighted(xe, ce), weighted(xe, se)
        ore, oim = weighted(xo, co), weighted(xo, so)
        out[k] = (add(ere, ore), add(eim, oim))
        if k != s.B - k:
            out[s.B - k] = (sub(ere, ore), sub(oim, eim))
    return out


def block_back(s, ts):
    half = s.B // 2
    sums = {}
    for k in range(half + 1):
        tre, tim = ts[k]
        if k == half:
            sums[k] = (tre, tre, tim, tim)
        else:
            ure, uim = ts[s.B - k]
            sums[k] = (tre + ure, tre - ure, tim - uim, tim + uim)
    out = []
    for i in range(s.B):
        acc = None
        for k in range(half + 1):
            c, w = wave(i * k, 2 * s.B)
            gain = 1.0 if k == 0 else 2.0
            re = sums[k][i % 2]
            im = sums[k][2 + i % 2]
            acc = add(acc, weighted([re, im], [gain * float(c), gain * float(w)]))
        out.append(acc)
    return out


CHUNK = 16
TAIL = 16
TW_PIECES = 2


def forward_rows(s, load, held, tw, pre, ready=()):
    def body(c, _):
        rows = pl.ds(pl.multiple_of(c * CHUNK, CHUNK), CHUNK)
        group = lane_group(s, CHUNK)
        spec = block_dft(s, [load(i, rows) for i in range(s.B)])
        for k in range(s.K):
            re, im = spec[k]
            pr, pi = pre[k, 0:1, :], pre[k, 1:2, :]
            if k == 0:
                im = jnp.zeros_like(re)
            elif im is None:
                re, im = re * pr, re * pi
            else:
                re, im = re * pr - im * pi, re * pi + im * pr
            re, im = lane_dft(s, re, im, group, 1.0)
            tr, ti = tw[k, 0, rows, :], tw[k, 1, rows, :]
            held[k, rows, 0:LANES] = (re * tr - im * ti).astype(BF16)
            held[k, rows, LANES : 2 * LANES] = (re * ti + im * tr).astype(BF16)
        return 0

    pieces = max(len(ready), 1)
    per = s.R // CHUNK // pieces
    for n in range(pieces):
        if ready:
            ready[n].wait()
        lax.fori_loop(n * per, (n + 1) * per, body, 0, unroll=min(4, per))


def forward_bins(s, held_k, dft):
    o = jnp.dot(dft[...], held_k, preferred_element_type=F32)
    re = o[: s.R, :LANES] + o[s.R :, LANES:]
    im = o[: s.R, LANES:] - o[s.R :, :LANES]
    return re, im


def inverse_bins(s, re, im, k, dft, tw, pre, back):
    z = jnp.concatenate([re.astype(BF16), im.astype(BF16)], axis=1)
    o = jnp.dot(dft[...], z, preferred_element_type=F32)
    re = o[: s.R, :LANES] - o[s.R :, LANES:]
    im = o[: s.R, LANES:] + o[s.R :, :LANES]
    tr, ti = tw[k, 0], tw[k, 1]
    re, im = re * tr + im * ti, im * tr - re * ti
    re, im = lane_dft(s, re, im, lane_group(s, s.R), -1.0)
    pr, pi = pre[k, 0:1, :], pre[k, 1:2, :]
    back[k, 0] = re * pr + im * pi
    back[k, 1] = im * pr - re * pi


def inverse_rows(s, back, rows):
    return block_back(s, [(back[k, 0, rows, :], back[k, 1, rows, :]) for k in range(s.K)])


def each_bin(s, body):
    for k in range(s.K):
        body(k)


def each_chunk(s, body):
    def step(c, _):
        body(pl.ds(pl.multiple_of(c * CHUNK, CHUNK), CHUNK), c)
        return 0

    lax.fori_loop(0, s.R // CHUNK, step, 0, unroll=4)


def params(limit=60):
    return pltpu.CompilerParams(vmem_limit_bytes=limit * MIB)


def hbm():
    return pl.BlockSpec(memory_space=pl.ANY)


def vmem():
    return pl.BlockSpec(memory_space=pltpu.VMEM)


def cost(flops, nbytes):
    return pl.CostEstimate(flops=int(flops), bytes_accessed=int(nbytes), transcendentals=0)


def pack_kernel(s, n, *refs):
    arrays, owner, slot, out_at = refs[:n], *refs[n : n + 3]
    out, held, held_owner, held_slot, tail, sems, out_sems = refs[n + 3 :]
    me = lax.axis_index("bins")
    group = lane_group(s, s.R)
    copies = [pltpu.make_async_copy(owner, held_owner, sems.at[n])]
    copies.append(pltpu.make_async_copy(slot, held_slot, sems.at[n + 1]))
    copies += [pltpu.make_async_copy(arrays[a], held.at[a], sems.at[a]) for a in range(n)]
    for c in copies:
        c.start()
    stores = []

    def store(at):
        sem = out_sems.at[len(stores)]
        stores.append(pltpu.make_async_copy(out.at[:, at, :], out_at.at[:, at, :], sem))
        stores[-1].start()

    copies[0].wait()
    copies[1].wait()
    tail[...] = jnp.zeros_like(tail)
    tail[: s.B, : s.cols] = held_owner[...].astype(F32)
    tail[: s.B, s.cols : 2 * s.cols] = (held_slot[...] - me * s.send).astype(F32)
    for b in range(s.B):
        out[b, n * s.R :, :] = tail[...].astype(BF16)
    store(slice(n * s.R, n * s.R + TAIL))
    for a in range(n):
        copies[2 + a].wait()
        for m in range(s.tiles):
            parts = [
                held[a, p * s.R : (p + 1) * s.R, m * LANES : (m + 1) * LANES].astype(F32)
                for p in range(s.G)
            ]
            for q, v in enumerate(lane_transpose(s, parts, group)):
                out[s.G * m + q, a * s.R : (a + 1) * s.R, :] = v.astype(BF16)
        store(slice(a * s.R, (a + 1) * s.R))
    for c in stores:
        c.wait()


def pack(s, owner, slot, *arrays):
    n = len(arrays)
    rows = n * s.R + TAIL
    return pl.pallas_call(
        functools.partial(pack_kernel, s, n),
        out_shape=jax.ShapeDtypeStruct((s.B, rows, LANES), BF16),
        in_specs=[hbm()] * (n + 2),
        out_specs=hbm(),
        scratch_shapes=[
            pltpu.VMEM((s.B, rows, LANES), BF16),
            pltpu.VMEM((n, s.T, s.C), BF16),
            pltpu.VMEM((s.B, s.cols), jnp.int32),
            pltpu.VMEM((s.B, s.cols), jnp.int32),
            pltpu.VMEM((TAIL, LANES), F32),
            pltpu.SemaphoreType.DMA((n + 2,)),
            pltpu.SemaphoreType.DMA((n + 1,)),
        ],
        compiler_params=params(),
        cost_estimate=cost(n * s.T * s.C * 4, n * s.T * s.C * 4),
        name="pack_channels",
    )(*arrays, owner, slot)


def skip_kernel(s, skip, out):
    me = lax.axis_index("bins")
    row = skip[pl.ds(me // s.G, 1), :]
    lane = lane_group(s, 1)
    for q in range(s.G):
        v = lane_transpose(s, [jnp.where(lane == q, row, 0.0)] * s.G, lane)[q]

        @pl.when(me % s.G == q)
        def _():
            out[...] = v


def own_skip(s, skip):
    return pl.pallas_call(
        functools.partial(skip_kernel, s),
        out_shape=jax.ShapeDtypeStruct((1, LANES), F32),
        in_specs=[vmem()],
        out_specs=vmem(),
        compiler_params=params(),
        cost_estimate=cost(LANES, s.C * 4),
        name="own_skip",
    )(skip.reshape(s.tiles, LANES))


def swap_partners(s, parts, after):
    out = [None] * s.B
    out[0] = parts[0]
    for x in [*range(s.B // 2, s.B), *range(s.B // 2 - 1, 0, -1)]:
        part = parts[x]
        if x in after:
            part, out[after[x]] = lax.optimization_barrier((part, out[after[x]]))
        out[x] = lax.ppermute(part, "bins", [(b, b ^ x) for b in range(s.B)])
    return out


def load_parts(s, hops, pieces, weight, piece_held, weight_held, sems):
    chan = lax.axis_index("chan")
    feats = pieces[0].shape[1]
    copies = []
    for a, hop in enumerate(hops):
        at = pl.ds(pl.multiple_of((chan ^ hop) * feats, feats), feats)
        copies.append(
            (
                pltpu.make_async_copy(pieces[a], piece_held.at[a], sems.at[2 * a]),
                pltpu.make_async_copy(weight.at[:, at], weight_held.at[a], sems.at[2 * a + 1]),
            )
        )
    return copies


def multiply(piece, weight):
    return lax.dot_general(
        piece[...], weight[...], (((1,), (1,)), ((), ())), preferred_element_type=F32
    )


def project_part_kernel(s, hops, *refs):
    n = len(hops)
    pieces, weight, refs = refs[:n], refs[n], refs[n + 1 :]
    out_at, out, piece_held, weight_held, sems = refs[-5:]
    start = refs[:-5]
    copies = load_parts(s, hops, pieces, weight, piece_held, weight_held, sems)
    for pair in copies:
        for c in pair:
            c.start()
    if start:
        first = pltpu.make_async_copy(start[0], out, sems.at[2 * n])
        first.start()
    for a, pair in enumerate(copies):
        for c in pair:
            c.wait()
        v = multiply(piece_held.at[a], weight_held.at[a])
        if start and a == 0:
            first.wait()
        out[...] = out[...] + v if start or a else v
    store = pltpu.make_async_copy(out, out_at, sems.at[2 * n + 1])
    store.start()
    store.wait()


def project_scratch(s, n, feats):
    return [
        pltpu.VMEM((s.T, s.C), F32),
        pltpu.VMEM((n, s.T, feats), BF16),
        pltpu.VMEM((n, s.C, feats), BF16),
        pltpu.SemaphoreType.DMA((2 * n + 2,)),
    ]


def project_cost(s, n, feats):
    return cost(s.T * s.C * n, s.T * s.C)


def project_part(s, pieces, hops, weight, start=()):
    n, feats = len(pieces), pieces[0].shape[1]
    return pl.pallas_call(
        functools.partial(project_part_kernel, s, hops),
        out_shape=jax.ShapeDtypeStruct((s.T, s.C), F32),
        in_specs=[hbm()] * (n + 1 + len(start)),
        out_specs=hbm(),
        scratch_shapes=project_scratch(s, n, feats),
        compiler_params=params(40),
        cost_estimate=project_cost(s, n, feats),
        name="project_part",
    )(*pieces, weight, *start)


def project_finish_kernel(s, hops, *refs):
    pieces, weight, start, gate_at, refs = refs[:1], refs[1], refs[2], refs[3], refs[4:]
    dy_at, (away_at, kept_at, acc, piece_held, weight_held, sems) = refs[: s.B], refs[s.B : s.B + 6]
    gate, dy, g, out_sems = refs[s.B + 6 :]
    me = lax.axis_index("bins")
    ((piece_copy, weight_copy),) = load_parts(
        s, hops, pieces, weight, piece_held, weight_held, sems
    )
    first = pltpu.make_async_copy(start, acc, sems.at[2])
    gate_copy = pltpu.make_async_copy(gate_at, gate, sems.at[3])
    loads = (weight_copy, piece_copy, first, gate_copy)
    for c in loads:
        c.start()
    for c in loads:
        c.wait()
    stores = []

    def store(src, dst):
        stores.append(pltpu.make_async_copy(src, dst, out_sems.at[len(stores)]))
        stores[-1].start()

    v = acc[...] + multiply(piece_held.at[0], weight_held.at[0])
    g[...] = v.astype(BF16)
    group = lane_group(s, s.R)
    for m in range(s.tiles):
        lanes = slice(m * LANES, (m + 1) * LANES)
        parts = []
        for p in range(s.G):
            at = (slice(p * s.R, (p + 1) * s.R), lanes)
            parts.append((g[at].astype(F32) * gate[at].astype(F32)).astype(BF16).astype(F32))
        for q, v in enumerate(lane_transpose(s, parts, group)):
            dy[s.G * m + q] = v.astype(BF16)
    for x in range(s.B):
        store(dy.at[me ^ x], dy_at[x])
    half = s.T // 2
    mine = me // (s.B // 2)
    store(g.at[pl.ds(pl.multiple_of(mine * half, half), half), :], kept_at)
    store(g.at[pl.ds(pl.multiple_of((1 - mine) * half, half), half), :], away_at)
    for c in stores:
        c.wait()


def project_finish(s, piece, hop, weight, start, gate):
    feats = piece.shape[1]
    half = jax.ShapeDtypeStruct((s.T // 2, s.C), BF16)
    return pl.pallas_call(
        functools.partial(project_finish_kernel, s, (hop,)),
        out_shape=[pltpu.HBM((s.R, LANES), BF16)] * s.B + [pltpu.HBM(half.shape, BF16)] * 2,
        in_specs=[hbm()] * 4,
        out_specs=[hbm()] * (s.B + 2),
        scratch_shapes=project_scratch(s, 1, feats)
        + [
            pltpu.VMEM((s.T, s.C), BF16),
            pltpu.VMEM((s.B, s.R, LANES), BF16),
            pltpu.VMEM((s.T, s.C), BF16),
            pltpu.SemaphoreType.DMA((s.B + 2,)),
        ],
        compiler_params=params(40),
        cost_estimate=project_cost(s, 1, feats),
        name="project_finish",
    )(piece, weight, start, gate)


def swap_halves(s, away):
    return lax.ppermute(away, "bins", [(b, b ^ (s.B // 2)) for b in range(s.B)])


def column_blocks(s, out, rows, c, values):
    group = lane_group(s, CHUNK)
    per = s.cols // CHUNK
    q = c // per
    inner = pl.ds(pl.multiple_of(c % per * CHUNK, CHUNK), CHUNK)
    for i2 in range(s.Q):
        parts = [values[s.G * i2 + a] for a in range(s.G)]
        for p, v in enumerate(lane_transpose(s, parts, group)):
            out[p * s.Q + q, i2, inner, :] = v.astype(BF16)


def tw_copies(s, tw_at, tw, sems, first):
    part = s.R // TW_PIECES
    out = []
    for n in range(TW_PIECES):
        rows = slice(n * part, (n + 1) * part)
        src, dst = tw_at.at[:, :, rows, :], tw.at[:, :, rows, :]
        out.append(pltpu.make_async_copy(src, dst, sems.at[first + n]))
    return out


def spectrum_kernel(s, xh_at, dft_at, tw_at, pre, *refs):
    h_at, x_at, codes_at, h, x, codes, dft, tw, h_spec, held, sems, out_sems = refs
    h_copy = pltpu.make_async_copy(xh_at.at[:, s.R : 2 * s.R, :], h, sems.at[0])
    dft_copy = pltpu.make_async_copy(dft_at, dft, sems.at[1])
    tables_in = tw_copies(s, tw_at, tw, sems, 2)
    base = 2 + TW_PIECES
    through = [
        pltpu.make_async_copy(xh_at.at[:, : s.R, :], x, sems.at[base]),
        pltpu.make_async_copy(xh_at.at[:, 2 * s.R :, :], codes, sems.at[base + 1]),
    ]
    stores = [
        pltpu.make_async_copy(x, x_at, out_sems.at[s.K]),
        pltpu.make_async_copy(codes, codes_at, out_sems.at[s.K + 1]),
    ]
    for c in [h_copy] + tables_in + [dft_copy] + through:
        c.start()
    h_copy.wait()
    forward_rows(s, lambda i, rows: h[i, rows, :].astype(F32), held, tw, pre, tables_in)
    dft_copy.wait()
    for came, kept in zip(through, stores):
        came.wait()
        kept.start()

    def bins(k):
        re, im = forward_bins(s, held[k], dft)
        h_spec[k, 0] = re
        h_spec[k, 1] = im
        stores.append(pltpu.make_async_copy(h_spec.at[k], h_at.at[k], out_sems.at[k]))
        stores[-1].start()

    each_bin(s, bins)
    for c in stores:
        c.wait()


def row_choice(s, codes, q):
    per = LANES // s.cols
    target = lax.broadcasted_iota(jnp.int32, (s.B * s.send, LANES), 0).astype(F32)
    lane = lax.broadcasted_iota(jnp.int32, (1, LANES), 1) // s.cols
    hits = []
    for p in range(s.G):
        v = codes[p * s.Q + q].astype(F32)
        v = v * float(s.send) + turn(v, -s.cols)
        for t in range(s.B // per):
            row = v[t * per : t * per + 1, :]
            for a in range(1, per):
                other = turn(v[t * per + a : t * per + a + 1, :], a * s.cols)
                row = jnp.where(lane == a, other, row)
            hits.append(jnp.where(target == row, 1.0, 0.0).astype(BF16))
    return jnp.concatenate(hits, axis=1)


def arrival_order(s):
    return [*range(s.B // 2, s.B), 0, *range(2, s.B // 2), 1]


def token_kernel(s, *refs):
    parts, refs = refs[: s.B], refs[s.B :]
    codes_at, h_at, skip_at, dft_at, tw_at, pre_at, y_at, out_at = refs[:8]
    dy, codes, h_spec, skip, dft, tw, pre, y_spec, out, held, back, tok, sems, y_sems = refs[8:]
    me = lax.axis_index("bins")
    pairs = [(codes_at, codes), (pre_at, pre), (skip_at, skip)]
    pairs += [(parts[n], dy.at[me ^ x]) for n, x in enumerate(arrival_order(s))]
    pairs += [(dft_at, dft), (h_at, h_spec)]
    copies = [pltpu.make_async_copy(a, b, sems.at[n]) for n, (a, b) in enumerate(pairs)]
    copies[-2:-2] = tw_copies(s, tw_at, tw, sems, len(pairs))
    for c in copies:
        c.start()
    copies[0].wait()
    first = s.B + 3
    for c in copies[1:first]:
        c.wait()
    forward_rows(s, lambda i, rows: dy[i, rows, :].astype(F32), held, tw, pre, copies[first:-2])
    copies[-2].wait()
    copies[-1].wait()
    stores = []

    def bins(k):
        yre, yim = forward_bins(s, held[k], dft)
        y_spec[k, 0] = yre
        y_spec[k, 1] = yim
        stores.append(pltpu.make_async_copy(y_spec.at[k], y_at.at[k], y_sems.at[k]))
        stores[-1].start()
        hre, him = h_spec[k, 0], h_spec[k, 1]
        inverse_bins(s, hre * yre + him * yim, hre * yim - him * yre, k, dft, tw, pre, back)

    each_bin(s, bins)

    def last(rows, c):
        back_rows = inverse_rows(s, back, rows)
        for i in range(s.B):
            v = back_rows[i] * (1.0 / s.N) + skip[...] * dy[i, rows, :].astype(F32)
            tok[i, rows, :] = v.astype(BF16)

    each_chunk(s, last)

    group = lane_group(s, s.B * s.cols)
    for q in range(s.Q):
        rows = slice(q * s.cols, (q + 1) * s.cols)
        v = jnp.concatenate([tok[i, rows, :] for i in range(s.B)], axis=0)
        zero = jnp.zeros_like(v)
        v = jnp.concatenate([jnp.where(group == p, v, zero) for p in range(s.G)], axis=0)
        o = jnp.dot(row_choice(s, codes, q), v, preferred_element_type=F32)
        at = slice(q * s.send, (q + 1) * s.send)
        for b in range(s.B):
            out[b, at, :] = o[b * s.send : (b + 1) * s.send].astype(BF16)
        sem = y_sems.at[s.K + q]
        stores.append(pltpu.make_async_copy(out.at[:, at, :], out_at.at[:, at, :], sem))
        stores[-1].start()
    for c in stores:
        c.wait()


def products_kernel(s, x_at, h_at, y_at, kept, g_came, skip, dft_at, tw_at, pre, *refs):
    outs, refs = refs[: s.B], refs[s.B :]
    x, h_spec, y_spec, dft, tw, x_spec, held, back, u, lags, sems = refs
    x_copy = pltpu.make_async_copy(x_at, x, sems.at[0])
    dft_copy = pltpu.make_async_copy(dft_at, dft, sems.at[1])
    h_copy = pltpu.make_async_copy(h_at, h_spec, sems.at[2])
    y_copy = pltpu.make_async_copy(y_at, y_spec, sems.at[3])
    tables_in = tw_copies(s, tw_at, tw, sems, 4)
    for c in [x_copy] + tables_in + [dft_copy, h_copy, y_copy]:
        c.start()
    x_copy.wait()
    forward_rows(s, lambda i, rows: x[i, rows, :].astype(F32), held, tw, pre, tables_in)
    dft_copy.wait()
    h_copy.wait()

    def x_bins(k):
        xre, xim = forward_bins(s, held[k], dft)
        x_spec[k, 0] = xre
        x_spec[k, 1] = xim
        hre, him = h_spec[k, 0], h_spec[k, 1]
        inverse_bins(s, xre * hre - xim * him, xre * him + xim * hre, k, dft, tw, pre, back)

    each_bin(s, x_bins)

    def conv_rows(rows, c):
        conv = inverse_rows(s, back, rows)
        values = [
            conv[i] * (1.0 / s.N) + skip[...] * x[i, rows, :].astype(F32) for i in range(s.B)
        ]
        column_blocks(s, u, rows, c, values)

    each_chunk(s, conv_rows)
    y_copy.wait()

    def lag_bins(k):
        xre, xim = x_spec[k, 0], x_spec[k, 1]
        yre, yim = y_spec[k, 0], y_spec[k, 1]
        inverse_bins(s, yre * xre + yim * xim, yim * xre - yre * xim, k, dft, tw, pre, back)

    each_bin(s, lag_bins)
    scale = 1.0 / (s.N * math.sqrt(s.B * s.T))

    def lag_rows(rows, c):
        column_blocks(s, lags, rows, c, [v * scale for v in inverse_rows(s, back, rows)])

    each_chunk(s, lag_rows)
    me = lax.axis_index("bins")
    for d in range(s.B):
        outs[d][0] = u[me ^ d]
        outs[d][1] = lags[me ^ d]
        if d < s.B // 2:
            at = (me ^ d) % (s.B // 2) * s.cols
            rows = pl.ds(pl.multiple_of(at, s.cols), s.cols)
            for m in range(s.tiles):
                lanes = slice(m * LANES, (m + 1) * LANES)
                outs[d][2, m] = kept[rows, lanes]
                outs[d][3, m] = g_came[rows, lanes]


def rows_kernel(s, inbox_at, rows_at, inbox, rows, in_sems, sems):
    copies = []
    for m in range(s.tiles):
        at = slice(m * s.G, (m + 1) * s.G)
        copies.append(pltpu.make_async_copy(inbox_at.at[at], inbox.at[at], in_sems.at[m]))
        copies[-1].start()
    stores = []
    group = lane_group(s, s.send)
    for m in range(s.tiles):
        copies[m].wait()
        lanes = slice(m * LANES, (m + 1) * LANES)
        for q in range(s.Q):
            vs = [
                inbox[s.G * m + a, q * s.send : (q + 1) * s.send, :].astype(F32)
                for a in range(s.G)
            ]
            for p, v in enumerate(lane_transpose(s, vs, group)):
                at = (p * s.Q + q) * s.send
                rows[at : at + s.send, lanes] = v.astype(BF16)
        src, dst = rows.at[:, lanes], rows_at.at[:, lanes]
        stores.append(pltpu.make_async_copy(src, dst, sems.at[m]))
        stores[-1].start()
    for c in stores:
        c.wait()


def owner_rows(s, inbox):
    rows_shape = (s.B * s.send, s.C)
    return pl.pallas_call(
        functools.partial(rows_kernel, s),
        out_shape=jax.ShapeDtypeStruct(rows_shape, BF16),
        in_specs=[hbm()],
        out_specs=hbm(),
        scratch_shapes=[
            pltpu.VMEM(inbox.shape, BF16),
            pltpu.VMEM(rows_shape, BF16),
            pltpu.SemaphoreType.DMA((s.tiles,)),
            pltpu.SemaphoreType.DMA((s.tiles,)),
        ],
        compiler_params=params(40),
        cost_estimate=cost(s.T * s.C * 4, s.T * s.C * 8),
        name="owner_rows",
    )(inbox)


def columns_kernel(s, *refs):
    parts, refs = refs[: s.B], refs[s.B :]
    half = s.B // 2
    gate_at, filter_at, src, g, gate_grad, filter_grad, part_sems, g_sems, sems = refs
    me = lax.axis_index("bins")
    copies = []
    for x in range(s.B):
        block = src.at[me ^ x]
        copies.append(pltpu.make_async_copy(parts[x].at[:2], block, part_sems.at[x]))
    for x in range(half):
        for far in range(2):
            block = g.at[me ^ x ^ (far * half)]
            sem = g_sems.at[2 * x + far]
            copies.append(pltpu.make_async_copy(parts[x].at[2 + far], block, sem))
    for c in copies:
        c.start()
    for c in copies[s.B :]:
        c.wait()
    stores = []
    group = lane_group(s, s.cols)
    for n in range(s.tiles):
        for c in copies[s.G * n : s.G * (n + 1)]:
            c.wait()
        m = me // s.G ^ n
        lanes = pl.ds(pl.multiple_of(m * LANES, LANES), LANES)
        for kind, (out, out_at) in enumerate(((gate_grad, gate_at), (filter_grad, filter_at))):
            for i2 in range(s.Q):
                vs = [src[s.G * m + a, kind, i2].astype(F32) for a in range(s.G)]
                for a, v in enumerate(lane_transpose(s, vs, group)):
                    i = s.G * i2 + a
                    if kind == 0:
                        v = (v * g[i, m].astype(F32)).astype(BF16)
                    out[i, :, lanes] = v
            sem = sems.at[len(stores)]
            at = (slice(None), slice(None), lanes)
            stores.append(pltpu.make_async_copy(out.at[at], out_at.at[at], sem))
            stores[-1].start()
    for c in stores:
        c.wait()


def columns(s, parts):
    cols_shape = (s.B, s.cols, s.C)
    return pl.pallas_call(
        functools.partial(columns_kernel, s),
        out_shape=[
            jax.ShapeDtypeStruct(cols_shape, BF16),
            jax.ShapeDtypeStruct(cols_shape, F32),
        ],
        in_specs=[hbm()] * s.B,
        out_specs=[hbm()] * 2,
        scratch_shapes=[
            pltpu.VMEM((s.B,) + parts[-1].shape, BF16),
            pltpu.VMEM((s.B, s.tiles, s.cols, LANES), BF16),
            pltpu.VMEM(cols_shape, BF16),
            pltpu.VMEM(cols_shape, F32),
            pltpu.SemaphoreType.DMA((s.B,)),
            pltpu.SemaphoreType.DMA((s.B,)),
            pltpu.SemaphoreType.DMA((2 * s.tiles,)),
        ],
        compiler_params=params(56),
        cost_estimate=cost(s.T * s.C * 8, s.T * s.C * 12),
        name="columns",
    )(*parts)


def exchange(v):
    return lax.all_to_all(v, "bins", split_axis=0, concat_axis=0, tiled=True)


def shards(tokens_in, filters, gate, skip, out_grad, out_weight, owner, slot):
    s = Plan(lax.axis_size("bins"), *tokens_in.shape)
    me = lax.axis_index("bins")
    nchan = lax.axis_size("chan")
    dft, tw, pre = tables(s)
    spec_shape = jax.ShapeDtypeStruct((s.K, 2, s.R, LANES), F32)
    spec_bytes = s.K * 2 * s.R * LANES * 4
    transform = 2 * 2 * s.R * s.R * 2 * LANES * s.K
    held = pltpu.VMEM((s.K, s.R, 2 * LANES), BF16)
    back = pltpu.VMEM((s.K, 2, s.R, LANES), F32)

    packed = pack(s, owner, slot, tokens_in, filters)
    came = exchange(packed)

    core_pairs = [(c, c ^ 1) for c in range(nchan)]
    hops = list(range(2, nchan, 2))
    far = [lax.ppermute(out_grad, "chan", [(c, c ^ h) for c in range(nchan)]) for h in hops]
    near = lax.ppermute(out_grad, "chan", core_pairs)
    start = project_part(s, [out_grad], (0,), out_weight)
    my_skip = own_skip(s, skip)
    *far, start, my_skip = lax.optimization_barrier((*far, start, my_skip))
    far_near = [lax.ppermute(v, "chan", core_pairs) for v in far]
    start = project_part(s, [near, *far], (1, *hops), out_weight, (start,))
    for v, h in zip(far_near[:-1], hops[:-1]):
        start = project_part(s, [v], (h ^ 1,), out_weight, (start,))
    *dy, away, kept = project_finish(s, far_near[-1], hops[-1] ^ 1, out_weight, start, gate)
    dy = swap_partners(s, dy, {1: 2})

    block = pltpu.VMEM((s.B, s.R, LANES), BF16)
    dft_held = pltpu.VMEM((2 * s.R, s.R), BF16)
    h_spec, x, codes = pl.pallas_call(
        functools.partial(spectrum_kernel, s),
        out_shape=[
            pltpu.HBM(spec_shape.shape, F32),
            pltpu.HBM((s.B, s.R, LANES), BF16),
            pltpu.HBM((s.B, TAIL, LANES), BF16),
        ],
        in_specs=[hbm(), hbm(), hbm(), vmem()],
        out_specs=[hbm()] * 3,
        scratch_shapes=[
            block,
            block,
            pltpu.VMEM((s.B, TAIL, LANES), BF16),
            dft_held,
            back,
            back,
            held,
            pltpu.SemaphoreType.DMA((4 + TW_PIECES,)),
            pltpu.SemaphoreType.DMA((s.K + 2,)),
        ],
        compiler_params=params(58),
        cost_estimate=cost(10 * transform, 2 * spec_bytes),
        name="filter_spectrum",
    )(came, dft, tw, pre)

    away, dy[s.B - 1] = lax.optimization_barrier((away, dy[s.B - 1]))
    g_came = swap_halves(s, away)

    outbox_shape = (s.B, s.Q * s.send, LANES)
    y_spec, outbox = pl.pallas_call(
        functools.partial(token_kernel, s),
        out_shape=[pltpu.HBM(spec_shape.shape, F32), pltpu.HBM(outbox_shape, BF16)],
        in_specs=[hbm()] * (s.B + 6),
        out_specs=[hbm()] * 2,
        scratch_shapes=[
            block,
            pltpu.VMEM((s.B, TAIL, LANES), BF16),
            back,
            pltpu.VMEM((1, LANES), F32),
            dft_held,
            back,
            pltpu.VMEM((s.K, 2, LANES), F32),
            back,
            pltpu.VMEM(outbox_shape, BF16),
            held,
            back,
            block,
            pltpu.SemaphoreType.DMA((s.B + 5 + TW_PIECES,)),
            pltpu.SemaphoreType.DMA((s.K + s.Q,)),
        ],
        compiler_params=params(60),
        cost_estimate=cost(20 * transform, 3 * spec_bytes),
        name="token_products",
    )(*[dy[x] for x in arrival_order(s)], codes, h_spec, my_skip, dft, tw, pre)
    outbox, g_came = lax.optimization_barrier((outbox, g_came))
    inbox = exchange(outbox)

    cols_shape = (s.Q, s.cols, LANES)
    by_dest = pltpu.VMEM((s.B,) + cols_shape, BF16)
    parts = pl.pallas_call(
        functools.partial(products_kernel, s),
        out_shape=[
            jax.ShapeDtypeStruct((4 if x < s.B // 2 else 2,) + cols_shape, BF16)
            for x in range(s.B)
        ],
        in_specs=[hbm()] * 3 + [vmem()] * 3 + [hbm()] * 2 + [vmem()],
        out_specs=[vmem()] * s.B,
        scratch_shapes=[
            block,
            back,
            back,
            dft_held,
            back,
            back,
            held,
            back,
            by_dest,
            by_dest,
            pltpu.SemaphoreType.DMA((4 + TW_PIECES,)),
        ],
        compiler_params=params(),
        cost_estimate=cost(3 * transform, 4 * spec_bytes),
        name="conv_and_filter",
    )(x, h_spec, y_spec, kept, g_came, my_skip, dft, tw, pre)
    grad_rows = owner_rows(s, inbox)
    *parts, last = parts
    last, grad_rows = lax.optimization_barrier((last, grad_rows))
    parts = swap_partners(s, [*parts, last], {1: 2})
    gate_grad, filter_grad = columns(s, parts)
    return (gate_grad, filter_grad, grad_rows)


def solution(mesh):
    return jax.shard_map(
        shards,
        mesh=mesh,
        in_specs=(
            P("bins", "chan"),
            P("bins", "chan"),
            P("bins", "chan"),
            P("chan"),
            P("bins", "chan"),
            P("chan", None),
            P(None, "bins"),
            P(None, "bins"),
        ),
        out_specs=(P(None, "bins", "chan"), P(None, "bins", "chan"), P("bins", "chan")),
        check_vma=False,
    )
```
